32 devices in a mesh: ctx: 8 (over z, core), fsdp: 4 (over y, x).
Axes of the slice: x: 2, y: 2, z: 4, core: 2. Of those that a mesh axis runs over, the one named last changes fastest.
Arguments:
- tokens: bfloat16 [4, 2048, 2048], P('fsdp', 'ctx'), may hold values from -6 to 6
- cotangent: bfloat16 [4, 2048, 2048], P('fsdp', 'ctx'), may hold values from -6 to 6
- lengths: int32 [4, 4], P('fsdp'), may hold values from 1 to 1793, 2048 in all within a row
- attn_gain: bfloat16 [2048], P(('ctx', 'fsdp')), may hold values from 0.099609375 to 1.8984375
- query_weight: bfloat16 [2048, 2048], P(('ctx', 'fsdp')), may hold values from -0.1875 to 0.1875
- key_weight: bfloat16 [2048, 512], P(('ctx', 'fsdp')), may hold values from -0.1875 to 0.1875
- value_weight: bfloat16 [2048, 512], P(('ctx', 'fsdp')), may hold values from -0.125 to 0.125
- out_weight: bfloat16 [2048, 2048], P(('ctx', 'fsdp')), may hold values from -1 to 1
- mlp_gain: bfloat16 [2048], P(('ctx', 'fsdp')), may hold values from 0.099609375 to 1.8984375
- gate_weight: bfloat16 [2048, 8192], P(('ctx', 'fsdp')), may hold values from -0.125 to 0.125
- up_weight: bfloat16 [2048, 8192], P(('ctx', 'fsdp')), may hold values from -0.125 to 0.125
- down_weight: bfloat16 [8192, 2048], P(('ctx', 'fsdp')), may hold values from -0.09375 to 0.09375
Outputs:
- mixed: bfloat16 [4, 2048, 2048], P('fsdp', 'ctx')
- grad_tokens: bfloat16 [4, 2048, 2048], P('fsdp', 'ctx')
- grad_attn_gain: float32 [2048], P(('ctx', 'fsdp'))
- grad_query: float32 [2048, 2048], P(('ctx', 'fsdp'))
- grad_key: float32 [2048, 512], P(('ctx', 'fsdp'))
- grad_value: float32 [2048, 512], P(('ctx', 'fsdp'))
- grad_out: float32 [2048, 2048], P(('ctx', 'fsdp'))
- grad_mlp_gain: float32 [2048], P(('ctx', 'fsdp'))
- grad_gate: float32 [2048, 8192], P(('ctx', 'fsdp'))
- grad_up: float32 [2048, 8192], P(('ctx', 'fsdp'))
- grad_down: float32 [8192, 2048], P(('ctx', 'fsdp'))
The draws below stay inside these ranges and needn't reach their ends.
Inputs may be any that keep to these rules, and one draw needn't show every extreme that they name: Row s holds the lengths of the 4 documents that fill sequence s in order; one of them is 1793 tokens long.
All inputs are finite; a program needn't handle non-finite values.
Results may differ from the reference program's by a relative error of at most 0.015.
The reference program's roundings to bfloat16 on the way count: a program that leaves them out, or rounds other values in their place, can miss the bound.
Values may be sent and summed in bfloat16 or wider, within the bound.
A program may use at most 640 MiB of HBM per device.

```python
import math
import jax
import jax.numpy as jnp
import numpy as np
from jax import lax

D = 2048
FF = 8192
HEADS = 32
KV_HEADS = 8
HEAD_DIM = 64
WINDOW = 1024
DOCS = 4
STRETCH = 256
LENGTH = 2048
SEQS = 4


def levels(own_key, dims, shards, smallest, high):
    gain = 1.0
    for dim, parts in shards:
        heights = jax.random.uniform(jax.random.fold_in(jax.random.fold_in(own_key, 6), dim), (parts,), jnp.float32, smallest / len(shards), high / len(shards))
        gain = gain * jnp.repeat(jnp.exp(heights), dims[dim] // parts).reshape((-1,) + (1,) * (len(dims) - 1 - dim))
    return gain


def profile(count, total, reach, skew):
    loads = [(1 << 20) // math.isqrt(standing ** skew) + 1 for standing in range(2, count + 1)]
    spare, counts = total - reach - (count - 1), [1] * (count - 1)
    while spare > 0:
        movable = [i for i in range(count - 1) if counts[i] < reach]
        pool, remaining = sum([loads[i] for i in movable]), spare
        for i in movable:
            more = min(reach - counts[i], max(1, remaining * loads[i] // pool), spare)
            counts[i] = counts[i] + more
            spare = spare - more
    return np.array([reach] + counts)


def uneven_parts(key, amount, total, most, skew):
    if amount == 2:
        one = jax.random.randint(key, (), max(1, total - most), min(most, total - 1) + 1)
        return jnp.stack([one, total - one])
    sizes = jnp.asarray(profile(amount, total, most, skew), jnp.int32)
    twos = (amount - 1) // 2
    donor, sink = sizes[1:1 + 2 * twos:2], sizes[2:2 + 2 * twos:2]
    room = jnp.minimum(donor - 1, most - sink)
    moved = jax.random.randint(jax.random.fold_in(key, 1), (twos,), 0, 1 << 20) % (room + 1)
    sizes = sizes.at[1:1 + 2 * twos:2].set(donor - moved).at[2:2 + 2 * twos:2].set(sink + moved)
    return sizes[jax.random.permutation(jax.random.fold_in(key, 2), amount)]


def gaussian(own_key, shape, scale, reach, pieces=(), kind=jnp.bfloat16):
    level = levels(own_key, shape, pieces, -0.22, 0.18) if pieces else 1.0
    array = jax.random.normal(own_key, shape, jnp.float32) * scale * level
    return jnp.minimum(jnp.maximum(array, -reach), reach).astype(kind)


def setup_inputs(seed: int = 0) -> dict:
    keys = jax.random.split(jax.random.key(seed), 13)
    tokens = gaussian(keys[0], (SEQS, LENGTH, D), 1.0, 6.0, ((0, 4), (1, 8)))
    cotangent = gaussian(keys[1], (SEQS, LENGTH, D), 1.0, 6.0, ((0, 4), (1, 8)))
    lengths = jax.vmap(lambda own: uneven_parts(own, DOCS, LENGTH, LENGTH - STRETCH + 1, 0))(jax.random.split(keys[2], SEQS)).reshape((SEQS, DOCS)).astype(jnp.int32)
    attn_gain = jnp.clip(1.0 + 0.18 * jax.random.normal(keys[3], (D,), jnp.float32), 0.099609375, 1.8984375).astype(jnp.bfloat16)
    query_weight = gaussian(keys[4], (D, D), (D // 2) ** -0.5, 0.1875, ((0, 32),))
    key_weight = gaussian(keys[5], (D, KV_HEADS * HEAD_DIM), (D // 2) ** -0.5, 0.1875, ((0, 32),))
    value_weight = gaussian(keys[6], (D, KV_HEADS * HEAD_DIM), D ** -0.5, 0.125, ((0, 32),))
    out_weight = gaussian(keys[7], (D, D), (D // 64) ** -0.5, 1.0, ((0, 32),))
    mlp_gain = jnp.clip(1.0 + 0.18 * jax.random.normal(keys[8], (D,), jnp.float32), 0.099609375, 1.8984375).astype(jnp.bfloat16)
    gate_weight = gaussian(keys[9], (D, FF), D ** -0.5, 0.125, ((0, 32),))
    up_weight = gaussian(keys[10], (D, FF), D ** -0.5, 0.125, ((0, 32),))
    down_weight = gaussian(keys[11], (FF, D), (FF // 2) ** -0.5, 0.09375, ((0, 32),))
    return {"tokens": tokens, "cotangent": cotangent, "lengths": lengths, "attn_gain": attn_gain, "query_weight": query_weight, "key_weight": key_weight, "value_weight": value_weight, "out_weight": out_weight, "mlp_gain": mlp_gain, "gate_weight": gate_weight, "up_weight": up_weight, "down_weight": down_weight}


EPS = 1e-05
THETA = 500000.0
HIGH = lax.Precision.HIGHEST

@jax.custom_vjp
def low(v):
    return lax.optimization_barrier(v.astype(jnp.bfloat16)).astype(jnp.float32)

@jax.custom_vjp
def low_back(v):
    return v

def low_keep(v):
    return (low(v), None)

def low_pass(kept, grad):
    return (grad,)

def back_keep(v):
    return (v, None)

def back_low(kept, grad):
    return (low(grad),)
low.defvjp(low_keep, low_pass)
low_back.defvjp(back_keep, back_low)

def matmul(left, right):
    return jnp.dot(left, right, precision=HIGH, preferred_element_type=jnp.float32)

def doc_info(doc_lengths, index):
    doc_ends = jnp.cumsum(doc_lengths).astype(jnp.int32)
    doc_starts = doc_ends - doc_lengths
    segment = lax.optimization_barrier(jnp.sum((index[:, None] >= doc_ends[None, :]).astype(jnp.int32), axis=1))
    member = segment[:, None] == jnp.arange(doc_lengths.shape[0], dtype=jnp.int32)[None, :]
    position = index - lax.optimization_barrier(jnp.sum(jnp.where(member, doc_starts[None, :], 0), axis=1))
    return (segment, position)

def rotate(heads, position, direction):
    half_dim = heads.shape[-1] // 2
    frequency = THETA ** (-2.0 * jnp.arange(half_dim, dtype=jnp.float32) / heads.shape[-1])
    angles = position.astype(jnp.float32)[:, None] * frequency[None, :]
    cosine = jnp.cos(angles)[:, None, :]
    sine_part = direction * jnp.sin(angles)[:, None, :]
    first_half = heads[..., :half_dim]
    second_half = heads[..., half_dim:]
    return jnp.concatenate([first_half * cosine - second_half * sine_part, second_half * cosine + first_half * sine_part], axis=-1)

def normalize(values):
    return values * lax.rsqrt(lax.optimization_barrier(jnp.mean(values * values, axis=-1, keepdims=True)) + EPS)

def attention(queries, key_all, value_all, segment):
    seq_len = queries.shape[0]
    group_size = HEADS // KV_HEADS
    num_blocks = seq_len // STRETCH
    key_pad = jnp.pad(key_all, ((WINDOW, 0), (0, 0), (0, 0)))
    value_pad = jnp.pad(value_all, ((WINDOW, 0), (0, 0), (0, 0)))
    seg_pad = jnp.pad(segment, (WINDOW, 0), constant_values=-1)
    query_blocks = queries.reshape(num_blocks, STRETCH, KV_HEADS, group_size, HEAD_DIM)

    def attend(inputs):
        block_id, query_block = inputs
        first_row = block_id * STRETCH
        key_block = lax.dynamic_slice_in_dim(key_pad, first_row, STRETCH + WINDOW, 0)
        value_block = lax.dynamic_slice_in_dim(value_pad, first_row, STRETCH + WINDOW, 0)
        query_index = first_row + jnp.arange(STRETCH, dtype=jnp.int32)
        key_index = first_row - WINDOW + jnp.arange(STRETCH + WINDOW, dtype=jnp.int32)
        query_seg = lax.dynamic_slice_in_dim(segment, first_row, STRETCH, 0)
        key_seg = lax.dynamic_slice_in_dim(seg_pad, first_row, STRETCH + WINDOW, 0)
        visible = (key_index[None, :] >= 0) & (key_index[None, :] <= query_index[:, None])
        visible = visible & (query_index[:, None] - key_index[None, :] < WINDOW) & (query_seg[:, None] == key_seg[None, :])
        scores = low_back(jnp.einsum('qkgd,jkd->kgqj', query_block, key_block, precision=HIGH) * HEAD_DIM ** (-0.5))
        scores = jnp.where(visible[None, None], scores, -1e+30)
        row_max = lax.optimization_barrier(jnp.max(scores, axis=-1, keepdims=True))
        raised = jnp.exp(scores - row_max)
        probability = raised / lax.optimization_barrier(jnp.sum(raised, axis=-1, keepdims=True))
        return jnp.einsum('kgqj,jkd->qkgd', low(probability), value_block, precision=HIGH)
    outputs = lax.map(jax.checkpoint(attend), (jnp.arange(num_blocks, dtype=jnp.int32), query_blocks))
    return outputs.reshape(seq_len, HEADS * HEAD_DIM)

def layer(stream, attn_gain, query_weight, key_weight, value_weight, out_weight, mlp_gain, gate_weight, up_weight, down_weight, segment, position):
    seq_len = stream.shape[0]
    normed_one = low(normalize(stream) * attn_gain)
    queries = low_back(matmul(normed_one, query_weight)).reshape(seq_len, HEADS, HEAD_DIM)
    key_all = low_back(matmul(normed_one, key_weight)).reshape(seq_len, KV_HEADS, HEAD_DIM)
    value_all = low(low_back(matmul(normed_one, value_weight))).reshape(seq_len, KV_HEADS, HEAD_DIM)
    queries = low(rotate(queries, position, 1.0))
    key_all = low(rotate(key_all, position, 1.0))
    mixed_heads = low(low_back(attention(queries, key_all, value_all, segment)))
    resid = stream + low_back(matmul(mixed_heads, out_weight))
    normed_two = low(normalize(resid) * mlp_gain)
    gate_sum = low_back(matmul(normed_two, gate_weight))
    up_sum = low_back(matmul(normed_two, up_weight))
    hidden = low(gate_sum * jax.nn.sigmoid(gate_sum) * up_sum)
    return resid + matmul(hidden, down_weight)

def reference(tokens, cotangent, lengths, attn_gain, query_weight, key_weight, value_weight, out_weight, mlp_gain, gate_weight, up_weight, down_weight):
    weights = tuple((weight.astype(jnp.float32) for weight in (attn_gain, query_weight, key_weight, value_weight, out_weight, mlp_gain, gate_weight, up_weight, down_weight)))

    def one_sequence(totals, inputs):
        stream, grad_low, doc_lengths = inputs
        index = jnp.arange(stream.shape[0], dtype=jnp.int32)
        segment, position = doc_info(doc_lengths, index)

        def forward(stream_in, *params):
            return layer(stream_in, *params, segment, position)
        output, pullback = jax.vjp(forward, stream.astype(jnp.float32), *weights)
        grads = pullback(grad_low.astype(jnp.float32))
        totals = tuple((total + grad for total, grad in zip(totals, grads[1:])))
        return (totals, (output.astype(jnp.bfloat16), grads[0].astype(jnp.bfloat16)))
    zeros_init = tuple((jnp.zeros(weight.shape, jnp.float32) for weight in weights))
    totals, outputs = lax.scan(one_sequence, zeros_init, (tokens, cotangent, lengths))
    return (outputs[0], outputs[1], totals[0], totals[1], totals[2], totals[3], totals[4], totals[5], totals[6], totals[7], totals[8])
```

```python
import jax
import jax.numpy as jnp
from jax import lax
from jax.sharding import PartitionSpec as P

D = 2048
FF = 8192
HEADS = 32
KV_HEADS = 8
HEAD_DIM = 64
WINDOW = 1024
STRETCH = 256


EPS = 1e-05
THETA = 500000.0


def passed_along(x, axis, by):
    size = lax.axis_size(axis)
    pairs = [(i, i + by) for i in range(size) if 0 <= i + by < size]
    return lax.ppermute(x, axis, pairs)


def product(left, right):
    return jnp.dot(left, right, preferred_element_type=jnp.float32)


def against(left, right):
    return lax.dot_general(
        left, right, (((1,), (1,)), ((), ())), preferred_element_type=jnp.float32
    )


def across(left, right):
    return lax.dot_general(
        left, right, (((0,), (0,)), ((), ())), preferred_element_type=jnp.float32
    )


def doc_segment(doc_lengths, index):
    doc_ends = jnp.cumsum(doc_lengths)
    return jnp.sum((index[:, None] >= doc_ends[None, :]).astype(jnp.int32), axis=1)


def doc_position(doc_lengths, index, segment):
    doc_ends = jnp.cumsum(doc_lengths)
    doc_starts = doc_ends - doc_lengths
    member = segment[:, None] == jnp.arange(doc_lengths.shape[0], dtype=jnp.int32)[None, :]
    return index - jnp.sum(jnp.where(member, doc_starts[None, :], 0), axis=1)


def rotate(heads, position, direction):
    half_dim = heads.shape[-1] // 2
    frequency = THETA ** (-2.0 * jnp.arange(half_dim, dtype=jnp.float32) / heads.shape[-1])
    angles = position.astype(jnp.float32)[:, None] * frequency[None, :]
    cosine = jnp.cos(angles)[:, None, :]
    sine_part = direction * jnp.sin(angles)[:, None, :]
    first_half = heads[..., :half_dim]
    second_half = heads[..., half_dim:]
    return jnp.concatenate(
        [
            first_half * cosine - second_half * sine_part,
            second_half * cosine + first_half * sine_part,
        ],
        axis=-1,
    )


def to_groups(matrix, tok_rows):
    shaped = matrix.reshape(tok_rows, KV_HEADS, HEADS // KV_HEADS, HEAD_DIM).transpose(1, 2, 0, 3)
    return shaped.reshape(KV_HEADS, -1, HEAD_DIM)


def from_groups(stacked, tok_rows):
    shaped = stacked.reshape(KV_HEADS, HEADS // KV_HEADS, tok_rows, HEAD_DIM).transpose(2, 0, 1, 3)
    return shaped.reshape(tok_rows, HEADS * HEAD_DIM)


def to_kv_heads(matrix):
    return matrix.reshape(matrix.shape[0], KV_HEADS, HEAD_DIM).transpose(1, 0, 2)


def from_kv_heads(stacked):
    return stacked.transpose(1, 0, 2).reshape(stacked.shape[1], KV_HEADS * HEAD_DIM)


def attend_forward(query_heads, key_heads, value_heads, visible):
    score_scale = HEAD_DIM ** (-0.5)

    def one_head(inputs):
        query_block, key_block, value_block = inputs
        scores = jnp.where(visible, against(query_block, key_block) * score_scale, -1e30)
        row_max = jnp.max(scores, axis=1, keepdims=True)
        raised = jnp.exp(scores - row_max)
        row_total = jnp.sum(raised, axis=1, keepdims=True)
        probability = (raised / row_total).astype(jnp.bfloat16)
        return (product(probability, value_block), row_max, row_total)

    return lax.map(one_head, (query_heads, key_heads, value_heads))


def attend_backward(query_heads, key_heads, value_heads, grad_heads, row_max, row_total, visible):
    score_scale = HEAD_DIM ** (-0.5)

    def one_head(inputs):
        query_block, key_block, value_block, grad_block, block_max, block_total = inputs
        scores = jnp.where(visible, against(query_block, key_block) * score_scale, -1e30)
        probability = jnp.exp(scores - block_max) / block_total
        grad_prob = against(grad_block, value_block)
        delta = jnp.sum(probability * grad_prob, axis=1, keepdims=True)
        grad_scores = (probability * (grad_prob - delta)).astype(jnp.bfloat16)
        grad_query = product(grad_scores, key_block) * score_scale
        grad_key = across(grad_scores, query_block) * score_scale
        grad_value = across(probability.astype(jnp.bfloat16), grad_block)
        return (grad_query, grad_key, grad_value)

    return lax.map(one_head, (query_heads, key_heads, value_heads, grad_heads, row_max, row_total))


def norm_back(grad_normal, normal, inverse):
    return inverse * (grad_normal - normal * jnp.mean(grad_normal * normal, axis=1, keepdims=True))


def swapped(x, axis, mask):
    size = lax.axis_size(axis)
    return lax.ppermute(x, axis, [(i, i ^ mask) for i in range(size)])


def mask_orders(axis):
    size = lax.axis_size(axis)
    masks = [1 << bit for bit in range(size.bit_length() - 1)]
    return [masks, masks[::-1]]


def gather_swapping(x, axis):
    size = lax.axis_size(axis)
    orders = mask_orders(axis)
    place = lax.axis_index(axis)
    parts = []
    for part, order in zip(jnp.split(x, len(orders), axis=0), orders):
        bits = size.bit_length() - 1
        held = part.reshape((1,) * bits + part.shape)
        for mask in order:
            got = swapped(held, axis, mask)
            dim = bits - mask.bit_length()
            low = (place & mask) == 0
            held = jnp.concatenate(
                [jnp.where(low, held, got), jnp.where(low, got, held)], axis=dim
            )
        parts.append(held.reshape((size,) + part.shape))
    return jnp.concatenate(parts, axis=1)


def scatter_swapping(x, axis):
    size = lax.axis_size(axis)
    orders = mask_orders(axis)
    place = lax.axis_index(axis)
    parts = []
    for part, order in zip(jnp.split(x, len(orders), axis=1), orders):
        bits = size.bit_length() - 1
        held = part.reshape((2,) * bits + part.shape[1:])
        for mask in order:
            dim = bits - mask.bit_length()
            bit = (place & mask) // mask
            sent = lax.dynamic_slice_in_dim(held, 1 - bit, 1, dim).astype(jnp.bfloat16)
            own = lax.dynamic_slice_in_dim(held, bit, 1, dim)
            held = own + swapped(sent, axis, mask).astype(jnp.float32)
        parts.append(held.reshape(part.shape[1:]))
    return jnp.concatenate(parts, axis=0)


def local(
    tokens,
    cotangent,
    lengths,
    attn_gain,
    query_weight,
    key_weight,
    value_weight,
    out_weight,
    mlp_gain,
    gate_weight,
    up_weight,
    down_weight,
):
    both = ("ctx", "fsdp")
    ctx_size = lax.axis_size("ctx")
    fsdp_size = lax.axis_size("fsdp")
    stream = tokens[0].astype(jnp.float32)
    tok_rows = stream.shape[0]
    own_rows = query_weight.shape[0]
    group_size = HEADS // KV_HEADS
    kv_width = KV_HEADS * HEAD_DIM
    reach_blocks = WINDOW // STRETCH
    ctx_place = lax.axis_index("ctx")
    doc_lengths = lengths[0]
    query_index = ctx_place * tok_rows + jnp.arange(tok_rows, dtype=jnp.int32)
    key_index = (ctx_place - reach_blocks) * tok_rows + jnp.arange(
        (reach_blocks + 1) * tok_rows, dtype=jnp.int32
    )
    query_doc = doc_segment(doc_lengths, query_index)
    key_doc = doc_segment(doc_lengths, key_index)
    position = doc_position(doc_lengths, query_index, query_doc)
    visible = (key_index[None, :] >= 0) & (key_index[None, :] <= query_index[:, None])
    visible = (
        visible
        & (query_index[:, None] - key_index[None, :] < WINDOW)
        & (query_doc[:, None] == key_doc[None, :])
    )
    visible = jnp.tile(visible, (group_size, 1))

    gains = jnp.zeros((own_rows, 128), jnp.bfloat16)
    gains = gains.at[:, 0].set(attn_gain).at[:, 1].set(mlp_gain)
    front_all = lax.all_gather(
        jnp.concatenate([query_weight, key_weight, value_weight, gains], axis=1),
        both, axis=0, tiled=True,
    )
    front_weight = front_all[:, : D + 2 * kv_width]
    gain_one = front_all[:, D + 2 * kv_width].astype(jnp.float32)
    gain_two = front_all[:, D + 2 * kv_width + 1].astype(jnp.float32)
    out_all = lax.all_gather(out_weight, both, axis=0, tiled=True)

    ff_own = FF // ctx_size
    pair = jnp.stack([gate_weight, up_weight]).reshape(2, own_rows, ctx_size, ff_own)
    pair = lax.all_to_all(
        pair.transpose(2, 0, 1, 3), "ctx", split_axis=0, concat_axis=0, tiled=True
    )
    pair = gather_swapping(pair.reshape(ctx_size * 2 * own_rows, ff_own), "fsdp")
    pair = pair.reshape(fsdp_size, ctx_size, 2, own_rows, ff_own).transpose(2, 1, 0, 3, 4)
    pair = pair.reshape(2, D, ff_own)
    gate_own, up_own = pair[0], pair[1]
    down_own = gather_swapping(down_weight, "fsdp").reshape(ff_own, D)
    cot_all = lax.all_gather(cotangent[0], "ctx", axis=0, tiled=True)

    inv_one = lax.rsqrt(jnp.mean(stream * stream, axis=1, keepdims=True) + EPS)
    normal_one = stream * inv_one
    normed_one = (normal_one * gain_one).astype(jnp.bfloat16)
    front = product(normed_one, front_weight)
    query_rot = (
        rotate(front[:, :D].reshape(tok_rows, HEADS, HEAD_DIM), position, 1.0)
        .astype(jnp.bfloat16)
        .reshape(tok_rows, D)
    )
    key_rot = (
        rotate(front[:, D : D + kv_width].reshape(tok_rows, KV_HEADS, HEAD_DIM), position, 1.0)
        .astype(jnp.bfloat16)
        .reshape(tok_rows, kv_width)
    )
    value_low = front[:, D + kv_width :].astype(jnp.bfloat16)
    key_list = [key_rot]
    value_list = [value_low]
    own_pair = jnp.stack([key_rot, value_low])
    for step in range(1, reach_blocks + 1):
        earlier = passed_along(own_pair, "ctx", step)
        key_list.insert(0, earlier[0])
        value_list.insert(0, earlier[1])
    key_heads = to_kv_heads(jnp.concatenate(key_list, axis=0))
    value_heads = to_kv_heads(jnp.concatenate(value_list, axis=0))
    query_heads = to_groups(query_rot, tok_rows)
    head_out, row_max, row_total = attend_forward(query_heads, key_heads, value_heads, visible)
    attn_mix = from_groups(head_out, tok_rows).astype(jnp.bfloat16)
    resid = stream + product(attn_mix, out_all)
    inv_two = lax.rsqrt(jnp.mean(resid * resid, axis=1, keepdims=True) + EPS)
    normal_two = resid * inv_two
    normed_two = (normal_two * gain_two).astype(jnp.bfloat16)

    normed_all = lax.all_gather(normed_two, "ctx", axis=0, tiled=True)
    gate_sum = product(normed_all, gate_own)
    up_sum = product(normed_all, up_own)
    sigmoid_gate = jax.nn.sigmoid(gate_sum)
    silu_gate = gate_sum * sigmoid_gate
    hidden = (silu_gate * up_sum).astype(jnp.bfloat16)
    grad_hidden = against(cot_all, down_own)
    grad_gate_low = (
        grad_hidden * up_sum * sigmoid_gate * (1.0 + gate_sum * (1.0 - sigmoid_gate))
    ).astype(jnp.bfloat16)
    grad_up_low = (grad_hidden * silu_gate).astype(jnp.bfloat16)
    columns_part = against(grad_gate_low, gate_own) + against(grad_up_low, up_own)
    columns = lax.psum_scatter(
        columns_part.astype(jnp.bfloat16), "ctx", scatter_dimension=0, tiled=True
    ).astype(jnp.float32)
    down_part = product(hidden, down_own).astype(jnp.bfloat16)
    down_sum = lax.psum_scatter(down_part, "ctx", scatter_dimension=0, tiled=True)
    mixed = (resid + down_sum.astype(jnp.float32)).astype(jnp.bfloat16)

    down_terms = across(hidden, cot_all).reshape(fsdp_size, -1, D)
    grad_down = scatter_swapping(down_terms, "fsdp")
    pair_terms = jnp.stack([across(normed_all, grad_gate_low), across(normed_all, grad_up_low)])
    pair_terms = pair_terms.reshape(2, ctx_size, fsdp_size, own_rows, ff_own)
    pair_terms = pair_terms.transpose(2, 1, 0, 3, 4)
    pair_sum = scatter_swapping(pair_terms.reshape(fsdp_size, -1, ff_own), "fsdp")
    pair_sum = pair_sum.astype(jnp.bfloat16).reshape(ctx_size, 2, own_rows, ff_own)
    pair_sum = lax.all_to_all(pair_sum, "ctx", split_axis=0, concat_axis=0, tiled=True)
    pair_sum = pair_sum.transpose(1, 2, 0, 3).reshape(2, own_rows, FF).astype(jnp.float32)

    grad_stream = cotangent[0].astype(jnp.float32)
    mlp_gain_local = jnp.sum(columns * normal_two, axis=0)
    grad_resid = grad_stream + norm_back(columns * gain_two, normal_two, inv_two)
    grad_resid_low = grad_resid.astype(jnp.bfloat16)
    grad_mix = against(grad_resid_low, out_all)
    grad_mix_low = grad_mix.astype(jnp.bfloat16)
    out_grad = lax.psum_scatter(
        lax.psum_scatter(
            across(attn_mix, grad_resid_low).astype(jnp.bfloat16),
            "ctx", scatter_dimension=0, tiled=True,
        ),
        "fsdp", scatter_dimension=0, tiled=True,
    ).astype(jnp.float32)
    grad_query_heads, grad_key_heads, grad_value_heads = attend_backward(
        query_heads,
        key_heads,
        value_heads,
        to_groups(grad_mix_low, tok_rows),
        row_max,
        row_total,
        visible,
    )
    grad_query_rot = from_groups(grad_query_heads, tok_rows)
    grad_key_window = from_kv_heads(grad_key_heads)
    grad_value_window = from_kv_heads(grad_value_heads)
    own_start = reach_blocks * tok_rows
    grad_key_total = grad_key_window[own_start:]
    grad_value_total = grad_value_window[own_start:]
    for step in range(1, reach_blocks + 1):
        first_row = (reach_blocks - step) * tok_rows
        sent_pair = jnp.stack(
            [
                grad_key_window[first_row : first_row + tok_rows],
                grad_value_window[first_row : first_row + tok_rows],
            ]
        )
        later = passed_along(sent_pair.astype(jnp.bfloat16), "ctx", -step).astype(sent_pair.dtype)
        grad_key_total = grad_key_total + later[0]
        grad_value_total = grad_value_total + later[1]
    grad_query_low = (
        rotate(grad_query_rot.reshape(tok_rows, HEADS, HEAD_DIM), position, -1.0)
        .reshape(tok_rows, D)
        .astype(jnp.bfloat16)
    )
    grad_key_low = (
        rotate(grad_key_total.reshape(tok_rows, KV_HEADS, HEAD_DIM), position, -1.0)
        .reshape(tok_rows, kv_width)
        .astype(jnp.bfloat16)
    )
    grad_value_low = grad_value_total.astype(jnp.bfloat16)
    front_low = jnp.concatenate([grad_query_low, grad_key_low, grad_value_low], axis=1)
    grad_normed_one = against(front_low, front_weight)
    attn_gain_local = jnp.sum(grad_normed_one * normal_one, axis=0)
    front_terms = jnp.concatenate(
        [
            across(normed_one, front_low),
            jnp.pad(jnp.stack([attn_gain_local, mlp_gain_local], axis=1), ((0, 0), (0, 126))),
        ],
        axis=1,
    ).astype(jnp.bfloat16)
    front_grad = lax.psum_scatter(
        lax.psum_scatter(front_terms, "ctx", scatter_dimension=0, tiled=True),
        "fsdp", scatter_dimension=0, tiled=True,
    ).astype(jnp.float32)
    grad_input = grad_resid + norm_back(grad_normed_one * gain_one, normal_one, inv_one)
    width = D + 2 * kv_width
    return (
        mixed[None],
        grad_input.astype(jnp.bfloat16)[None],
        front_grad[:, width],
        front_grad[:, :D],
        front_grad[:, D : D + kv_width],
        front_grad[:, D + kv_width : width],
        out_grad,
        front_grad[:, width + 1],
        pair_sum[0],
        pair_sum[1],
        grad_down,
    )


def solution(mesh):
    in_specs = (
        P("fsdp", "ctx", None),
        P("fsdp", "ctx", None),
        P("fsdp", None),
        P(("ctx", "fsdp")),
        P(("ctx", "fsdp"), None),
        P(("ctx", "fsdp"), None),
        P(("ctx", "fsdp"), None),
        P(("ctx", "fsdp"), None),
        P(("ctx", "fsdp")),
        P(("ctx", "fsdp"), None),
        P(("ctx", "fsdp"), None),
        P(("ctx", "fsdp"), None),
    )
    out_specs = (
        P("fsdp", "ctx", None),
        P("fsdp", "ctx", None),
        P(("ctx", "fsdp")),
        P(("ctx", "fsdp"), None),
        P(("ctx", "fsdp"), None),
        P(("ctx", "fsdp"), None),
        P(("ctx", "fsdp"), None),
        P(("ctx", "fsdp")),
        P(("ctx", "fsdp"), None),
        P(("ctx", "fsdp"), None),
        P(("ctx", "fsdp"), None),
    )
    return jax.shard_map(local, mesh=mesh, in_specs=in_specs, out_specs=out_specs, check_vma=False)
```

```python
import functools

import jax
import jax.numpy as jnp
from jax import lax
from jax.experimental import pallas as pl
from jax.experimental.pallas import tpu as pltpu
from jax.sharding import PartitionSpec as P

D = 2048
FF = 8192
HEADS = 32
KV_HEADS = 8
HEAD_DIM = 64
WINDOW = 1024
STRETCH = 256
QTILE = 128
LANES = 128
EPS = 1e-05
THETA = 500000.0


def passed_along(x, axis, by):
    size = lax.axis_size(axis)
    pairs = [(i, i + by) for i in range(size) if 0 <= i + by < size]
    return lax.ppermute(x, axis, pairs)


def product(left, right):
    return jnp.dot(left, right, preferred_element_type=jnp.float32)


def against(left, right):
    return lax.dot_general(
        left, right, (((1,), (1,)), ((), ())), preferred_element_type=jnp.float32
    )


def across(left, right):
    return lax.dot_general(
        left, right, (((0,), (0,)), ((), ())), preferred_element_type=jnp.float32
    )


def doc_segment(doc_lengths, index):
    doc_ends = jnp.cumsum(doc_lengths)
    return jnp.sum((index[:, None] >= doc_ends[None, :]).astype(jnp.int32), axis=1)


def doc_position(doc_lengths, index, segment):
    doc_ends = jnp.cumsum(doc_lengths)
    doc_starts = doc_ends - doc_lengths
    member = segment[:, None] == jnp.arange(doc_lengths.shape[0], dtype=jnp.int32)[None, :]
    return index - jnp.sum(jnp.where(member, doc_starts[None, :], 0), axis=1)


def swap_halves(u):
    half = HEAD_DIM // 2
    width = u.shape[1]
    lane = lax.broadcasted_iota(jnp.int32, u.shape, 1)
    ahead = pltpu.roll(u, width - half, 1)
    behind = pltpu.roll(u, half, 1)
    return jnp.where(lane % HEAD_DIM < half, ahead, behind)


def turn(u, cosine, sine):
    copies = u.shape[1] // cosine.shape[1]
    cosine = jnp.concatenate([cosine] * copies, axis=1)
    sine = jnp.concatenate([sine] * copies, axis=1)
    return u * cosine + swap_halves(u) * sine


def nt(left, right):
    return lax.dot_general(left, right, (((1,), (1,)), ((), ())), preferred_element_type=jnp.float32)


def nn(left, right):
    return lax.dot_general(left, right, (((1,), (0,)), ((), ())), preferred_element_type=jnp.float32)


def attend_forward_kernel(q_ref, k_ref, v_ref, bias_ref, cos_ref, sin_ref, o_ref, qr_ref, lse_ref):
    rows = q_ref.shape[0]
    group = HEADS // KV_HEADS
    span = k_ref.shape[0] - rows + QTILE
    rotated = turn(q_ref[...], cos_ref[...], sin_ref[...])
    qr_ref[...] = rotated.astype(jnp.bfloat16)
    scaled = (qr_ref[...].astype(jnp.float32) * HEAD_DIM ** (-0.5)).astype(jnp.bfloat16)
    for tile in range(rows // QTILE):
        first = tile * QTILE
        bias = bias_ref[first : first + span, first : first + QTILE]
        for kv in range(LANES // HEAD_DIM):
            lo = kv * HEAD_DIM
            keys = k_ref[first : first + span, lo : lo + HEAD_DIM]
            values = v_ref[first : first + span, lo : lo + HEAD_DIM]
            values_t = values.T
            raises, totals = [], []
            for h in range(group):
                head = kv * group + h
                q_h = scaled[first : first + QTILE, head * HEAD_DIM : (head + 1) * HEAD_DIM]
                s = nt(keys, q_h) + bias
                top = jnp.max(s, axis=0, keepdims=True)
                raised = jnp.exp(s - top)
                total = jnp.sum(raised, axis=0, keepdims=True)
                lse_ref[head : head + 1, first : first + QTILE] = top + jnp.log(total)
                raises.append(raised.astype(jnp.bfloat16))
                totals.append(total)
            o_wide = nn(values_t, jnp.concatenate(raises, axis=1)) / jnp.concatenate(totals, axis=1)
            o_t = jnp.concatenate(
                [o_wide[:, h * QTILE : (h + 1) * QTILE] for h in range(group)], axis=0
            )
            o_ref[first : first + QTILE, kv * group * HEAD_DIM : (kv + 1) * group * HEAD_DIM] = (
                o_t.T.astype(jnp.bfloat16)
            )


def attend_forward(q, k, v, bias, cosine, sine):
    rows, width = q.shape
    steps = KV_HEADS * HEAD_DIM // LANES
    qw = width // steps
    heads = HEADS // steps
    window = k.shape[0]
    return pl.pallas_call(
        attend_forward_kernel,
        grid=(steps,),
        in_specs=[
            pl.BlockSpec((rows, qw), lambda i: (0, i)),
            pl.BlockSpec((window, LANES), lambda i: (0, i)),
            pl.BlockSpec((window, LANES), lambda i: (0, i)),
            pl.BlockSpec((window, rows), lambda i: (0, 0)),
            pl.BlockSpec((rows, LANES), lambda i: (0, 0)),
            pl.BlockSpec((rows, LANES), lambda i: (0, 0)),
        ],
        out_specs=[
            pl.BlockSpec((rows, qw), lambda i: (0, i)),
            pl.BlockSpec((rows, qw), lambda i: (0, i)),
            pl.BlockSpec((heads, rows), lambda i: (i, 0)),
        ],
        out_shape=[
            jax.ShapeDtypeStruct((rows, width), jnp.bfloat16),
            jax.ShapeDtypeStruct((rows, width), jnp.bfloat16),
            jax.ShapeDtypeStruct((HEADS, rows), jnp.float32),
        ],
        compiler_params=pltpu.CompilerParams(vmem_limit_bytes=48 * 1024 * 1024),
        cost_estimate=pl.CostEstimate(flops=40_000_000_000, bytes_accessed=10_000_000, transcendentals=0),
    )(q, k, v, bias, cosine, sine)


def attend_backward_kernel(qr_ref, k_ref, v_ref, do_ref, o_ref, lse_ref, bias_ref, cos_ref, sin_ref, dq_ref, dk_ref, dv_ref):
    rows = qr_ref.shape[0]
    group = HEADS // KV_HEADS
    span = k_ref.shape[0] - rows + QTILE
    scale = HEAD_DIM ** (-0.5)
    dk_ref[...] = jnp.zeros_like(dk_ref)
    dv_ref[...] = jnp.zeros_like(dv_ref)
    scaled = (qr_ref[...].astype(jnp.float32) * scale).astype(jnp.bfloat16)
    wide = LANES // HEAD_DIM * group * HEAD_DIM
    owner = lax.broadcasted_iota(jnp.int32, (8, wide), 1) // HEAD_DIM
    pick = (owner == lax.broadcasted_iota(jnp.int32, (8, wide), 0)).astype(jnp.float32)
    for tile in range(rows // QTILE):
        first = tile * QTILE
        bias = bias_ref[first : first + span, first : first + QTILE]
        both = do_ref[first : first + QTILE, :].astype(jnp.float32) * o_ref[
            first : first + QTILE, :
        ].astype(jnp.float32)
        delta = lax.dot_general(
            pick, both, (((1,), (1,)), ((), ())),
            precision=lax.Precision.HIGHEST, preferred_element_type=jnp.float32,
        )
        dk_pair, dv_pair, dqs = [], [], []
        for kv in range(LANES // HEAD_DIM):
            lo = kv * HEAD_DIM
            keys = k_ref[first : first + span, lo : lo + HEAD_DIM]
            values = v_ref[first : first + span, lo : lo + HEAD_DIM]
            keys_t = keys.T
            probs, slopes, qs, dos = [], [], [], []
            for h in range(group):
                head = kv * group + h
                cols = slice(head * HEAD_DIM, (head + 1) * HEAD_DIM)
                q_h = scaled[first : first + QTILE, cols]
                do_h = do_ref[first : first + QTILE, cols]
                s = nt(keys, q_h) + bias
                p = jnp.exp(s - lse_ref[head : head + 1, first : first + QTILE])
                dp = nt(values, do_h)
                ds = (p * (dp - delta[head : head + 1, :])).astype(jnp.bfloat16)
                probs.append(p.astype(jnp.bfloat16))
                slopes.append(ds)
                qs.append(q_h)
                dos.append(do_h)
            p_all = jnp.concatenate(probs, axis=1)
            ds_all = jnp.concatenate(slopes, axis=1)
            dv_pair.append(nn(p_all, jnp.concatenate(dos, axis=0)))
            dk_pair.append(nn(ds_all, jnp.concatenate(qs, axis=0)))
            dq_t = nn(keys_t, ds_all) * scale
            dqs.extend(dq_t[:, h * QTILE : (h + 1) * QTILE] for h in range(group))
        dk_ref[first : first + span, :] += jnp.concatenate(dk_pair, axis=1)
        dv_ref[first : first + span, :] += jnp.concatenate(dv_pair, axis=1)
        dq = jnp.concatenate(dqs, axis=0).T
        dq_ref[first : first + QTILE, :] = turn(
            dq, cos_ref[first : first + QTILE, :], -sin_ref[first : first + QTILE, :]
        ).astype(jnp.bfloat16)


def attend_backward(qr, k, v, do, o, lse, bias, cosine, sine):
    rows, width = qr.shape
    steps = KV_HEADS * HEAD_DIM // LANES
    qw = width // steps
    heads = HEADS // steps
    window = k.shape[0]
    wide = pl.BlockSpec((rows, qw), lambda i: (0, i))
    tall = pl.BlockSpec((window, LANES), lambda i: (0, i))
    table = pl.BlockSpec((rows, LANES), lambda i: (0, 0))
    return pl.pallas_call(
        attend_backward_kernel,
        grid=(steps,),
        in_specs=[
            wide, tall, tall, wide, wide,
            pl.BlockSpec((heads, rows), lambda i: (i, 0)),
            pl.BlockSpec((window, rows), lambda i: (0, 0)),
            table, table,
        ],
        out_specs=[wide, tall, tall],
        out_shape=[
            jax.ShapeDtypeStruct((rows, width), jnp.bfloat16),
            jax.ShapeDtypeStruct(k.shape, jnp.float32),
            jax.ShapeDtypeStruct(k.shape, jnp.float32),
        ],
        compiler_params=pltpu.CompilerParams(vmem_limit_bytes=48 * 1024 * 1024),
        cost_estimate=pl.CostEstimate(flops=80_000_000_000, bytes_accessed=20_000_000, transcendentals=0),
    )(qr, k, v, do, o, lse, bias, cosine, sine)


def turn_tables(position):
    half_dim = HEAD_DIM // 2
    frequency = THETA ** (-2.0 * jnp.arange(half_dim, dtype=jnp.float32) / HEAD_DIM)
    angles = position.astype(jnp.float32)[:, None] * frequency[None, :]
    cosine, sine = jnp.cos(angles), jnp.sin(angles)
    copies = LANES // HEAD_DIM
    return (
        jnp.concatenate([cosine, cosine] * copies, axis=1),
        jnp.concatenate([-sine, sine] * copies, axis=1),
    )


def rope(u, cosine, sine):
    half = HEAD_DIM // 2
    parts = u.reshape(u.shape[0], -1, 2, half)
    swapped_parts = parts[:, :, ::-1, :].reshape(u.shape)
    copies = u.shape[1] // LANES
    return u * jnp.tile(cosine, (1, copies)) + swapped_parts * jnp.tile(sine, (1, copies))


def norm_back(grad_normal, normal, inverse):
    return inverse * (grad_normal - normal * jnp.mean(grad_normal * normal, axis=1, keepdims=True))


def after(x, *others):
    return lax.optimization_barrier((x,) + others)[0]


def peer_of(chip_mask, side_mask, fsdp_mask):
    ctx = lax.axis_index("ctx")
    return (ctx ^ (2 * chip_mask + side_mask), lax.axis_index("fsdp") ^ fsdp_mask)


def greet(peers):
    barrier = pltpu.get_barrier_semaphore()
    for peer in peers:
        pl.semaphore_signal(
            barrier, inc=1, device_id=peer_of(*peer), device_id_type=pl.DeviceIdType.MESH
        )
    pl.semaphore_wait(barrier, len(peers))


def run_copies(copies, send_sems, recv_sems):
    started, arrived = {}, set()

    def arrive(name):
        if name not in arrived:
            arrived.add(name)
            started[name].wait_recv()

    for at, (name, awaited, source, target, peer) in enumerate(copies):
        for other in awaited:
            arrive(other)
        started[name] = pltpu.make_async_remote_copy(
            src_ref=source,
            dst_ref=target,
            send_sem=send_sems.at[at],
            recv_sem=recv_sems.at[at],
            device_id=peer_of(*peer),
            device_id_type=pl.DeviceIdType.MESH,
        )
        started[name].start()
    for name in started:
        arrive(name)
    for name in started:
        started[name].wait_send()


def doubling(name, size, order, awaited, block, target):
    hops, held = [], {0: awaited}
    for mask in order:
        hop, got = [], {}
        for r, needs in held.items():
            key = (name, r, mask)
            hop.append((key, needs, block(r), target(r), (0, 0, mask)))
            got[r ^ mask] = (key,)
        held.update(got)
        hops.append(hop)
    return hops, held


def front_masks(ctx_size, fsdp_size, paired):
    chips = ctx_size // 2
    peers = [
        (m, s, 0)
        for m in range(chips)
        for s in range(2)
        if (m or s) and (paired or not m or not s)
    ]
    return peers + [(0, 0, m) for m in range(1, fsdp_size)]


def front_copies(parts, wholes, pair_ref, pair_all, down_ref, down_all, sizes):
    ctx_size, fsdp_size = sizes
    chips = ctx_size // 2
    ctx, fsdp = lax.axis_index("ctx"), lax.axis_index("fsdp")
    chip, side = ctx // 2, ctx % 2
    masks = [1 << bit for bit in range(fsdp_size.bit_length() - 1)]
    orders = [masks, masks[::-1]]
    copies = []
    for n, (own, whole) in enumerate(zip(parts, wholes)):
        for m in range(1, chips):
            copies.append((("z", n, m), (), own, whole.at[chip, side, fsdp], (m, 0, 0)))
    exchange = []
    if pair_ref is not None:
        ff_own = pair_ref.shape[2] // ctx_size
        for m in range(chips):
            for s in range(2):
                if m or s:
                    other = ctx ^ (2 * m + s)
                    columns = pl.ds(pl.multiple_of(other * ff_own, ff_own), ff_own)
                    exchange.append(
                        (
                            ("pair", m, s), (), pair_ref.at[:, :, columns],
                            pair_all.at[:, ctx, fsdp], (m, s, 0),
                        )
                    )
    queues = []
    if down_ref is not None:
        width = down_ref.shape[1] // 2
        lists = []
        for h, order in enumerate(orders):
            cols = pl.ds(h * width, width)
            target = lambda r, cols=cols: down_all.at[fsdp ^ r, :, cols]
            block = lambda r, cols=cols: (
                down_all.at[fsdp ^ r, :, cols] if r else down_ref.at[:, cols]
            )
            lists.append(doubling(("down", h), fsdp_size, order, (), block, target)[0])
        stages = [[copy for pieces in zip(*hop) for copy in pieces] for hop in zip(*lists)]
        queues.append(stages + [[]])
    for n, (own, whole) in enumerate(zip(parts, wholes)):
        width = own.shape[1]
        cut = (width // 2 + LANES - 1) // LANES * LANES
        halves = [(0, cut), (cut, width - cut)]
        for m in range(chips):
            first = (("z", n, m),) if m else ()
            lists, last = [], []
            for h, ((lo, span), order) in enumerate(zip(halves, orders)):
                cols = pl.ds(lo, span)

                def block(r, m=m, cols=cols, own=own, whole=whole):
                    if m == 0 and r == 0:
                        return own.at[:, cols]
                    return whole.at[chip ^ m, side, fsdp ^ r, :, cols]

                def target(r, m=m, cols=cols, whole=whole):
                    return whole.at[chip ^ m, side, fsdp ^ r, :, cols]

                hops, held = doubling(("f", n, m, h), fsdp_size, order, first, block, target)
                lists.append(hops)
                last.extend(key for keys in held.values() for key in keys)
            stages = [[copy for pieces in zip(*hop) for copy in pieces] for hop in zip(*lists)]
            row = whole.at[chip ^ m, side]
            if m:
                stages.append([(("core", n, m), tuple(last), row, row, (0, 1, 0))])
            else:
                stages.append(
                    [
                        (
                            ("core", n, m, r), tuple(last),
                            row.at[fsdp ^ r] if r else own, row.at[fsdp ^ r], (0, 1, 0),
                        )
                        for r in range(fsdp_size)
                    ]
                )
            queues.append(stages)
    sharing = []
    lag = 2
    for turn in range(len(queues) + lag * (len(orders[0]) + 1)):
        for stage in range(len(orders[0]) + 1):
            at = turn - lag * stage
            if 0 <= at < len(queues):
                sharing.extend(queues[at][stage])
        if turn == chips:
            sharing.extend(exchange)
    return copies + sharing


def front_kernel(sizes, count, paired, *refs):
    parts, refs = refs[:count], refs[count:]
    pair_ref, down_ref, refs = (refs[0], refs[1], refs[3:]) if paired else (None, None, refs)
    wholes, refs = refs[:count], refs[count:]
    pair_all, down_all, refs = (refs[0], refs[1], refs[2:]) if paired else (None, None, refs)
    send_sems, recv_sems, own_sems = refs
    greet(front_masks(*sizes, paired))
    ctx, fsdp = lax.axis_index("ctx"), lax.axis_index("fsdp")
    kept = []
    for n, (own, whole) in enumerate(zip(parts, wholes)):
        kept.append(
            pltpu.make_async_copy(own, whole.at[ctx // 2, ctx % 2, fsdp], own_sems.at[n])
        )
    if paired:
        ff_own = pair_ref.shape[2] // sizes[0]
        columns = pl.ds(pl.multiple_of(ctx * ff_own, ff_own), ff_own)
        kept.append(
            pltpu.make_async_copy(
                pair_ref.at[:, :, columns], pair_all.at[:, ctx, fsdp], own_sems.at[count]
            )
        )
        kept.append(
            pltpu.make_async_copy(down_ref, down_all.at[fsdp], own_sems.at[count + 1])
        )
    for copy in kept:
        copy.start()
    copies = front_copies(parts, wholes, pair_ref, pair_all, down_ref, down_all, sizes)
    run_copies(copies, send_sems, recv_sems)
    for copy in kept:
        copy.wait()


def gather_front(parts, pair, down, earlier, sizes, collective_id):
    ctx_size, fsdp_size = sizes
    chips = ctx_size // 2
    rows = parts[0].shape[0]
    paired = pair is not None
    count = len(parts) * (chips - 1 + chips * (2 * (fsdp_size - 1) + 1) + fsdp_size - 1)
    shapes = [
        jax.ShapeDtypeStruct((chips, 2, fsdp_size, rows, part.shape[1]), part.dtype)
        for part in parts
    ]
    if paired:
        count += ctx_size - 1 + 2 * (fsdp_size - 1)
        shapes.append(
            jax.ShapeDtypeStruct(
                (2, ctx_size, fsdp_size, rows, pair.shape[2] // ctx_size), pair.dtype
            )
        )
        shapes.append(jax.ShapeDtypeStruct((fsdp_size,) + down.shape, down.dtype))
    hbm = pl.BlockSpec(memory_space=pl.ANY)
    vmem = pl.BlockSpec(memory_space=pltpu.VMEM)
    return pl.pallas_call(
        functools.partial(front_kernel, sizes, len(parts), paired),
        in_specs=[vmem] * len(shapes) + ([hbm] if paired else []),
        out_specs=[hbm] * len(shapes),
        out_shape=shapes,
        scratch_shapes=[
            pltpu.SemaphoreType.DMA((count,)),
            pltpu.SemaphoreType.DMA((count,)),
            pltpu.SemaphoreType.DMA((len(shapes),)),
        ],
        compiler_params=pltpu.CompilerParams(collective_id=collective_id, has_side_effects=True),
        cost_estimate=pl.CostEstimate(flops=90_000_000_000, bytes_accessed=30_000_000, transcendentals=0),
    )(*parts, *([pair, down, earlier] if paired else []))


def hidden_kernel(sizes, pair_in, pair_all, send_sems, recv_sems):
    ctx_size, fsdp_size = sizes
    fsdp = lax.axis_index("fsdp")
    masks = [1 << bit for bit in range(fsdp_size.bit_length() - 1)]
    greet([(0, 0, m) for m in masks])
    lists = []
    for h, order in enumerate([masks, masks[::-1]]):
        view = lambda r, h=h: pair_all.at[h, :, fsdp ^ r]
        lists.append(doubling(("pair", h), fsdp_size, order, (), view, view)[0])
    copies = []
    for hop in zip(*lists):
        for pieces in zip(*hop):
            copies.extend(pieces)
    run_copies(copies, send_sems, recv_sems)


def gather_hidden(pair_all, sizes):
    count = 2 * (sizes[1] - 1)
    hbm = pl.BlockSpec(memory_space=pl.ANY)
    return pl.pallas_call(
        functools.partial(hidden_kernel, sizes),
        in_specs=[hbm],
        out_specs=hbm,
        out_shape=jax.ShapeDtypeStruct(pair_all.shape, pair_all.dtype),
        input_output_aliases={0: 0},
        scratch_shapes=[pltpu.SemaphoreType.DMA((count,)), pltpu.SemaphoreType.DMA((count,))],
        compiler_params=pltpu.CompilerParams(collective_id=2, has_side_effects=True),
        cost_estimate=pl.CostEstimate(flops=60_000_000_000, bytes_accessed=30_000_000, transcendentals=0),
    )(pair_all)


def hop_slots(size, order):
    slots, held = [], list(range(size))
    for mask in order:
        held = [r for r in held if not r & mask]
        slots.append(held)
    return slots


def remote(source, target, send_sem, recv_sem, peer):
    return pltpu.make_async_remote_copy(
        src_ref=source,
        dst_ref=target,
        send_sem=send_sem,
        recv_sem=recv_sem,
        device_id=peer_of(*peer),
        device_id_type=pl.DeviceIdType.MESH,
    )


def reduce_kernel(
    sizes, chunk, products, extras, lefts, right, extra, total, terms, core_got, line_sent, line_got,
    core_send, core_recv, hop_send, hop_recv, line_send, line_recv, *hop_buffers
):
    ctx_size, fsdp_size = sizes
    chips = ctx_size // 2
    rows = total.shape[0]
    count = products + extras
    half = chunk // 2
    masks = [1 << bit for bit in range(fsdp_size.bit_length() - 1)]
    orders = [masks, masks[::-1]]
    bits = len(masks)
    hops = [
        [hop_buffers[(h * bits + j) * 2 : (h * bits + j) * 2 + 2] for j in range(bits)]
        for h in range(2)
    ]
    slots = [hop_slots(fsdp_size, order) for order in orders]
    ctx, fsdp = lax.axis_index("ctx"), lax.axis_index("fsdp")
    chip, side = ctx // 2, ctx % 2
    greet(
        [(0, 1, 0)] + [(0, 0, m) for m in masks] + [(m, 0, 0) for m in range(1, chips)]
    )

    def core_copy(i):
        return remote(
            terms.at[i, :, 1 - side], core_got.at[i], core_send.at[i], core_recv.at[i], (0, 1, 0)
        )

    def hop_copy(h, j, i):
        sent, got = hops[h][j]
        return remote(
            sent.at[i], got.at[i], hop_send.at[h, j, i], hop_recv.at[h, j, i], (0, 0, orders[h][j])
        )

    def line_copy(m, i):
        return remote(
            line_sent.at[i, m - 1], line_got.at[i, m - 1],
            line_send.at[i, m - 1], line_recv.at[i, m - 1], (m, 0, 0),
        )

    def held(h, upto, i, z, r):
        cols = pl.ds(h * half, half)
        value = terms[i, z, side, fsdp ^ r, :, cols].astype(jnp.float32)
        value += core_got[i, z, fsdp ^ r, :, cols].astype(jnp.float32)
        for j in range(upto):
            value += hops[h][j][1][i, slots[h][j].index(r), z].astype(jnp.float32)
        return value

    def step(t, carry):
        @pl.when(t < products)
        def _():
            per_left = products // lefts.shape[0]
            cols = pl.ds(pl.multiple_of(t * chunk, chunk), chunk)
            term = jnp.dot(
                lefts[t // per_left], right[:, cols], preferred_element_type=jnp.float32
            )
            terms[t] = term.astype(jnp.bfloat16).reshape(terms.shape[1:])

        if extras:
            @pl.when((t >= products) & (t < count))
            def _():
                terms[t] = extra[t - products].reshape(terms.shape[1:])

        @pl.when(t < count)
        def _():
            core_copy(t).start()

        for j in range(bits):
            @pl.when((t >= j + 1) & (t < count + j + 1))
            def _(j=j):
                i = t - (j + 1)
                if j == 0:
                    core_copy(i).wait_recv()
                for h in range(2):
                    if j:
                        hop_copy(h, j - 1, i).wait_recv()
                    for s, r in enumerate(slots[h][j]):
                        for z in range(chips):
                            hops[h][j][0][i, s, z] = held(h, j, i, z, r | orders[h][j]).astype(
                                jnp.bfloat16
                            )
                    hop_copy(h, j, i).start()

        @pl.when((t >= bits + 1) & (t < count + bits + 1))
        def _():
            i = t - (bits + 1)
            for h in range(2):
                hop_copy(h, bits - 1, i).wait_recv()
                for m in range(1, chips):
                    line_sent[i, m - 1, :, h * half : (h + 1) * half] = held(
                        h, bits, i, chip ^ m, 0
                    ).astype(jnp.bfloat16)
            for m in range(1, chips):
                line_copy(m, i).start()

        @pl.when(t >= bits + 2)
        def _():
            i = t - (bits + 2)
            for m in range(1, chips):
                line_copy(m, i).wait_recv()
            for h in range(2):
                value = held(h, bits, i, chip, 0)
                for m in range(1, chips):
                    value += line_got[i, m - 1, :, h * half : (h + 1) * half].astype(jnp.float32)
                total[:, pl.ds(pl.multiple_of(i * chunk + h * half, half), half)] = value

        return carry

    lax.fori_loop(0, count + bits + 2, step, 0)

    def finish(i, carry):
        core_copy(i).wait_send()
        for h in range(2):
            for j in range(bits):
                hop_copy(h, j, i).wait_send()
        for m in range(1, chips):
            line_copy(m, i).wait_send()
        return carry

    lax.fori_loop(0, count, finish, 0)


def reduce_rows(lefts, right, extra, chunk, sizes, collective_id):
    ctx_size, fsdp_size = sizes
    chips = ctx_size // 2
    depth = lefts.shape[1]
    rows = depth // (ctx_size * fsdp_size)
    products = right.shape[1] // chunk
    extras = 0 if extra is None else extra.shape[0]
    if extra is None:
        extra = jnp.zeros((1, 16, LANES), jnp.bfloat16)
    count = products + extras
    bits = fsdp_size.bit_length() - 1
    half = chunk // 2
    buffers = []
    for _ in range(2):
        for j in range(bits):
            shape = (count, fsdp_size >> (j + 1), chips, rows, half)
            buffers += [pltpu.VMEM(shape, jnp.bfloat16)] * 2
    line = pltpu.VMEM((count, max(chips - 1, 1), rows, chunk), jnp.bfloat16)
    vmem = pl.BlockSpec(memory_space=pltpu.VMEM)
    return pl.pallas_call(
        functools.partial(reduce_kernel, sizes, chunk, products, extras),
        in_specs=[vmem] * 3,
        out_specs=vmem,
        out_shape=jax.ShapeDtypeStruct((rows, count * chunk), jnp.float32),
        scratch_shapes=[
            pltpu.VMEM((count, chips, 2, fsdp_size, rows, chunk), jnp.bfloat16),
            pltpu.VMEM((count, chips, fsdp_size, rows, chunk), jnp.bfloat16),
            line,
            line,
            pltpu.SemaphoreType.DMA((count,)),
            pltpu.SemaphoreType.DMA((count,)),
            pltpu.SemaphoreType.DMA((2, bits, count)),
            pltpu.SemaphoreType.DMA((2, bits, count)),
            pltpu.SemaphoreType.DMA((count, max(chips - 1, 1))),
            pltpu.SemaphoreType.DMA((count, max(chips - 1, 1))),
        ]
        + buffers,
        compiler_params=pltpu.CompilerParams(
            collective_id=collective_id, has_side_effects=True, vmem_limit_bytes=56 * 1024 * 1024
        ),
        cost_estimate=pl.CostEstimate(flops=80_000_000_000, bytes_accessed=30_000_000, transcendentals=0),
    )(lefts, right, extra)


def hidden_grad_kernel(
    sizes, normed, gate, up, pair_sum, terms, pair_sent, pair_got, pair_send, pair_recv
):
    ctx_size, fsdp_size = sizes
    count, span = terms.shape[1], normed.shape[1] // terms.shape[1]
    masks = [1 << bit for bit in range(fsdp_size.bit_length() - 1)]
    orders = [masks, masks[::-1]]
    bits = len(masks)
    slots = [hop_slots(fsdp_size, order) for order in orders]
    fsdp = lax.axis_index("fsdp")
    greet([(0, 0, m) for m in masks])
    first = [sum(fsdp_size >> (k + 1) for k in range(j)) for j in range(bits)]

    def pair_copy(h, j, i):
        rows = pl.ds(first[j], fsdp_size >> (j + 1))
        return remote(
            pair_sent.at[h, i, rows], pair_got.at[h, i, rows],
            pair_send.at[h, j, i], pair_recv.at[h, j, i], (0, 0, orders[h][j]),
        )

    def pair_held(h, upto, i, r):
        value = terms[h, i, fsdp ^ r].astype(jnp.float32)
        for j in range(upto):
            value += pair_got[h, i, first[j] + slots[h][j].index(r)].astype(jnp.float32)
        return value

    def step(t, carry):
        @pl.when(t < count)
        def _():
            columns = normed[:, pl.ds(pl.multiple_of(t * span, span), span)]
            for h, grad in enumerate((gate, up)):
                term = across(columns, grad[...])
                terms[h, t] = term.astype(jnp.bfloat16).reshape(terms.shape[2:])

        for j in range(bits):
            @pl.when((t >= j) & (t < count + j))
            def _(j=j):
                i = t - j
                for h in range(2):
                    if j:
                        pair_copy(h, j - 1, i).wait_recv()
                    for s, r in enumerate(slots[h][j]):
                        pair_sent[h, i, first[j] + s] = pair_held(
                            h, j, i, r | orders[h][j]
                        ).astype(jnp.bfloat16)
                    pair_copy(h, j, i).start()

        @pl.when(t >= bits)
        def _():
            i = t - bits
            for h in range(2):
                pair_copy(h, bits - 1, i).wait_recv()
                pair_sum[i, h] = pair_held(h, bits, i, 0).astype(jnp.bfloat16)

        return carry

    lax.fori_loop(0, count + bits, step, 0)

    def finish(i, carry):
        for h in range(2):
            for j in range(bits):
                pair_copy(h, j, i).wait_send()
        return carry

    lax.fori_loop(0, count, finish, 0)


def reduce_hidden(normed, gate, up, sizes):
    ctx_size, fsdp_size = sizes
    bits = fsdp_size.bit_length() - 1
    rows, columns = normed.shape[1] // (ctx_size * fsdp_size), gate.shape[1]
    pair = pltpu.VMEM((2, ctx_size, fsdp_size - 1, rows, columns), jnp.bfloat16)
    vmem = pl.BlockSpec(memory_space=pltpu.VMEM)
    return pl.pallas_call(
        functools.partial(hidden_grad_kernel, sizes),
        in_specs=[vmem] * 3,
        out_specs=vmem,
        out_shape=jax.ShapeDtypeStruct((ctx_size, 2, rows, columns), jnp.bfloat16),
        scratch_shapes=[
            pltpu.VMEM((2, ctx_size, fsdp_size, rows, columns), jnp.bfloat16), pair, pair,
        ]
        + [pltpu.SemaphoreType.DMA((2, bits, ctx_size))] * 2,
        compiler_params=pltpu.CompilerParams(
            collective_id=3, has_side_effects=True, vmem_limit_bytes=60 * 1024 * 1024
        ),
        cost_estimate=pl.CostEstimate(flops=60_000_000_000, bytes_accessed=30_000_000, transcendentals=0),
    )(normed, gate, up)


def local(
    tokens,
    cotangent,
    lengths,
    attn_gain,
    query_weight,
    key_weight,
    value_weight,
    out_weight,
    mlp_gain,
    gate_weight,
    up_weight,
    down_weight,
):
    both = ("ctx", "fsdp")
    ctx_size = lax.axis_size("ctx")
    fsdp_size = lax.axis_size("fsdp")
    chips = ctx_size // 2
    stream = tokens[0].astype(jnp.float32)
    tok_rows = stream.shape[0]
    own_rows = query_weight.shape[0]
    kv_width = KV_HEADS * HEAD_DIM
    ff_own = FF // ctx_size
    reach_blocks = WINDOW // STRETCH
    ctx_place = lax.axis_index("ctx")
    doc_lengths = lengths[0]
    query_index = ctx_place * tok_rows + jnp.arange(tok_rows, dtype=jnp.int32)
    key_index = (ctx_place - reach_blocks) * tok_rows + jnp.arange(
        (reach_blocks + 1) * tok_rows, dtype=jnp.int32
    )
    query_doc = doc_segment(doc_lengths, query_index)
    key_doc = doc_segment(doc_lengths, key_index)
    position = doc_position(doc_lengths, query_index, query_doc)
    visible = (key_index[:, None] >= 0) & (key_index[:, None] <= query_index[None, :])
    visible = (
        visible
        & (query_index[None, :] - key_index[:, None] < WINDOW)
        & (query_doc[None, :] == key_doc[:, None])
    )
    bias = jnp.where(visible, 0.0, -1e30).astype(jnp.float32)
    cosine, sine = turn_tables(position)

    cot_all = lax.all_gather(cotangent[0], "ctx", axis=0, tiled=True)

    sizes = (ctx_size, fsdp_size)
    gains = jnp.zeros((own_rows, LANES), jnp.bfloat16)
    gains = gains.at[:, 0].set(attn_gain).at[:, 1].set(mlp_gain)
    (kv_all,) = gather_front(
        (jnp.concatenate([key_weight, value_weight, gains], axis=1),), None, None, None, sizes, 1
    )
    kv_all = kv_all.reshape(D, -1)
    gain_one = kv_all[:, 2 * kv_width].astype(jnp.float32)
    gain_two = kv_all[:, 2 * kv_width + 1].astype(jnp.float32)

    inv_one = lax.rsqrt(jnp.mean(stream * stream, axis=1, keepdims=True) + EPS)
    normal_one = stream * inv_one
    normed_one = (normal_one * gain_one).astype(jnp.bfloat16)
    kv_front = product(normed_one, kv_all)
    key_low = rope(kv_front[:, :kv_width], cosine, sine).astype(jnp.bfloat16)
    value_low = kv_front[:, kv_width : 2 * kv_width].astype(jnp.bfloat16)
    own_pair = jnp.concatenate([key_low, value_low], axis=1)
    query_all, out_all, pair_all, down_own = gather_front(
        (after(query_weight, own_pair), out_weight),
        jnp.stack([gate_weight, up_weight]),
        down_weight, cot_all, sizes, 6,
    )
    down_own = down_own.reshape(ff_own, D)
    query_all = query_all.reshape(D, D)
    out_all = out_all.reshape(D, D)
    blocks = [own_pair]
    for step in range(1, reach_blocks + 1):
        blocks.insert(0, passed_along(own_pair, "ctx", step))
    window = jnp.concatenate(blocks, axis=0)
    key_window, value_window = window[:, :kv_width], window[:, kv_width:]
    query_front = product(normed_one, query_all)
    attn_mix, query_low, log_total = attend_forward(
        query_front, key_window, value_window, bias, cosine, sine
    )
    resid = stream + product(attn_mix, out_all)
    inv_two = lax.rsqrt(jnp.mean(resid * resid, axis=1, keepdims=True) + EPS)
    normal_two = resid * inv_two
    normed_two = (normal_two * gain_two).astype(jnp.bfloat16)

    normed_all = lax.all_gather(normed_two, "ctx", axis=0, tiled=True)
    pair = gather_hidden(after(pair_all, normed_two), sizes)
    pair = pair.reshape(2, D, ff_own)
    gate_own, up_own = pair[0], pair[1]
    gate_sum = product(normed_all, gate_own)
    up_sum = product(normed_all, up_own)
    sigmoid_gate = jax.nn.sigmoid(gate_sum)
    silu_gate = gate_sum * sigmoid_gate
    hidden = (silu_gate * up_sum).astype(jnp.bfloat16)
    down_part = product(hidden, down_own).astype(jnp.bfloat16)
    grad_hidden = against(cot_all, down_own)
    grad_gate_low = (
        grad_hidden * up_sum * sigmoid_gate * (1.0 + gate_sum * (1.0 - sigmoid_gate))
    ).astype(jnp.bfloat16)
    grad_up_low = (grad_hidden * silu_gate).astype(jnp.bfloat16)
    columns_part = against(grad_gate_low, gate_own) + against(grad_up_low, up_own)
    half = D // 2
    first_sum = lax.psum_scatter(
        down_part[:, :half], "ctx", scatter_dimension=0, tiled=True
    )
    columns = lax.psum_scatter(
        after(columns_part.astype(jnp.bfloat16), first_sum), "ctx", scatter_dimension=0, tiled=True
    )
    down_terms = across(hidden, cot_all).astype(jnp.bfloat16)
    pair_sum = reduce_hidden(
        normed_all, after(grad_gate_low, down_terms), grad_up_low, sizes
    )
    grad_down = lax.psum_scatter(
        after(down_terms, columns, pair_sum), "fsdp", scatter_dimension=0, tiled=True
    )
    second_sum = lax.psum_scatter(
        after(down_part[:, half:], grad_down), "ctx", scatter_dimension=0, tiled=True
    )
    down_sum = jnp.concatenate([first_sum, second_sum], axis=1)
    columns = columns.astype(jnp.float32)
    mixed = (resid + down_sum.astype(jnp.float32)).astype(jnp.bfloat16)

    pair_sum = lax.all_to_all(pair_sum, "ctx", split_axis=0, concat_axis=0, tiled=True)
    grad_stream = cotangent[0].astype(jnp.float32)
    mlp_gain_local = jnp.sum(columns * normal_two, axis=0)
    grad_resid = grad_stream + norm_back(columns * gain_two, normal_two, inv_two)
    grad_resid_low = grad_resid.astype(jnp.bfloat16)
    grad_mix_low = against(grad_resid_low, out_all).astype(jnp.bfloat16)
    grad_query_low, grad_key_window, grad_value_window = attend_backward(
        query_low, key_window, value_window, grad_mix_low, attn_mix, log_total, bias, cosine, sine
    )
    wide_grad = reduce_rows(
        jnp.stack([normed_one.T, attn_mix.T]),
        after(jnp.concatenate([grad_query_low, grad_resid_low], axis=1), second_sum),
        None, 512, sizes, 4,
    )
    own_start = reach_blocks * tok_rows
    grad_pair = jnp.concatenate([grad_key_window, grad_value_window], axis=1)
    grad_pair_total = after(grad_pair[own_start:], wide_grad)
    grad_pair_low = grad_pair[:own_start].astype(jnp.bfloat16)
    for step in range(1, reach_blocks + 1):
        first_row = (reach_blocks - step) * tok_rows
        later = passed_along(grad_pair_low[first_row : first_row + tok_rows], "ctx", -step)
        grad_pair_total = grad_pair_total + later.astype(jnp.float32)
    grad_key_low = rope(grad_pair_total[:, :kv_width], cosine, -sine).astype(jnp.bfloat16)
    grad_value_low = grad_pair_total[:, kv_width:].astype(jnp.bfloat16)
    kv_low = jnp.concatenate([grad_key_low, grad_value_low], axis=1)
    grad_normed_one = against(grad_query_low, query_all) + against(
        jnp.pad(kv_low, ((0, 0), (0, LANES))), kv_all
    )
    attn_gain_local = jnp.sum(grad_normed_one * normal_one, axis=0)
    gain_terms = jnp.stack([attn_gain_local, mlp_gain_local], axis=1).astype(jnp.bfloat16)
    gain_terms = jnp.pad(gain_terms, ((0, 0), (0, 2 * LANES - 2)))[None]
    kv_grad = reduce_rows(normed_one.T[None], kv_low, gain_terms, 2 * LANES, sizes, 5)
    pair_sum = after(pair_sum, kv_grad)
    pair_sum = pair_sum.transpose(1, 2, 0, 3).reshape(2, own_rows, FF).astype(jnp.float32)
    grad_input = grad_resid + norm_back(grad_normed_one * gain_one, normal_one, inv_one)
    return (
        mixed[None],
        grad_input.astype(jnp.bfloat16)[None],
        kv_grad[:, 2 * kv_width],
        wide_grad[:, :D],
        kv_grad[:, :kv_width],
        kv_grad[:, kv_width : 2 * kv_width],
        wide_grad[:, D:],
        kv_grad[:, 2 * kv_width + 1],
        pair_sum[0],
        pair_sum[1],
        grad_down.astype(jnp.float32),
    )


def solution(mesh):
    in_specs = (
        P("fsdp", "ctx", None),
        P("fsdp", "ctx", None),
        P("fsdp", None),
        P(("ctx", "fsdp")),
        P(("ctx", "fsdp"), None),
        P(("ctx", "fsdp"), None),
        P(("ctx", "fsdp"), None),
        P(("ctx", "fsdp"), None),
        P(("ctx", "fsdp")),
        P(("ctx", "fsdp"), None),
        P(("ctx", "fsdp"), None),
        P(("ctx", "fsdp"), None),
    )
    out_specs = (
        P("fsdp", "ctx", None),
        P("fsdp", "ctx", None),
        P(("ctx", "fsdp")),
        P(("ctx", "fsdp"), None),
        P(("ctx", "fsdp"), None),
        P(("ctx", "fsdp"), None),
        P(("ctx", "fsdp"), None),
        P(("ctx", "fsdp")),
        P(("ctx", "fsdp"), None),
        P(("ctx", "fsdp"), None),
        P(("ctx", "fsdp"), None),
    )
    return jax.shard_map(local, mesh=mesh, in_specs=in_specs, out_specs=out_specs, check_vma=False)
```

```python
import functools

import jax
import jax.numpy as jnp
from jax import lax
from jax.experimental import pallas as pl
from jax.experimental.pallas import tpu as pltpu
from jax.sharding import PartitionSpec as P

D = 2048
FF = 8192
HEADS = 32
KV_HEADS = 8
HEAD_DIM = 64
WINDOW = 1024
STRETCH = 256
QTILE = 128
LANES = 128
EPS = 1e-05
THETA = 500000.0


def passed_along(x, axis, by):
    size = lax.axis_size(axis)
    pairs = [(i, i + by) for i in range(size) if 0 <= i + by < size]
    return lax.ppermute(x, axis, pairs)


def product(left, right):
    return jnp.dot(left, right, preferred_element_type=jnp.float32)


def against(left, right):
    return lax.dot_general(
        left, right, (((1,), (1,)), ((), ())), preferred_element_type=jnp.float32
    )


def across(left, right):
    return lax.dot_general(
        left, right, (((0,), (0,)), ((), ())), preferred_element_type=jnp.float32
    )


def doc_segment(doc_lengths, index):
    doc_ends = jnp.cumsum(doc_lengths)
    return jnp.sum((index[:, None] >= doc_ends[None, :]).astype(jnp.int32), axis=1)


def doc_position(doc_lengths, index, segment):
    doc_ends = jnp.cumsum(doc_lengths)
    doc_starts = doc_ends - doc_lengths
    member = segment[:, None] == jnp.arange(doc_lengths.shape[0], dtype=jnp.int32)[None, :]
    return index - jnp.sum(jnp.where(member, doc_starts[None, :], 0), axis=1)


def swap_halves(u):
    half = HEAD_DIM // 2
    width = u.shape[1]
    lane = lax.broadcasted_iota(jnp.int32, u.shape, 1)
    ahead = pltpu.roll(u, width - half, 1)
    behind = pltpu.roll(u, half, 1)
    return jnp.where(lane % HEAD_DIM < half, ahead, behind)


def turn(u, cosine, sine):
    copies = u.shape[1] // cosine.shape[1]
    cosine = jnp.concatenate([cosine] * copies, axis=1)
    sine = jnp.concatenate([sine] * copies, axis=1)
    return u * cosine + swap_halves(u) * sine


def nt(left, right):
    return lax.dot_general(left, right, (((1,), (1,)), ((), ())), preferred_element_type=jnp.float32)


def nn(left, right):
    return lax.dot_general(left, right, (((1,), (0,)), ((), ())), preferred_element_type=jnp.float32)


def attend_forward_kernel(
    q_ref, k_ref, v_ref, bias_ref, cos_ref, sin_ref, o_ref, qr_ref, lse_ref
):
    rows = q_ref.shape[0]
    group = HEADS // KV_HEADS
    span = k_ref.shape[0] - rows + QTILE
    rotated = turn(q_ref[...], cos_ref[...], sin_ref[...])
    qr_ref[...] = rotated.astype(jnp.bfloat16)
    scaled = (qr_ref[...].astype(jnp.float32) * HEAD_DIM ** (-0.5)).astype(jnp.bfloat16)
    for tile in range(rows // QTILE):
        first = tile * QTILE
        bias = bias_ref[first : first + span, first : first + QTILE]
        for kv in range(LANES // HEAD_DIM):
            lo = kv * HEAD_DIM
            keys = k_ref[first : first + span, lo : lo + HEAD_DIM]
            values = v_ref[first : first + span, lo : lo + HEAD_DIM]
            values_t = values.T
            raises, totals = [], []
            for h in range(group):
                head = kv * group + h
                q_h = scaled[first : first + QTILE, head * HEAD_DIM : (head + 1) * HEAD_DIM]
                s = nt(keys, q_h) + bias
                top = jnp.max(s, axis=0, keepdims=True)
                raised = jnp.exp(s - top)
                total = jnp.sum(raised, axis=0, keepdims=True)
                lse_ref[head : head + 1, first : first + QTILE] = top + jnp.log(total)
                raises.append(raised.astype(jnp.bfloat16))
                totals.append(total)
            o_wide = nn(values_t, jnp.concatenate(raises, axis=1)) / jnp.concatenate(totals, axis=1)
            o_t = jnp.concatenate(
                [o_wide[:, h * QTILE : (h + 1) * QTILE] for h in range(group)], axis=0
            )
            o_ref[first : first + QTILE, kv * group * HEAD_DIM : (kv + 1) * group * HEAD_DIM] = (
                o_t.T.astype(jnp.bfloat16)
            )


def attend_forward(q, k, v, bias, cosine, sine):
    rows, width = q.shape
    steps = KV_HEADS * HEAD_DIM // LANES
    qw = width // steps
    heads = HEADS // steps
    window = k.shape[0]
    return pl.pallas_call(
        attend_forward_kernel,
        grid=(steps,),
        in_specs=[
            pl.BlockSpec((rows, qw), lambda i: (0, i)),
            pl.BlockSpec((window, LANES), lambda i: (0, i)),
            pl.BlockSpec((window, LANES), lambda i: (0, i)),
            pl.BlockSpec((window, rows), lambda i: (0, 0)),
            pl.BlockSpec((rows, LANES), lambda i: (0, 0)),
            pl.BlockSpec((rows, LANES), lambda i: (0, 0)),
        ],
        out_specs=[
            pl.BlockSpec((rows, qw), lambda i: (0, i)),
            pl.BlockSpec((rows, qw), lambda i: (0, i)),
            pl.BlockSpec((heads, rows), lambda i: (i, 0)),
        ],
        out_shape=[
            jax.ShapeDtypeStruct((rows, width), jnp.bfloat16),
            jax.ShapeDtypeStruct((rows, width), jnp.bfloat16),
            jax.ShapeDtypeStruct((HEADS, rows), jnp.float32),
        ],
        compiler_params=pltpu.CompilerParams(vmem_limit_bytes=48 * 1024 * 1024),
        cost_estimate=pl.CostEstimate(flops=40_000_000_000, bytes_accessed=10_000_000, transcendentals=0),
    )(q, k, v, bias, cosine, sine)


def attend_backward_kernel(
    qr_ref, k_ref, v_ref, do_ref, o_ref, lse_ref, bias_ref, cos_ref, sin_ref, earlier,
    dq_ref, dk_ref, dv_ref
):
    rows = qr_ref.shape[0]
    group = HEADS // KV_HEADS
    span = k_ref.shape[0] - rows + QTILE
    scale = HEAD_DIM ** (-0.5)
    dk_ref[...] = jnp.zeros_like(dk_ref)
    dv_ref[...] = jnp.zeros_like(dv_ref)
    scaled = (qr_ref[...].astype(jnp.float32) * scale).astype(jnp.bfloat16)
    wide = LANES // HEAD_DIM * group * HEAD_DIM
    owner = lax.broadcasted_iota(jnp.int32, (8, wide), 1) // HEAD_DIM
    pick = (owner == lax.broadcasted_iota(jnp.int32, (8, wide), 0)).astype(jnp.float32)
    for tile in range(rows // QTILE):
        first = tile * QTILE
        bias = bias_ref[first : first + span, first : first + QTILE]
        both = do_ref[first : first + QTILE, :].astype(jnp.float32) * o_ref[
            first : first + QTILE, :
        ].astype(jnp.float32)
        delta = lax.dot_general(
            pick, both, (((1,), (1,)), ((), ())),
            precision=lax.Precision.HIGHEST, preferred_element_type=jnp.float32,
        )
        dk_pair, dv_pair, dqs = [], [], []
        for kv in range(LANES // HEAD_DIM):
            lo = kv * HEAD_DIM
            keys = k_ref[first : first + span, lo : lo + HEAD_DIM]
            values = v_ref[first : first + span, lo : lo + HEAD_DIM]
            keys_t = keys.T
            probs, slopes, qs, dos = [], [], [], []
            for h in range(group):
                head = kv * group + h
                cols = slice(head * HEAD_DIM, (head + 1) * HEAD_DIM)
                q_h = scaled[first : first + QTILE, cols]
                do_h = do_ref[first : first + QTILE, cols]
                s = nt(keys, q_h) + bias
                p = jnp.exp(s - lse_ref[head : head + 1, first : first + QTILE])
                dp = nt(values, do_h)
                ds = (p * (dp - delta[head : head + 1, :])).astype(jnp.bfloat16)
                probs.append(p.astype(jnp.bfloat16))
                slopes.append(ds)
                qs.append(q_h)
                dos.append(do_h)
            p_all = jnp.concatenate(probs, axis=1)
            ds_all = jnp.concatenate(slopes, axis=1)
            dv_pair.append(nn(p_all, jnp.concatenate(dos, axis=0)))
            dk_pair.append(nn(ds_all, jnp.concatenate(qs, axis=0)))
            dq_t = nn(keys_t, ds_all) * scale
            dqs.extend(dq_t[:, h * QTILE : (h + 1) * QTILE] for h in range(group))
        dk_ref[first : first + span, :] += jnp.concatenate(dk_pair, axis=1)
        dv_ref[first : first + span, :] += jnp.concatenate(dv_pair, axis=1)
        dq = jnp.concatenate(dqs, axis=0).T
        dq_ref[first : first + QTILE, :] = turn(
            dq, cos_ref[first : first + QTILE, :], -sin_ref[first : first + QTILE, :]
        ).astype(jnp.bfloat16)


def attend_backward(qr, k, v, do, o, lse, bias, cosine, sine, earlier):
    rows, width = qr.shape
    steps = KV_HEADS * HEAD_DIM // LANES
    qw = width // steps
    heads = HEADS // steps
    window = k.shape[0]
    wide = pl.BlockSpec((rows, qw), lambda i: (0, i))
    tall = pl.BlockSpec((window, LANES), lambda i: (0, i))
    table = pl.BlockSpec((rows, LANES), lambda i: (0, 0))
    return pl.pallas_call(
        attend_backward_kernel,
        grid=(steps,),
        in_specs=[
            wide, tall, tall, wide, wide,
            pl.BlockSpec((heads, rows), lambda i: (i, 0)),
            pl.BlockSpec((window, rows), lambda i: (0, 0)),
            table, table,
            pl.BlockSpec(memory_space=pl.ANY),
        ],
        out_specs=[wide, tall, tall],
        out_shape=[
            jax.ShapeDtypeStruct((rows, width), jnp.bfloat16),
            jax.ShapeDtypeStruct(k.shape, jnp.float32),
            jax.ShapeDtypeStruct(k.shape, jnp.float32),
        ],
        compiler_params=pltpu.CompilerParams(vmem_limit_bytes=48 * 1024 * 1024),
        cost_estimate=pl.CostEstimate(flops=80_000_000_000, bytes_accessed=20_000_000, transcendentals=0),
    )(qr, k, v, do, o, lse, bias, cosine, sine, earlier)


def turn_tables(position):
    half_dim = HEAD_DIM // 2
    frequency = THETA ** (-2.0 * jnp.arange(half_dim, dtype=jnp.float32) / HEAD_DIM)
    angles = position.astype(jnp.float32)[:, None] * frequency[None, :]
    cosine, sine = jnp.cos(angles), jnp.sin(angles)
    copies = LANES // HEAD_DIM
    return (
        jnp.concatenate([cosine, cosine] * copies, axis=1),
        jnp.concatenate([-sine, sine] * copies, axis=1),
    )


def rope(u, cosine, sine):
    half = HEAD_DIM // 2
    parts = u.reshape(u.shape[0], -1, 2, half)
    swapped_parts = parts[:, :, ::-1, :].reshape(u.shape)
    copies = u.shape[1] // LANES
    return u * jnp.tile(cosine, (1, copies)) + swapped_parts * jnp.tile(sine, (1, copies))


def norm_back(grad_normal, normal, inverse):
    return inverse * (grad_normal - normal * jnp.mean(grad_normal * normal, axis=1, keepdims=True))


def after(x, *others):
    return lax.optimization_barrier((x,) + others)[0]


def peer_of(chip_mask, side_mask, fsdp_mask):
    ctx = lax.axis_index("ctx")
    return (ctx ^ (2 * chip_mask + side_mask), lax.axis_index("fsdp") ^ fsdp_mask)


def greet(peers):
    barrier = pltpu.get_barrier_semaphore()
    for peer in peers:
        pl.semaphore_signal(
            barrier, inc=1, device_id=peer_of(*peer), device_id_type=pl.DeviceIdType.MESH
        )
    pl.semaphore_wait(barrier, len(peers))


def run_copies(copies, send_sems, recv_sems):
    started, arrived = {}, set()

    def arrive(name):
        if name not in arrived:
            arrived.add(name)
            started[name].wait_recv()

    for at, (name, awaited, source, target, peer) in enumerate(copies):
        for other in awaited:
            arrive(other)
        started[name] = pltpu.make_async_remote_copy(
            src_ref=source,
            dst_ref=target,
            send_sem=send_sems.at[at],
            recv_sem=recv_sems.at[at],
            device_id=peer_of(*peer),
            device_id_type=pl.DeviceIdType.MESH,
        )
        started[name].start()
    for name in started:
        arrive(name)
    for name in started:
        started[name].wait_send()


def doubling(name, size, order, awaited, block, target, along=2):
    hops, held = [], {0: awaited}
    for mask in order:
        hop, got = [], {}
        for r, needs in held.items():
            key = (name, r, mask)
            peer = tuple(mask if place == along else 0 for place in range(3))
            hop.append((key, needs, block(r), target(r), peer))
            got[r ^ mask] = (key,)
        held.update(got)
        hops.append(hop)
    return hops, held


def line_gather(name, own, whole, sizes):
    chips = sizes[0] // 2
    ctx = lax.axis_index("ctx")
    chip, side = ctx // 2, ctx % 2
    far_first = [1 << bit for bit in range(chips.bit_length() - 1)][::-1]
    target = lambda r: whole.at[chip ^ r, side]
    block = lambda r: target(r) if r else own
    hops, held = doubling((name, "z"), chips, far_first, (), block, target, 0)
    last = [
        ((name, "core", r), held[r], block(r), target(r), (0, 1, 0)) for r in range(chips)
    ]
    return hops + [last]


def front_masks(ctx_size, fsdp_size, paired):
    chips = ctx_size // 2
    peers = [
        (m, s, 0)
        for m in range(chips)
        for s in range(2)
        if (m or s) and (paired or m + s == 1 or (not s and not m & (m - 1)))
    ]
    return peers + [(0, 0, m) for m in range(1, fsdp_size)]


def front_copies(parts, wholes, pair_ref, pair_all, down_ref, down_all, line, sizes):
    ctx_size, fsdp_size = sizes
    chips = ctx_size // 2
    ctx, fsdp = lax.axis_index("ctx"), lax.axis_index("fsdp")
    chip, side = ctx // 2, ctx % 2
    masks = [1 << bit for bit in range(fsdp_size.bit_length() - 1)]
    orders = [masks, masks[::-1]]
    far_first = [1 << bit for bit in range(chips.bit_length() - 1)][::-1]
    copies, arrival = [], {}
    lines = []
    for n, (own, whole) in enumerate(zip(parts, wholes)):
        view = lambda r, own=own, whole=whole: (
            whole.at[chip ^ r, side, fsdp] if r else own
        )
        target = lambda r, whole=whole: whole.at[chip ^ r, side, fsdp]
        hops, held = doubling(("z", n), chips, far_first, (), view, target, 0)
        lines.append(hops)
        for r, keys in held.items():
            arrival[n, r] = keys
    for hop in zip(*lines):
        for pieces in hop:
            copies.extend(pieces)
    exchange = []
    if pair_ref is not None:
        ff_own = pair_ref.shape[2] // ctx_size
        for m in range(chips):
            for s in range(2):
                if m or s:
                    other = ctx ^ (2 * m + s)
                    columns = pl.ds(pl.multiple_of(other * ff_own, ff_own), ff_own)
                    exchange.append(
                        (
                            ("pair", m, s), (), pair_ref.at[:, :, columns],
                            pair_all.at[:, ctx, fsdp], (m, s, 0),
                        )
                    )
    queues = []
    if down_ref is not None:
        width = down_ref.shape[1] // 2
        lists = []
        for h, order in enumerate(orders):
            cols = pl.ds(h * width, width)
            target = lambda r, cols=cols: down_all.at[fsdp ^ r, :, cols]
            block = lambda r, cols=cols: (
                down_all.at[fsdp ^ r, :, cols] if r else down_ref.at[:, cols]
            )
            lists.append(doubling(("down", h), fsdp_size, order, (), block, target)[0])
        stages = [[copy for pieces in zip(*hop) for copy in pieces] for hop in zip(*lists)]
        queues.append(stages + [[]])
    for n, (own, whole) in enumerate(zip(parts, wholes)):
        width = own.shape[1]
        cut = (width // 2 + LANES - 1) // LANES * LANES
        halves = [(0, cut), (cut, width - cut)]
        for m in range(chips):
            first = arrival[n, m]
            lists, last = [], []
            for h, ((lo, span), order) in enumerate(zip(halves, orders)):
                cols = pl.ds(lo, span)

                def block(r, m=m, cols=cols, own=own, whole=whole):
                    if m == 0 and r == 0:
                        return own.at[:, cols]
                    return whole.at[chip ^ m, side, fsdp ^ r, :, cols]

                def target(r, m=m, cols=cols, whole=whole):
                    return whole.at[chip ^ m, side, fsdp ^ r, :, cols]

                hops, held = doubling(("f", n, m, h), fsdp_size, order, first, block, target)
                lists.append(hops)
                last.extend(key for keys in held.values() for key in keys)
            stages = [[copy for pieces in zip(*hop) for copy in pieces] for hop in zip(*lists)]
            row = whole.at[chip ^ m, side]
            if m:
                stages.append([(("core", n, m), tuple(last), row, row, (0, 1, 0))])
            else:
                stages.append(
                    [
                        (
                            ("core", n, m, r), tuple(last),
                            row.at[fsdp ^ r] if r else own, row.at[fsdp ^ r], (0, 1, 0),
                        )
                        for r in range(fsdp_size)
                    ]
                )
            queues.append(stages)
    sharing = []
    lag, done = 2, 0
    for turn in range(len(queues) + lag * (len(orders[0]) + 1)):
        for stage in range(len(orders[0]) + 1):
            at = turn - lag * stage
            if 0 <= at < len(queues):
                sharing.extend(queues[at][stage])
        if turn == chips:
            sharing.extend(exchange)
            for hop in line[:1]:
                sharing.extend(hop)
        if turn > chips and (turn - chips) % 4 == 0 and (turn - chips) // 4 < len(line) - 1:
            sharing.extend(line[(turn - chips) // 4])
            done = (turn - chips) // 4
    for hop in line[done + 1 :]:
        sharing.extend(hop)
    return copies + sharing


def front_kernel(sizes, count, paired, *refs):
    parts, refs = refs[:count], refs[count:]
    if paired:
        pair_ref, down_ref, cot_ref, kv_ref, zero_ref, *refs = refs
    else:
        pair_ref = down_ref = None
    wholes, refs = refs[:count], refs[count:]
    if paired:
        pair_all, down_all, cot_all, window, *refs = refs
    else:
        pair_all = down_all = None
    send_sems, recv_sems, own_sems, halo_send, halo_recv = refs
    greet(front_masks(*sizes, paired))
    ctx, fsdp = lax.axis_index("ctx"), lax.axis_index("fsdp")
    reach = halo_send.shape[0]
    halos = []
    if paired:
        for step in range(1, reach + 1):
            copy = pltpu.make_async_remote_copy(
                src_ref=kv_ref,
                dst_ref=window.at[reach - step],
                send_sem=halo_send.at[step - 1],
                recv_sem=halo_recv.at[step - 1],
                device_id=(lax.rem(ctx + step, sizes[0]), fsdp),
                device_id_type=pl.DeviceIdType.MESH,
            )
            halos.append((step, copy))
            pl.when(ctx + step < sizes[0])(copy.start)
    kept = []
    for n, (own, whole) in enumerate(zip(parts, wholes)):
        kept.append(
            pltpu.make_async_copy(own, whole.at[ctx // 2, ctx % 2, fsdp], own_sems.at[n])
        )
    empty = []
    if paired:
        ff_own = pair_ref.shape[2] // sizes[0]
        columns = pl.ds(pl.multiple_of(ctx * ff_own, ff_own), ff_own)
        for n, (source, target) in enumerate(
            (
                (pair_ref.at[:, :, columns], pair_all.at[:, ctx, fsdp]),
                (down_ref, down_all.at[fsdp]),
                (cot_ref, cot_all.at[ctx // 2, ctx % 2]),
                (kv_ref, window.at[reach]),
            )
        ):
            kept.append(pltpu.make_async_copy(source, target, own_sems.at[count + n]))
        for step in range(1, reach + 1):
            copy = pltpu.make_async_copy(
                zero_ref, window.at[reach - step], own_sems.at[count + 3 + step]
            )
            empty.append((step, copy))
    for copy in kept:
        copy.start()
    for step, copy in empty:
        pl.when(ctx - step < 0)(copy.start)
    line = line_gather("cot", cot_ref, cot_all, sizes) if paired else []
    copies = front_copies(parts, wholes, pair_ref, pair_all, down_ref, down_all, line, sizes)
    run_copies(copies, send_sems, recv_sems)
    for copy in kept:
        copy.wait()
    for step, copy in empty:
        pl.when(ctx - step < 0)(copy.wait)
    for step, copy in halos:
        pl.when(ctx - step >= 0)(copy.wait_recv)
    for step, copy in halos:
        pl.when(ctx + step < sizes[0])(copy.wait_send)


def gather_front(parts, pair, down, cot, key_value, sizes, collective_id):
    ctx_size, fsdp_size = sizes
    chips = ctx_size // 2
    rows = parts[0].shape[0]
    paired = pair is not None
    reach = WINDOW // STRETCH
    count = len(parts) * (chips - 1 + chips * (2 * (fsdp_size - 1) + 1) + fsdp_size - 1)
    shapes = [
        jax.ShapeDtypeStruct((chips, 2, fsdp_size, rows, part.shape[1]), part.dtype)
        for part in parts
    ]
    arrays = list(parts)
    if paired:
        count += ctx_size - 1 + 2 * (fsdp_size - 1) + 2 * chips - 1
        columns = pair.shape[2] // ctx_size
        shapes += [
            jax.ShapeDtypeStruct((2, ctx_size, fsdp_size, rows, columns), pair.dtype),
            jax.ShapeDtypeStruct((fsdp_size,) + down.shape, down.dtype),
            jax.ShapeDtypeStruct((chips, 2) + cot.shape, cot.dtype),
            jax.ShapeDtypeStruct((reach + 1,) + key_value.shape, key_value.dtype),
        ]
        arrays += [pair, down, cot, key_value, jnp.zeros_like(key_value)]
    hbm = pl.BlockSpec(memory_space=pl.ANY)
    vmem = pl.BlockSpec(memory_space=pltpu.VMEM)
    return pl.pallas_call(
        functools.partial(front_kernel, sizes, len(parts), paired),
        in_specs=[vmem] * len(arrays),
        out_specs=[hbm] * len(shapes),
        out_shape=shapes,
        scratch_shapes=[
            pltpu.SemaphoreType.DMA((count,)),
            pltpu.SemaphoreType.DMA((count,)),
            pltpu.SemaphoreType.DMA((len(shapes) + reach,)),
            pltpu.SemaphoreType.DMA((reach,)),
            pltpu.SemaphoreType.DMA((reach,)),
        ],
        compiler_params=pltpu.CompilerParams(collective_id=collective_id, has_side_effects=True),
        cost_estimate=pl.CostEstimate(
            flops=90_000_000_000, bytes_accessed=1_000_000, transcendentals=0
        ),
    )(*arrays)


def hidden_kernel(sizes, pieces, pair_in, normed_ref, pair_all, normed_all, send_sems, recv_sems, own_sem):
    ctx_size, fsdp_size = sizes
    ctx, fsdp = lax.axis_index("ctx"), lax.axis_index("fsdp")
    masks = [1 << bit for bit in range(fsdp_size.bit_length() - 1)]
    far = [1 << bit for bit in range((ctx_size // 2).bit_length() - 1)]
    greet([(0, 0, m) for m in masks] + [(m, 0, 0) for m in far] + [(0, 1, 0)])
    mine = pltpu.make_async_copy(normed_ref, normed_all.at[ctx // 2, ctx % 2], own_sem)
    mine.start()
    lists = []
    for h, order in enumerate([masks, masks[::-1]]):
        view = lambda r, h=h: pair_all.at[h, :, fsdp ^ r]
        lists.append(doubling(("pair", h), fsdp_size, order, (), view, view)[0])
    rows = normed_ref.shape[0] // pieces
    lines = []
    for n in range(pieces):
        strip = pl.ds(n * rows, rows)
        lines.append(
            line_gather(("normed", n), normed_ref.at[strip], normed_all.at[:, :, strip], sizes)
        )
    copies = [copy for line in lines for copy in line[0]]
    pair_hops = [
        [copy for pieces in zip(*(hops[n] for hops in lists)) for copy in pieces]
        for n in range(len(masks))
    ]
    copies += pair_hops[0]
    depth = len(lines[0])
    for turn in range(pieces + depth - 2):
        for stage in range(1, depth):
            if 0 <= turn - stage + 1 < pieces:
                copies.extend(lines[turn - stage + 1][stage])
        if turn == pieces // 2:
            for hop in pair_hops[1:]:
                copies.extend(hop)
    run_copies(copies, send_sems, recv_sems)
    mine.wait()


def gather_hidden(pair_all, normed, sizes):
    ctx_size, fsdp_size = sizes
    chips = ctx_size // 2
    pieces = 4
    count = 2 * (fsdp_size - 1) + pieces * (2 * chips - 1)
    hbm = pl.BlockSpec(memory_space=pl.ANY)
    return pl.pallas_call(
        functools.partial(hidden_kernel, sizes, pieces),
        in_specs=[hbm, pl.BlockSpec(memory_space=pltpu.VMEM)],
        out_specs=[hbm, hbm],
        out_shape=[
            jax.ShapeDtypeStruct(pair_all.shape, pair_all.dtype),
            jax.ShapeDtypeStruct((chips, 2) + normed.shape, normed.dtype),
        ],
        input_output_aliases={0: 0},
        scratch_shapes=[
            pltpu.SemaphoreType.DMA((count,)),
            pltpu.SemaphoreType.DMA((count,)),
            pltpu.SemaphoreType.DMA,
        ],
        compiler_params=pltpu.CompilerParams(collective_id=2, has_side_effects=True),
        cost_estimate=pl.CostEstimate(flops=90_000_000_000, bytes_accessed=30_000_000, transcendentals=0),
    )(pair_all, normed)


def hop_slots(size, order):
    slots, held = [], list(range(size))
    for mask in order:
        held = [r for r in held if not r & mask]
        slots.append(held)
    return slots


def remote(source, target, send_sem, recv_sem, peer):
    return pltpu.make_async_remote_copy(
        src_ref=source,
        dst_ref=target,
        send_sem=send_sem,
        recv_sem=recv_sem,
        device_id=peer_of(*peer),
        device_id_type=pl.DeviceIdType.MESH,
    )


def reduce_kernel(
    sizes, chunk, products, extras, carried, lefts, right, extra, *refs
):
    total, refs = refs[carried], refs[1 + 2 * carried :]
    terms, core_got, line_sent, line_got = refs[:4]
    core_send, core_recv, hop_send, hop_recv, line_send, line_recv = refs[4:10]
    hop_buffers = refs[10:]
    ctx_size, fsdp_size = sizes
    chips = ctx_size // 2
    rows = total.shape[0]
    count = products + extras
    half = chunk // 2
    masks = [1 << bit for bit in range(fsdp_size.bit_length() - 1)]
    orders = [masks, masks[::-1]]
    bits = len(masks)
    hops = [
        [hop_buffers[(h * bits + j) * 2 : (h * bits + j) * 2 + 2] for j in range(bits)]
        for h in range(2)
    ]
    slots = [hop_slots(fsdp_size, order) for order in orders]
    ctx, fsdp = lax.axis_index("ctx"), lax.axis_index("fsdp")
    chip, side = ctx // 2, ctx % 2
    greet(
        [(0, 1, 0)]
        + [(0, 0, m) for m in masks]
        + [(1 << bit, 0, 0) for bit in range(chips.bit_length() - 1)]
    )

    def core_copy(i):
        return remote(
            terms.at[i, :, 1 - side], core_got.at[i], core_send.at[i], core_recv.at[i], (0, 1, 0)
        )

    def hop_copy(h, j, i):
        sent, got = hops[h][j]
        return remote(
            sent.at[i], got.at[i], hop_send.at[h, j, i], hop_recv.at[h, j, i], (0, 0, orders[h][j])
        )

    near_first = [1 << bit for bit in range(chips.bit_length() - 1)]
    line_slots = hop_slots(chips, near_first)
    line_first = [sum(chips >> (k + 1) for k in range(j)) for j in range(len(near_first))]

    def line_copy(j, i):
        blocks = pl.ds(line_first[j], chips >> (j + 1))
        return remote(
            line_sent.at[i, blocks], line_got.at[i, blocks],
            line_send.at[i, j], line_recv.at[i, j], (near_first[j], 0, 0),
        )

    def line_held(h, upto, i, r):
        cols = slice(h * half, (h + 1) * half)
        value = held(h, bits, i, chip ^ r, 0)
        for j in range(upto):
            value += line_got[i, line_first[j] + line_slots[j].index(r), :, cols].astype(
                jnp.float32
            )
        return value

    def held(h, upto, i, z, r):
        cols = pl.ds(h * half, half)
        value = terms[i, z, side, fsdp ^ r, :, cols].astype(jnp.float32)
        value += core_got[i, z, fsdp ^ r, :, cols].astype(jnp.float32)
        for j in range(upto):
            value += hops[h][j][1][i, slots[h][j].index(r), z].astype(jnp.float32)
        return value

    slack = 3
    last = bits + 1 + slack * len(near_first)

    def step(t, carry):
        @pl.when(t < products)
        def _():
            per_left = products // lefts.shape[0]
            cols = pl.ds(pl.multiple_of(t * chunk, chunk), chunk)
            term = jnp.dot(
                lefts[t // per_left], right[:, cols], preferred_element_type=jnp.float32
            )
            terms[t] = term.astype(jnp.bfloat16).reshape(terms.shape[1:])

        if extras:
            @pl.when((t >= products) & (t < count))
            def _():
                terms[t] = extra[t - products].reshape(terms.shape[1:])

        @pl.when(t < count)
        def _():
            core_copy(t).start()

        for j in range(bits):
            @pl.when((t >= j + 1) & (t < count + j + 1))
            def _(j=j):
                i = t - (j + 1)
                if j == 0:
                    core_copy(i).wait_recv()
                for h in range(2):
                    if j:
                        hop_copy(h, j - 1, i).wait_recv()
                    for s, r in enumerate(slots[h][j]):
                        for z in range(chips):
                            hops[h][j][0][i, s, z] = held(h, j, i, z, r | orders[h][j]).astype(
                                jnp.bfloat16
                            )
                    hop_copy(h, j, i).start()

        for j in range(len(near_first)):
            lag = bits + 1 + slack * j

            @pl.when((t >= lag) & (t < count + lag))
            def _(j=j, lag=lag):
                i = t - lag
                if j:
                    line_copy(j - 1, i).wait_recv()
                for h in range(2):
                    if j == 0:
                        hop_copy(h, bits - 1, i).wait_recv()
                    for s, r in enumerate(line_slots[j]):
                        line_sent[i, line_first[j] + s, :, h * half : (h + 1) * half] = line_held(
                            h, j, i, r | near_first[j]
                        ).astype(jnp.bfloat16)
                line_copy(j, i).start()

        @pl.when(t >= last)
        def _():
            i = t - last
            line_copy(len(near_first) - 1, i).wait_recv()
            for h in range(2):
                value = line_held(h, len(near_first), i, 0)
                total[:, pl.ds(pl.multiple_of(i * chunk + h * half, half), half)] = value

        return carry

    lax.fori_loop(0, count + last, step, 0)

    def finish(i, carry):
        core_copy(i).wait_send()
        for h in range(2):
            for j in range(bits):
                hop_copy(h, j, i).wait_send()
        for j in range(len(near_first)):
            line_copy(j, i).wait_send()
        return carry

    lax.fori_loop(0, count, finish, 0)


def reduce_rows(lefts, right, extra, carried, chunk, sizes, collective_id):
    ctx_size, fsdp_size = sizes
    chips = ctx_size // 2
    depth = lefts.shape[1]
    rows = depth // (ctx_size * fsdp_size)
    products = right.shape[1] // chunk
    extras = 0 if extra is None else extra.shape[0]
    if extra is None:
        extra = jnp.zeros((1, 16, LANES), jnp.bfloat16)
    count = products + extras
    bits = fsdp_size.bit_length() - 1
    half = chunk // 2
    buffers = []
    for _ in range(2):
        for j in range(bits):
            shape = (count, fsdp_size >> (j + 1), chips, rows, half)
            buffers += [pltpu.VMEM(shape, jnp.bfloat16)] * 2
    line = pltpu.VMEM((count, max(chips - 1, 1), rows, chunk), jnp.bfloat16)
    vmem = pl.BlockSpec(memory_space=pltpu.VMEM)
    hbm = pl.BlockSpec(memory_space=pl.ANY)
    return pl.pallas_call(
        functools.partial(reduce_kernel, sizes, chunk, products, extras, len(carried)),
        in_specs=[vmem] * 3 + [hbm] * len(carried),
        out_specs=[vmem] + [hbm] * len(carried),
        out_shape=[jax.ShapeDtypeStruct((rows, count * chunk), jnp.float32)]
        + [jax.ShapeDtypeStruct(array.shape, array.dtype) for array in carried],
        input_output_aliases={3 + n: 1 + n for n in range(len(carried))},
        scratch_shapes=[
            pltpu.VMEM((count, chips, 2, fsdp_size, rows, chunk), jnp.bfloat16),
            pltpu.VMEM((count, chips, fsdp_size, rows, chunk), jnp.bfloat16),
            line,
            line,
            pltpu.SemaphoreType.DMA((count,)),
            pltpu.SemaphoreType.DMA((count,)),
            pltpu.SemaphoreType.DMA((2, bits, count)),
            pltpu.SemaphoreType.DMA((2, bits, count)),
            pltpu.SemaphoreType.DMA((count, chips.bit_length() - 1)),
            pltpu.SemaphoreType.DMA((count, chips.bit_length() - 1)),
        ]
        + buffers,
        compiler_params=pltpu.CompilerParams(
            collective_id=collective_id, has_side_effects=True, vmem_limit_bytes=56 * 1024 * 1024
        ),
        cost_estimate=pl.CostEstimate(flops=80_000_000_000, bytes_accessed=30_000_000, transcendentals=0),
    )(lefts, right, extra, *carried)


def hidden_grad_kernel(
    sizes, normed, gate, up, carried_in, pair_sum, carried,
    terms, pair_sent, pair_got, pair_send, pair_recv
):
    ctx_size, fsdp_size = sizes
    count, span = terms.shape[1], normed.shape[1] // terms.shape[1]
    masks = [1 << bit for bit in range(fsdp_size.bit_length() - 1)]
    orders = [masks, masks[::-1]]
    bits = len(masks)
    slots = [hop_slots(fsdp_size, order) for order in orders]
    fsdp = lax.axis_index("fsdp")
    greet([(0, 0, m) for m in masks])
    first = [sum(fsdp_size >> (k + 1) for k in range(j)) for j in range(bits)]

    def pair_copy(h, j, i):
        rows = pl.ds(first[j], fsdp_size >> (j + 1))
        return remote(
            pair_sent.at[h, i, rows], pair_got.at[h, i, rows],
            pair_send.at[h, j, i], pair_recv.at[h, j, i], (0, 0, orders[h][j]),
        )

    def pair_held(h, upto, i, r):
        value = terms[h, i, fsdp ^ r].astype(jnp.float32)
        for j in range(upto):
            value += pair_got[h, i, first[j] + slots[h][j].index(r)].astype(jnp.float32)
        return value

    def step(t, carry):
        @pl.when(t < count)
        def _():
            rows = pl.ds(pl.multiple_of(t * span, span), span)
            for h, grad in enumerate((gate, up)):
                term = across(normed[:, rows], grad[...])
                terms[h, t] = term.astype(jnp.bfloat16).reshape(terms.shape[2:])

        for j in range(bits):
            @pl.when((t >= j) & (t < count + j))
            def _(j=j):
                i = t - j
                for h in range(2):
                    if j:
                        pair_copy(h, j - 1, i).wait_recv()
                    for s, r in enumerate(slots[h][j]):
                        pair_sent[h, i, first[j] + s] = pair_held(
                            h, j, i, r | orders[h][j]
                        ).astype(jnp.bfloat16)
                    pair_copy(h, j, i).start()

        @pl.when(t >= bits)
        def _():
            i = t - bits
            for h in range(2):
                pair_copy(h, bits - 1, i).wait_recv()
                pair_sum[i, h] = pair_held(h, bits, i, 0).astype(jnp.bfloat16)

        return carry

    lax.fori_loop(0, count + bits, step, 0)

    def finish(i, carry):
        for h in range(2):
            for j in range(bits):
                pair_copy(h, j, i).wait_send()
        return carry

    lax.fori_loop(0, count, finish, 0)


def reduce_hidden(normed, gate, up, carried, sizes):
    ctx_size, fsdp_size = sizes
    bits = fsdp_size.bit_length() - 1
    rows, columns = normed.shape[1] // (ctx_size * fsdp_size), gate.shape[1]
    pair = pltpu.VMEM((2, ctx_size, fsdp_size - 1, rows, columns), jnp.bfloat16)
    vmem = pl.BlockSpec(memory_space=pltpu.VMEM)
    hbm = pl.BlockSpec(memory_space=pl.ANY)
    return pl.pallas_call(
        functools.partial(hidden_grad_kernel, sizes),
        in_specs=[vmem] * 3 + [hbm],
        out_specs=[vmem, hbm],
        out_shape=[
            jax.ShapeDtypeStruct((ctx_size, 2, rows, columns), jnp.bfloat16),
            jax.ShapeDtypeStruct(carried.shape, carried.dtype),
        ],
        input_output_aliases={3: 1},
        scratch_shapes=[
            pltpu.VMEM((2, ctx_size, fsdp_size, rows, columns), jnp.bfloat16), pair, pair,
        ]
        + [pltpu.SemaphoreType.DMA((2, bits, ctx_size))] * 2,
        compiler_params=pltpu.CompilerParams(
            collective_id=3, has_side_effects=True, vmem_limit_bytes=60 * 1024 * 1024
        ),
        cost_estimate=pl.CostEstimate(flops=60_000_000_000, bytes_accessed=30_000_000, transcendentals=0),
    )(normed, gate, up, carried)


def out_norm_kernel(mix, weight, stream, gain, resid, normed, total):
    i, steps = pl.program_id(0), pl.num_programs(0)
    span = weight.shape[1]
    cols = pl.ds(pl.multiple_of(i * span, span), span)
    total[:, cols] = stream[:, cols].astype(jnp.float32) + product(mix[...], weight[...])

    @pl.when(i == steps - 1)
    def _():
        h = total[...]
        resid[...] = h
        inverse = lax.rsqrt(jnp.mean(h * h, axis=1, keepdims=True) + EPS)
        normed[...] = (h * inverse * gain[...]).astype(jnp.bfloat16)


def out_norm(mix, weight, stream, gain):
    rows, width = mix.shape
    steps = 4
    whole = pl.BlockSpec((rows, width), lambda i: (0, 0))
    return pl.pallas_call(
        out_norm_kernel,
        grid=(steps,),
        in_specs=[
            whole,
            pl.BlockSpec((width, width // steps), lambda i: (0, i)),
            whole,
            pl.BlockSpec((1, width), lambda i: (0, 0)),
        ],
        out_specs=[whole, whole],
        out_shape=[
            jax.ShapeDtypeStruct((rows, width), jnp.float32),
            jax.ShapeDtypeStruct((rows, width), jnp.bfloat16),
        ],
        scratch_shapes=[pltpu.VMEM((rows, width), jnp.float32)],
        compiler_params=pltpu.CompilerParams(vmem_limit_bytes=40 * 1024 * 1024),
        cost_estimate=pl.CostEstimate(
            flops=2 * rows * width * width, bytes_accessed=14_000_000, transcendentals=0
        ),
    )(mix, weight, stream, gain)


def norm_back_kernel(columns, resid, gain, cot, weight, grad_ref, low_ref, mix_ref, gain_ref):
    @pl.when(pl.program_id(0) == 0)
    def _():
        h = resid[...]
        inverse = lax.rsqrt(jnp.mean(h * h, axis=1, keepdims=True) + EPS)
        normal = h * inverse
        slope = columns[...].astype(jnp.float32)
        gain_ref[...] = jnp.sum(slope * normal, axis=0, keepdims=True)
        grad = cot[...].astype(jnp.float32) + norm_back(slope * gain[...], normal, inverse)
        grad_ref[...] = grad
        low_ref[...] = grad.astype(jnp.bfloat16)

    mix_ref[...] = against(low_ref[...], weight[...]).astype(jnp.bfloat16)


def norm_back_mix(columns, resid, gain, cot, weight):
    rows, width = resid.shape
    steps = 4
    whole = pl.BlockSpec((rows, width), lambda i: (0, 0))
    line = pl.BlockSpec((1, width), lambda i: (0, 0))
    return pl.pallas_call(
        norm_back_kernel,
        grid=(steps,),
        in_specs=[
            whole, whole, line, whole,
            pl.BlockSpec((width // steps, width), lambda i: (i, 0)),
        ],
        out_specs=[whole, whole, pl.BlockSpec((rows, width // steps), lambda i: (0, i)), line],
        out_shape=[
            jax.ShapeDtypeStruct((rows, width), jnp.float32),
            jax.ShapeDtypeStruct((rows, width), jnp.bfloat16),
            jax.ShapeDtypeStruct((rows, width), jnp.bfloat16),
            jax.ShapeDtypeStruct((1, width), jnp.float32),
        ],
        compiler_params=pltpu.CompilerParams(vmem_limit_bytes=40 * 1024 * 1024),
        cost_estimate=pl.CostEstimate(
            flops=2 * rows * width * width, bytes_accessed=16_000_000, transcendentals=0
        ),
    )(columns, resid, gain, cot, weight)


def hidden_layer_kernel(
    normed, cot, gate_weight, up_weight, down_weight,
    hidden_ref, dgate_ref, dup_ref, down_ref, columns_ref
):
    x = normed[...]
    gate = product(x, gate_weight[...])
    up = product(x, up_weight[...])
    grad = against(cot[...], down_weight[...])
    sigmoid = jax.nn.sigmoid(gate)
    silu = gate * sigmoid
    hidden = (silu * up).astype(jnp.bfloat16)
    dgate = (grad * up * sigmoid * (1.0 + gate * (1.0 - sigmoid))).astype(jnp.bfloat16)
    dup = (grad * silu).astype(jnp.bfloat16)
    hidden_ref[...] = hidden
    dgate_ref[...] = dgate
    dup_ref[...] = dup
    columns = against(dgate, gate_weight[...]) + against(dup, up_weight[...])
    columns_ref[...] = columns.astype(jnp.bfloat16)
    down_ref[...] = product(hidden, down_weight[...]).astype(jnp.bfloat16)


def hidden_layer(normed, cot, pair, down_weight):
    tokens, width = normed.shape
    share = pair.shape[2]
    tile = min(256, tokens)
    wide = pl.BlockSpec((tile, width), lambda i: (i, 0))
    thin = pl.BlockSpec((tile, share), lambda i: (i, 0))
    once = pl.Buffered(buffer_count=1)
    weights = [
        pl.BlockSpec((None,) + pair.shape[1:], lambda i, n=n: (n, 0, 0), pipeline_mode=once)
        for n in range(2)
    ]
    down = pl.BlockSpec(down_weight.shape, lambda i: (0, 0), pipeline_mode=once)
    thin_out = jax.ShapeDtypeStruct((tokens, share), jnp.bfloat16)
    wide_out = jax.ShapeDtypeStruct((tokens, width), jnp.bfloat16)
    return pl.pallas_call(
        hidden_layer_kernel,
        grid=(tokens // tile,),
        in_specs=[wide, wide] + weights + [down],
        out_specs=[thin, thin, thin, wide, wide],
        out_shape=[thin_out] * 3 + [wide_out] * 2,
        compiler_params=pltpu.CompilerParams(vmem_limit_bytes=56 * 1024 * 1024),
        cost_estimate=pl.CostEstimate(
            flops=16 * tokens * width * share, bytes_accessed=30_000_000, transcendentals=0
        ),
    )(normed, cot, pair, pair, down_weight)


def local(
    tokens,
    cotangent,
    lengths,
    attn_gain,
    query_weight,
    key_weight,
    value_weight,
    out_weight,
    mlp_gain,
    gate_weight,
    up_weight,
    down_weight,
):
    both = ("ctx", "fsdp")
    ctx_size = lax.axis_size("ctx")
    fsdp_size = lax.axis_size("fsdp")
    chips = ctx_size // 2
    stream = tokens[0].astype(jnp.float32)
    tok_rows = stream.shape[0]
    own_rows = query_weight.shape[0]
    kv_width = KV_HEADS * HEAD_DIM
    ff_own = FF // ctx_size
    reach_blocks = WINDOW // STRETCH
    ctx_place = lax.axis_index("ctx")
    doc_lengths = lengths[0]
    query_index = ctx_place * tok_rows + jnp.arange(tok_rows, dtype=jnp.int32)
    key_index = (ctx_place - reach_blocks) * tok_rows + jnp.arange(
        (reach_blocks + 1) * tok_rows, dtype=jnp.int32
    )
    query_doc = doc_segment(doc_lengths, query_index)
    key_doc = doc_segment(doc_lengths, key_index)
    position = doc_position(doc_lengths, query_index, query_doc)
    visible = (key_index[:, None] >= 0) & (key_index[:, None] <= query_index[None, :])
    visible = (
        visible
        & (query_index[None, :] - key_index[:, None] < WINDOW)
        & (query_doc[None, :] == key_doc[:, None])
    )
    bias = jnp.where(visible, 0.0, -1e30).astype(jnp.float32)
    cosine, sine = turn_tables(position)

    sizes = (ctx_size, fsdp_size)
    gains = jnp.zeros((own_rows, LANES), jnp.bfloat16)
    gains = gains.at[:, 0].set(attn_gain).at[:, 1].set(mlp_gain)
    (kv_all,) = gather_front(
        (jnp.concatenate([key_weight, value_weight, gains], axis=1),), None, None, None, None, sizes, 1
    )
    kv_all = kv_all.reshape(D, -1)
    gain_one = kv_all[:, 2 * kv_width].astype(jnp.float32)
    gain_two = kv_all[:, 2 * kv_width + 1].astype(jnp.float32)

    inv_one = lax.rsqrt(jnp.mean(stream * stream, axis=1, keepdims=True) + EPS)
    normal_one = stream * inv_one
    normed_one = (normal_one * gain_one).astype(jnp.bfloat16)
    kv_front = product(normed_one, kv_all)
    key_low = rope(kv_front[:, :kv_width], cosine, sine).astype(jnp.bfloat16)
    value_low = kv_front[:, kv_width : 2 * kv_width].astype(jnp.bfloat16)
    own_pair = jnp.concatenate([key_low, value_low], axis=1)
    query_all, out_all, pair_all, down_own, cot_all, window = gather_front(
        (query_weight, out_weight), jnp.stack([gate_weight, up_weight]), down_weight,
        cotangent[0], own_pair, sizes, 6,
    )
    cot_all = cot_all.reshape(ctx_size * tok_rows, D)
    query_all = query_all.reshape(D, D)
    out_all = out_all.reshape(D, D)
    down_own = down_own.reshape(ff_own, D)
    window = window.reshape(-1, 2 * kv_width)
    key_window, value_window = window[:, :kv_width], window[:, kv_width:]
    query_front = product(normed_one, query_all)
    attn_mix, query_low, log_total = attend_forward(
        query_front, key_window, value_window, bias, cosine, sine
    )
    resid, normed_two = out_norm(attn_mix, out_all, tokens[0], gain_two[None])
    pair, normed_all = gather_hidden(pair_all, normed_two, sizes)
    pair = pair.reshape(2, D, ff_own)
    normed_all = normed_all.reshape(ctx_size * tok_rows, D)
    hidden, grad_gate_low, grad_up_low, down_part, columns = hidden_layer(
        normed_all, cot_all, pair, down_own
    )
    columns = lax.psum_scatter(columns, "ctx", scatter_dimension=0, tiled=True)
    pair_sum, down_part = reduce_hidden(normed_all, grad_gate_low, grad_up_low, down_part, sizes)
    down_terms = across(hidden, cot_all).astype(jnp.bfloat16)
    down_sum = lax.psum_scatter(down_part, "ctx", scatter_dimension=0, tiled=True)
    grad_resid, grad_resid_low, grad_mix_low, mlp_gain_local = norm_back_mix(
        columns, resid, gain_two[None], cotangent[0], out_all
    )
    grad_query_low, grad_key_window, grad_value_window = attend_backward(
        query_low, key_window, value_window, grad_mix_low, attn_mix, log_total, bias, cosine, sine,
        pair_sum,
    )
    wide_grad, pair_sum, down_terms = reduce_rows(
        jnp.stack([normed_one.T, attn_mix.T]),
        jnp.concatenate([grad_query_low, grad_resid_low], axis=1),
        None, (pair_sum, down_terms), 512, sizes, 4,
    )
    grad_down = lax.psum_scatter(down_terms, "fsdp", scatter_dimension=0, tiled=True)
    pair_sum = lax.all_to_all(pair_sum, "ctx", split_axis=0, concat_axis=0, tiled=True)
    own_start = reach_blocks * tok_rows
    grad_pair = jnp.concatenate([grad_key_window, grad_value_window], axis=1)
    grad_pair_total = after(grad_pair[own_start:], wide_grad)
    grad_pair_low = grad_pair[:own_start].astype(jnp.bfloat16)
    for step in range(1, reach_blocks + 1):
        first_row = (reach_blocks - step) * tok_rows
        later = passed_along(grad_pair_low[first_row : first_row + tok_rows], "ctx", -step)
        grad_pair_total = grad_pair_total + later.astype(jnp.float32)
    grad_key_low = rope(grad_pair_total[:, :kv_width], cosine, -sine).astype(jnp.bfloat16)
    grad_value_low = grad_pair_total[:, kv_width:].astype(jnp.bfloat16)
    kv_low = jnp.concatenate([grad_key_low, grad_value_low], axis=1)
    grad_normed_one = against(grad_query_low, query_all) + against(
        jnp.pad(kv_low, ((0, 0), (0, LANES))), kv_all
    )
    attn_gain_local = jnp.sum(grad_normed_one * normal_one, axis=0)
    gain_terms = jnp.stack([attn_gain_local, mlp_gain_local[0]], axis=1).astype(jnp.bfloat16)
    gain_terms = jnp.pad(gain_terms, ((0, 0), (0, 2 * LANES - 2)))[None]
    (kv_grad,) = reduce_rows(
        normed_one.T[None], kv_low, gain_terms, (), 2 * LANES, sizes, 5
    )
    pair_sum = after(pair_sum, kv_grad)
    mixed = after(resid, kv_grad) + after(down_sum, kv_grad).astype(jnp.float32)
    mixed = mixed.astype(jnp.bfloat16)
    pair_sum = pair_sum.transpose(1, 2, 0, 3).reshape(2, own_rows, FF).astype(jnp.float32)
    grad_input = grad_resid + norm_back(grad_normed_one * gain_one, normal_one, inv_one)
    return (
        mixed[None],
        grad_input.astype(jnp.bfloat16)[None],
        kv_grad[:, 2 * kv_width],
        wide_grad[:, :D],
        kv_grad[:, :kv_width],
        kv_grad[:, kv_width : 2 * kv_width],
        wide_grad[:, D:],
        kv_grad[:, 2 * kv_width + 1],
        pair_sum[0],
        pair_sum[1],
        grad_down.astype(jnp.float32),
    )


def solution(mesh):
    in_specs = (
        P("fsdp", "ctx", None),
        P("fsdp", "ctx", None),
        P("fsdp", None),
        P(("ctx", "fsdp")),
        P(("ctx", "fsdp"), None),
        P(("ctx", "fsdp"), None),
        P(("ctx", "fsdp"), None),
        P(("ctx", "fsdp"), None),
        P(("ctx", "fsdp")),
        P(("ctx", "fsdp"), None),
        P(("ctx", "fsdp"), None),
        P(("ctx", "fsdp"), None),
    )
    out_specs = (
        P("fsdp", "ctx", None),
        P("fsdp", "ctx", None),
        P(("ctx", "fsdp")),
        P(("ctx", "fsdp"), None),
        P(("ctx", "fsdp"), None),
        P(("ctx", "fsdp"), None),
        P(("ctx", "fsdp"), None),
        P(("ctx", "fsdp")),
        P(("ctx", "fsdp"), None),
        P(("ctx", "fsdp"), None),
        P(("ctx", "fsdp"), None),
    )
    return jax.shard_map(local, mesh=mesh, in_specs=in_specs, out_specs=out_specs, check_vma=False)
```

```python
import functools

import jax
import jax.numpy as jnp
from jax import lax
from jax.experimental import pallas as pl
from jax.experimental.pallas import tpu as pltpu
from jax.sharding import PartitionSpec as P

D = 2048
FF = 8192
HEADS = 32
KV_HEADS = 8
HEAD_DIM = 64
WINDOW = 1024
STRETCH = 256
QTILE = 128
LANES = 128
EPS = 1e-05
THETA = 500000.0


def passed_along(x, axis, by):
    size = lax.axis_size(axis)
    pairs = [(i, i + by) for i in range(size) if 0 <= i + by < size]
    return lax.ppermute(x, axis, pairs)


def product(left, right):
    return jnp.dot(left, right, preferred_element_type=jnp.float32)


def against(left, right):
    return lax.dot_general(
        left, right, (((1,), (1,)), ((), ())), preferred_element_type=jnp.float32
    )


def across(left, right):
    return lax.dot_general(
        left, right, (((0,), (0,)), ((), ())), preferred_element_type=jnp.float32
    )


def doc_segment(doc_lengths, index):
    doc_ends = jnp.cumsum(doc_lengths)
    return jnp.sum((index[:, None] >= doc_ends[None, :]).astype(jnp.int32), axis=1)


def doc_position(doc_lengths, index, segment):
    doc_ends = jnp.cumsum(doc_lengths)
    doc_starts = doc_ends - doc_lengths
    member = segment[:, None] == jnp.arange(doc_lengths.shape[0], dtype=jnp.int32)[None, :]
    return index - jnp.sum(jnp.where(member, doc_starts[None, :], 0), axis=1)


def swap_halves(u):
    half = HEAD_DIM // 2
    width = u.shape[1]
    lane = lax.broadcasted_iota(jnp.int32, u.shape, 1)
    ahead = pltpu.roll(u, width - half, 1)
    behind = pltpu.roll(u, half, 1)
    return jnp.where(lane % HEAD_DIM < half, ahead, behind)


def turn(u, cosine, sine):
    copies = u.shape[1] // cosine.shape[1]
    cosine = jnp.concatenate([cosine] * copies, axis=1)
    sine = jnp.concatenate([sine] * copies, axis=1)
    return u * cosine + swap_halves(u) * sine


def nt(left, right):
    return lax.dot_general(left, right, (((1,), (1,)), ((), ())), preferred_element_type=jnp.float32)


def nn(left, right):
    return lax.dot_general(left, right, (((1,), (0,)), ((), ())), preferred_element_type=jnp.float32)


def attend_forward_kernel(
    n_ref, w_ref, k_ref, v_ref, bias_ref, cos_ref, sin_ref, o_ref, qr_ref, lse_ref
):
    rows = n_ref.shape[0]
    group = HEADS // KV_HEADS
    span = k_ref.shape[0] - rows + QTILE
    rotated = turn(product(n_ref[...], w_ref[...]), cos_ref[...], sin_ref[...])
    qr_ref[...] = rotated.astype(jnp.bfloat16)
    scaled = (qr_ref[...].astype(jnp.float32) * HEAD_DIM ** (-0.5)).astype(jnp.bfloat16)
    for tile in range(rows // QTILE):
        first = tile * QTILE
        bias = bias_ref[first : first + span, first : first + QTILE]
        for kv in range(LANES // HEAD_DIM):
            lo = kv * HEAD_DIM
            keys = k_ref[first : first + span, lo : lo + HEAD_DIM]
            values = v_ref[first : first + span, lo : lo + HEAD_DIM]
            values_t = values.T
            raises, totals = [], []
            for h in range(group):
                head = kv * group + h
                q_h = scaled[first : first + QTILE, head * HEAD_DIM : (head + 1) * HEAD_DIM]
                s = nt(keys, q_h) + bias
                top = jnp.max(s, axis=0, keepdims=True)
                raised = jnp.exp(s - top)
                total = jnp.sum(raised, axis=0, keepdims=True)
                lse_ref[head : head + 1, first : first + QTILE] = top + jnp.log(total)
                raises.append(raised.astype(jnp.bfloat16))
                totals.append(total)
            o_wide = nn(values_t, jnp.concatenate(raises, axis=1)) / jnp.concatenate(totals, axis=1)
            o_t = jnp.concatenate(
                [o_wide[:, h * QTILE : (h + 1) * QTILE] for h in range(group)], axis=0
            )
            o_ref[first : first + QTILE, kv * group * HEAD_DIM : (kv + 1) * group * HEAD_DIM] = (
                o_t.T.astype(jnp.bfloat16)
            )


def attend_forward(normed, weight, k, v, bias, cosine, sine):
    rows, width = normed.shape[0], weight.shape[1]
    steps = KV_HEADS * HEAD_DIM // LANES
    qw = width // steps
    heads = HEADS // steps
    window = k.shape[0]
    return pl.pallas_call(
        attend_forward_kernel,
        grid=(steps,),
        in_specs=[
            pl.BlockSpec(normed.shape, lambda i: (0, 0)),
            pl.BlockSpec((weight.shape[0], qw), lambda i: (0, i)),
            pl.BlockSpec((window, LANES), lambda i: (0, i)),
            pl.BlockSpec((window, LANES), lambda i: (0, i)),
            pl.BlockSpec((window, rows), lambda i: (0, 0)),
            pl.BlockSpec((rows, LANES), lambda i: (0, 0)),
            pl.BlockSpec((rows, LANES), lambda i: (0, 0)),
        ],
        out_specs=[
            pl.BlockSpec((rows, qw), lambda i: (0, i)),
            pl.BlockSpec((rows, qw), lambda i: (0, i)),
            pl.BlockSpec((heads, rows), lambda i: (i, 0)),
        ],
        out_shape=[
            jax.ShapeDtypeStruct((rows, width), jnp.bfloat16),
            jax.ShapeDtypeStruct((rows, width), jnp.bfloat16),
            jax.ShapeDtypeStruct((HEADS, rows), jnp.float32),
        ],
        compiler_params=pltpu.CompilerParams(vmem_limit_bytes=48 * 1024 * 1024),
        cost_estimate=pl.CostEstimate(flops=40_000_000_000, bytes_accessed=10_000_000, transcendentals=0),
    )(normed, weight, k, v, bias, cosine, sine)


def attend_backward_kernel(
    qr_ref, k_ref, v_ref, do_ref, o_ref, lse_ref, bias_ref, cos_ref, sin_ref,
    carried_in, dq_ref, dk_low, dv_low, dk_own, dv_own, carried, dk_ref, dv_ref
):
    rows = qr_ref.shape[0]
    group = HEADS // KV_HEADS
    span = k_ref.shape[0] - rows + QTILE
    scale = HEAD_DIM ** (-0.5)
    dk_ref[...] = jnp.zeros_like(dk_ref)
    dv_ref[...] = jnp.zeros_like(dv_ref)
    scaled = (qr_ref[...].astype(jnp.float32) * scale).astype(jnp.bfloat16)
    wide = LANES // HEAD_DIM * group * HEAD_DIM
    owner = lax.broadcasted_iota(jnp.int32, (8, wide), 1) // HEAD_DIM
    pick = (owner == lax.broadcasted_iota(jnp.int32, (8, wide), 0)).astype(jnp.float32)
    for tile in range(rows // QTILE):
        first = tile * QTILE
        bias = bias_ref[first : first + span, first : first + QTILE]
        both = do_ref[first : first + QTILE, :].astype(jnp.float32) * o_ref[
            first : first + QTILE, :
        ].astype(jnp.float32)
        delta = lax.dot_general(
            pick, both, (((1,), (1,)), ((), ())),
            precision=lax.Precision.HIGHEST, preferred_element_type=jnp.float32,
        )
        dk_pair, dv_pair, dqs = [], [], []
        for kv in range(LANES // HEAD_DIM):
            lo = kv * HEAD_DIM
            keys = k_ref[first : first + span, lo : lo + HEAD_DIM]
            values = v_ref[first : first + span, lo : lo + HEAD_DIM]
            keys_t = keys.T
            probs, slopes, qs, dos = [], [], [], []
            for h in range(group):
                head = kv * group + h
                cols = slice(head * HEAD_DIM, (head + 1) * HEAD_DIM)
                q_h = scaled[first : first + QTILE, cols]
                do_h = do_ref[first : first + QTILE, cols]
                s = nt(keys, q_h) + bias
                p = jnp.exp(s - lse_ref[head : head + 1, first : first + QTILE])
                dp = nt(values, do_h)
                ds = (p * (dp - delta[head : head + 1, :])).astype(jnp.bfloat16)
                probs.append(p.astype(jnp.bfloat16))
                slopes.append(ds)
                qs.append(q_h)
                dos.append(do_h)
            p_all = jnp.concatenate(probs, axis=1)
            ds_all = jnp.concatenate(slopes, axis=1)
            dv_pair.append(nn(p_all, jnp.concatenate(dos, axis=0)))
            dk_pair.append(nn(ds_all, jnp.concatenate(qs, axis=0)))
            dq_t = nn(keys_t, ds_all) * scale
            dqs.extend(dq_t[:, h * QTILE : (h + 1) * QTILE] for h in range(group))
        dk_ref[first : first + span, :] += jnp.concatenate(dk_pair, axis=1)
        dv_ref[first : first + span, :] += jnp.concatenate(dv_pair, axis=1)
        dq = jnp.concatenate(dqs, axis=0).T
        dq_ref[first : first + QTILE, :] = turn(
            dq, cos_ref[first : first + QTILE, :], -sin_ref[first : first + QTILE, :]
        ).astype(jnp.bfloat16)
    before = dk_low.shape[0]
    dk_low[...] = dk_ref[:before, :].astype(jnp.bfloat16)
    dv_low[...] = dv_ref[:before, :].astype(jnp.bfloat16)
    dk_own[...] = dk_ref[before:, :]
    dv_own[...] = dv_ref[before:, :]


def attend_backward(qr, k, v, do, o, lse, bias, cosine, sine, carried):
    rows, width = qr.shape
    steps = KV_HEADS * HEAD_DIM // LANES
    qw = width // steps
    heads = HEADS // steps
    window = k.shape[0]
    wide = pl.BlockSpec((rows, qw), lambda i: (0, i))
    tall = pl.BlockSpec((window, LANES), lambda i: (0, i))
    table = pl.BlockSpec((rows, LANES), lambda i: (0, 0))
    return pl.pallas_call(
        attend_backward_kernel,
        grid=(steps,),
        in_specs=[
            wide, tall, tall, wide, wide,
            pl.BlockSpec((heads, rows), lambda i: (i, 0)),
            pl.BlockSpec((window, rows), lambda i: (0, 0)),
            table, table,
            pl.BlockSpec(memory_space=pl.ANY),
        ],
        out_specs=[
            wide,
            pl.BlockSpec((window - rows, LANES), lambda i: (0, i)),
            pl.BlockSpec((window - rows, LANES), lambda i: (0, i)),
            pl.BlockSpec((rows, LANES), lambda i: (0, i)),
            pl.BlockSpec((rows, LANES), lambda i: (0, i)),
            pl.BlockSpec(memory_space=pl.ANY),
        ],
        out_shape=[
            jax.ShapeDtypeStruct((rows, width), jnp.bfloat16),
            jax.ShapeDtypeStruct((window - rows, k.shape[1]), jnp.bfloat16),
            jax.ShapeDtypeStruct((window - rows, k.shape[1]), jnp.bfloat16),
            jax.ShapeDtypeStruct((rows, k.shape[1]), jnp.float32),
            jax.ShapeDtypeStruct((rows, k.shape[1]), jnp.float32),
            jax.ShapeDtypeStruct(carried.shape, carried.dtype),
        ],
        input_output_aliases={9: 5},
        scratch_shapes=[pltpu.VMEM((window, LANES), jnp.float32)] * 2,
        compiler_params=pltpu.CompilerParams(vmem_limit_bytes=48 * 1024 * 1024),
        cost_estimate=pl.CostEstimate(flops=80_000_000_000, bytes_accessed=20_000_000, transcendentals=0),
    )(qr, k, v, do, o, lse, bias, cosine, sine, carried)


def turn_tables(position):
    half_dim = HEAD_DIM // 2
    frequency = THETA ** (-2.0 * jnp.arange(half_dim, dtype=jnp.float32) / HEAD_DIM)
    angles = position.astype(jnp.float32)[:, None] * frequency[None, :]
    cosine, sine = jnp.cos(angles), jnp.sin(angles)
    copies = LANES // HEAD_DIM
    return (
        jnp.concatenate([cosine, cosine] * copies, axis=1),
        jnp.concatenate([-sine, sine] * copies, axis=1),
    )


def rope(u, cosine, sine):
    half = HEAD_DIM // 2
    parts = u.reshape(u.shape[0], -1, 2, half)
    swapped_parts = parts[:, :, ::-1, :].reshape(u.shape)
    copies = u.shape[1] // LANES
    return u * jnp.tile(cosine, (1, copies)) + swapped_parts * jnp.tile(sine, (1, copies))


def norm_back(grad_normal, normal, inverse):
    return inverse * (grad_normal - normal * jnp.mean(grad_normal * normal, axis=1, keepdims=True))


def after(x, *others):
    return lax.optimization_barrier((x,) + others)[0]


def peer_of(chip_mask, side_mask, fsdp_mask):
    ctx = lax.axis_index("ctx")
    return (ctx ^ (2 * chip_mask + side_mask), lax.axis_index("fsdp") ^ fsdp_mask)


def greet(peers):
    barrier = pltpu.get_barrier_semaphore()
    for peer in peers:
        pl.semaphore_signal(
            barrier, inc=1, device_id=peer_of(*peer), device_id_type=pl.DeviceIdType.MESH
        )
    pl.semaphore_wait(barrier, len(peers))


def run_copies(copies, send_sems, recv_sems):
    started, arrived = {}, set()

    def arrive(name):
        if name not in arrived:
            arrived.add(name)
            started[name].wait_recv()

    for copy in copies:
        if callable(copy):
            copy()
            continue
        at = len(started)
        name, awaited, source, target, peer = copy
        for other in awaited:
            arrive(other)
        started[name] = pltpu.make_async_remote_copy(
            src_ref=source,
            dst_ref=target,
            send_sem=send_sems.at[at],
            recv_sem=recv_sems.at[at],
            device_id=peer_of(*peer),
            device_id_type=pl.DeviceIdType.MESH,
        )
        started[name].start()
    for name in started:
        arrive(name)
    for name in started:
        started[name].wait_send()


def doubling(name, size, order, awaited, block, target, along=2):
    hops, held = [], {0: awaited}
    for mask in order:
        hop, got = [], {}
        for r, needs in held.items():
            key = (name, r, mask)
            peer = tuple(mask if place == along else 0 for place in range(3))
            hop.append((key, needs, block(r), target(r), peer))
            got[r ^ mask] = (key,)
        held.update(got)
        hops.append(hop)
    return hops, held


def line_gather(name, own, whole, sizes):
    chips = sizes[0] // 2
    ctx = lax.axis_index("ctx")
    chip, side = ctx // 2, ctx % 2
    far_first = [1 << bit for bit in range(chips.bit_length() - 1)][::-1]
    target = lambda r: whole.at[chip ^ r, side]
    block = lambda r: target(r) if r else own
    hops, held = doubling((name, "z"), chips, far_first, (), block, target, 0)
    last = [
        ((name, "core", r), held[r], block(r), target(r), (0, 1, 0)) for r in range(chips)
    ]
    return hops + [last]


def front_masks(ctx_size, fsdp_size, paired):
    chips = ctx_size // 2
    peers = [
        (m, s, 0)
        for m in range(chips)
        for s in range(2)
        if (m or s) and (paired or m + s == 1 or (not s and not m & (m - 1)))
    ]
    return peers + [(0, 0, m) for m in range(1, fsdp_size)]


def front_copies(parts, wholes, pair_ref, pair_all, down_ref, down_all, sizes):
    ctx_size, fsdp_size = sizes
    chips = ctx_size // 2
    ctx, fsdp = lax.axis_index("ctx"), lax.axis_index("fsdp")
    chip, side = ctx // 2, ctx % 2
    masks = [1 << bit for bit in range(fsdp_size.bit_length() - 1)]
    orders = [masks, masks[::-1]]
    far_first = [1 << bit for bit in range(chips.bit_length() - 1)][::-1]
    copies, arrival = [], {}
    lines = []
    for n, (own, whole) in enumerate(zip(parts, wholes)):
        view = lambda r, own=own, whole=whole: (
            whole.at[chip ^ r, side, fsdp] if r else own
        )
        target = lambda r, whole=whole: whole.at[chip ^ r, side, fsdp]
        hops, held = doubling(("z", n), chips, far_first, (), view, target, 0)
        lines.append(hops)
        for r, keys in held.items():
            arrival[n, r] = keys
    for hop in zip(*lines):
        for pieces in hop:
            copies.extend(pieces)
    exchange = []
    if pair_ref is not None:
        ff_own = pair_ref.shape[2] // ctx_size
        for m in range(chips):
            for s in range(2):
                if m or s:
                    other = ctx ^ (2 * m + s)
                    columns = pl.ds(pl.multiple_of(other * ff_own, ff_own), ff_own)
                    exchange.append(
                        (
                            ("pair", m, s), (), pair_ref.at[:, :, columns],
                            pair_all.at[:, ctx, fsdp], (m, s, 0),
                        )
                    )
    queues = []
    if down_ref is not None:
        width = down_ref.shape[1] // 2
        lists = []
        for h, order in enumerate(orders):
            cols = pl.ds(h * width, width)
            target = lambda r, cols=cols: down_all.at[fsdp ^ r, :, cols]
            block = lambda r, cols=cols: (
                down_all.at[fsdp ^ r, :, cols] if r else down_ref.at[:, cols]
            )
            lists.append(doubling(("down", h), fsdp_size, order, (), block, target)[0])
        stages = [[copy for pieces in zip(*hop) for copy in pieces] for hop in zip(*lists)]
        queues.append(stages + [[]])
    for n, (own, whole) in enumerate(zip(parts, wholes)):
        width = own.shape[1]
        cut = (width // 2 + LANES - 1) // LANES * LANES
        halves = [(0, cut), (cut, width - cut)]
        for m in range(chips):
            first = arrival[n, m]
            lists, last = [], []
            for h, ((lo, span), order) in enumerate(zip(halves, orders)):
                cols = pl.ds(lo, span)

                def block(r, m=m, cols=cols, own=own, whole=whole):
                    if m == 0 and r == 0:
                        return own.at[:, cols]
                    return whole.at[chip ^ m, side, fsdp ^ r, :, cols]

                def target(r, m=m, cols=cols, whole=whole):
                    return whole.at[chip ^ m, side, fsdp ^ r, :, cols]

                hops, held = doubling(("f", n, m, h), fsdp_size, order, first, block, target)
                lists.append(hops)
                last.extend(key for keys in held.values() for key in keys)
            stages = [[copy for pieces in zip(*hop) for copy in pieces] for hop in zip(*lists)]
            row = whole.at[chip ^ m, side]
            if m:
                stages.append([(("core", n, m), tuple(last), row, row, (0, 1, 0))])
            else:
                stages.append(
                    [
                        (
                            ("core", n, m, r), tuple(last),
                            row.at[fsdp ^ r] if r else own, row.at[fsdp ^ r], (0, 1, 0),
                        )
                        for r in range(fsdp_size)
                    ]
                )
            queues.append(stages)
    sharing = []
    lag = 2
    for turn in range(len(queues) + lag * (len(orders[0]) + 1)):
        for stage in range(len(orders[0]) + 1):
            at = turn - lag * stage
            if 0 <= at < len(queues):
                sharing.extend(queues[at][stage])
        if turn == chips:
            sharing.extend(exchange)
    return copies, sharing


def front_kernel(sizes, count, paired, *refs):
    parts, refs = refs[:count], refs[count:]
    if paired:
        pair_ref, down_ref, kv_ref, zero_ref, cot_in, *refs = refs
    else:
        pair_ref = down_ref = None
    wholes, refs = refs[:count], refs[count:]
    if paired:
        pair_all, down_all, window, cot_out, *refs = refs
    else:
        pair_all = down_all = None
    send_sems, recv_sems, own_sems, halo_send, halo_recv = refs
    greet(front_masks(*sizes, paired))
    ctx, fsdp = lax.axis_index("ctx"), lax.axis_index("fsdp")
    reach = halo_send.shape[0]
    halos = []
    if paired:
        for step in range(1, reach + 1):
            copy = pltpu.make_async_remote_copy(
                src_ref=kv_ref,
                dst_ref=window.at[reach - step],
                send_sem=halo_send.at[step - 1],
                recv_sem=halo_recv.at[step - 1],
                device_id=(lax.rem(ctx + step, sizes[0]), fsdp),
                device_id_type=pl.DeviceIdType.MESH,
            )
            halos.append((step, copy))
    kept = []
    for n, (own, whole) in enumerate(zip(parts, wholes)):
        kept.append(
            pltpu.make_async_copy(own, whole.at[ctx // 2, ctx % 2, fsdp], own_sems.at[n])
        )
    empty = []
    if paired:
        ff_own = pair_ref.shape[2] // sizes[0]
        columns = pl.ds(pl.multiple_of(ctx * ff_own, ff_own), ff_own)
        for n, (source, target) in enumerate(
            (
                (pair_ref.at[:, :, columns], pair_all.at[:, ctx, fsdp]),
                (down_ref, down_all.at[fsdp]),
                (kv_ref, window.at[reach]),
            )
        ):
            kept.append(pltpu.make_async_copy(source, target, own_sems.at[count + n]))
        for step in range(1, reach + 1):
            copy = pltpu.make_async_copy(
                zero_ref, window.at[reach - step], own_sems.at[count + 2 + step]
            )
            empty.append((step, copy))
    for copy in kept:
        copy.start()
    for step, copy in empty:
        pl.when(ctx - step < 0)(copy.start)
    copies, sharing = front_copies(
        parts, wholes, pair_ref, pair_all, down_ref, down_all, sizes
    )
    for step, copy in halos:
        copies.append(lambda step=step, copy=copy: pl.when(ctx + step < sizes[0])(copy.start))
    copies += sharing
    run_copies(copies, send_sems, recv_sems)
    for copy in kept:
        copy.wait()
    for step, copy in empty:
        pl.when(ctx - step < 0)(copy.wait)
    for step, copy in halos:
        pl.when(ctx - step >= 0)(copy.wait_recv)
    for step, copy in halos:
        pl.when(ctx + step < sizes[0])(copy.wait_send)


def gather_front(parts, pair, down, cot, key_value, sizes, collective_id):
    ctx_size, fsdp_size = sizes
    chips = ctx_size // 2
    rows = parts[0].shape[0]
    paired = pair is not None
    reach = WINDOW // STRETCH
    count = len(parts) * (chips - 1 + chips * (2 * (fsdp_size - 1) + 1) + fsdp_size - 1)
    shapes = [
        jax.ShapeDtypeStruct((chips, 2, fsdp_size, rows, part.shape[1]), part.dtype)
        for part in parts
    ]
    arrays = list(parts)
    if paired:
        count += ctx_size - 1 + 2 * (fsdp_size - 1)
        columns = pair.shape[2] // ctx_size
        shapes += [
            jax.ShapeDtypeStruct((2, ctx_size, fsdp_size, rows, columns), pair.dtype),
            jax.ShapeDtypeStruct((fsdp_size,) + down.shape, down.dtype),
            jax.ShapeDtypeStruct((reach + 1,) + key_value.shape, key_value.dtype),
        ]
        arrays += [pair, down, key_value, jnp.zeros_like(key_value)]
    hbm = pl.BlockSpec(memory_space=pl.ANY)
    vmem = pl.BlockSpec(memory_space=pltpu.VMEM)
    return pl.pallas_call(
        functools.partial(front_kernel, sizes, len(parts), paired),
        in_specs=[vmem] * len(arrays) + [hbm] * paired,
        out_specs=[hbm] * (len(shapes) + paired),
        out_shape=shapes + ([jax.ShapeDtypeStruct(cot.shape, cot.dtype)] if paired else []),
        input_output_aliases={len(arrays): len(shapes)} if paired else {},
        scratch_shapes=[
            pltpu.SemaphoreType.DMA((count,)),
            pltpu.SemaphoreType.DMA((count,)),
            pltpu.SemaphoreType.DMA((len(shapes) + reach,)),
            pltpu.SemaphoreType.DMA((reach,)),
            pltpu.SemaphoreType.DMA((reach,)),
        ],
        compiler_params=pltpu.CompilerParams(collective_id=collective_id, has_side_effects=True),
        cost_estimate=pl.CostEstimate(
            flops=90_000_000_000, bytes_accessed=1_000_000, transcendentals=0
        ),
    )(*arrays, *([cot] if paired else []))


def hidden_kernel(sizes, pieces, pair_in, normed_ref, pair_all, normed_all, send_sems, recv_sems, own_sem):
    ctx_size, fsdp_size = sizes
    ctx, fsdp = lax.axis_index("ctx"), lax.axis_index("fsdp")
    masks = [1 << bit for bit in range(fsdp_size.bit_length() - 1)]
    far = [1 << bit for bit in range((ctx_size // 2).bit_length() - 1)]
    greet([(0, 0, m) for m in masks] + [(m, 0, 0) for m in far] + [(0, 1, 0)])
    mine = pltpu.make_async_copy(normed_ref, normed_all.at[ctx // 2, ctx % 2], own_sem)
    mine.start()
    lists = []
    for h, order in enumerate([masks, masks[::-1]]):
        view = lambda r, h=h: pair_all.at[h, :, fsdp ^ r]
        lists.append(doubling(("pair", h), fsdp_size, order, (), view, view)[0])
    rows = normed_ref.shape[0] // pieces
    lines = []
    for n in range(pieces):
        strip = pl.ds(n * rows, rows)
        lines.append(
            line_gather(("normed", n), normed_ref.at[strip], normed_all.at[:, :, strip], sizes)
        )
    ready = [[copy for hop in line for copy in hop if not copy[1]] for line in lines]
    later = [[copy for copy in hop if copy[1]] for line in lines for hop in line]
    later = [
        [hop for hop in later[n * len(lines[0]) : (n + 1) * len(lines[0])] if hop]
        for n in range(pieces)
    ]
    pair_hops = [
        [copy for pieces in zip(*(hops[n] for hops in lists)) for copy in pieces]
        for n in range(len(masks))
    ]
    ahead, depth = 2, len(later[0])
    copies = [copy for line in ready[:ahead] for copy in line] + pair_hops[0]
    for turn in range(pieces + depth - 1):
        for stage in range(depth):
            if 0 <= turn - stage < pieces:
                copies.extend(later[turn - stage][stage])
            if stage == 0 and turn + ahead < pieces:
                copies.extend(ready[turn + ahead])
        if turn == 1:
            for hop in pair_hops[1:]:
                copies.extend(hop)
    run_copies(copies, send_sems, recv_sems)
    mine.wait()


def gather_hidden(pair_all, normed, sizes):
    ctx_size, fsdp_size = sizes
    chips = ctx_size // 2
    pieces = 4
    count = 2 * (fsdp_size - 1) + pieces * (2 * chips - 1)
    hbm = pl.BlockSpec(memory_space=pl.ANY)
    return pl.pallas_call(
        functools.partial(hidden_kernel, sizes, pieces),
        in_specs=[hbm, pl.BlockSpec(memory_space=pltpu.VMEM)],
        out_specs=[hbm, hbm],
        out_shape=[
            jax.ShapeDtypeStruct(pair_all.shape, pair_all.dtype),
            jax.ShapeDtypeStruct((chips, 2) + normed.shape, normed.dtype),
        ],
        input_output_aliases={0: 0},
        scratch_shapes=[
            pltpu.SemaphoreType.DMA((count,)),
            pltpu.SemaphoreType.DMA((count,)),
            pltpu.SemaphoreType.DMA,
        ],
        compiler_params=pltpu.CompilerParams(collective_id=2, has_side_effects=True),
        cost_estimate=pl.CostEstimate(flops=90_000_000_000, bytes_accessed=30_000_000, transcendentals=0),
    )(pair_all, normed)


def hop_slots(size, order):
    slots, held = [], list(range(size))
    for mask in order:
        held = [r for r in held if not r & mask]
        slots.append(held)
    return slots


def remote(source, target, send_sem, recv_sem, peer):
    return pltpu.make_async_remote_copy(
        src_ref=source,
        dst_ref=target,
        send_sem=send_sem,
        recv_sem=recv_sem,
        device_id=peer_of(*peer),
        device_id_type=pl.DeviceIdType.MESH,
    )


def reduce_kernel(sizes, chunk, products, extras, halos, swaps, *refs):
    refs = list(refs)

    def take(amount):
        taken = refs[:amount]
        del refs[:amount]
        return taken

    lefts, right, extra = take(3)
    sent, swap_in = take(halos), take(swaps)
    (total,) = take(1)
    halo_got, swap_out = take(halos), take(swaps)
    terms, core_got, line_sent, line_got = take(4)
    core_send, core_recv, hop_send, hop_recv, line_send, line_recv = take(6)
    halo_send, halo_recv, swap_send, swap_recv, swap_own = take(5)
    hop_buffers = refs
    ctx_size, fsdp_size = sizes
    chips = ctx_size // 2
    rows = total.shape[0]
    count = products + extras
    half = chunk // 2
    masks = [1 << bit for bit in range(fsdp_size.bit_length() - 1)]
    orders = [masks, masks[::-1]]
    bits = len(masks)
    hops = [
        [hop_buffers[(h * bits + j) * 2 : (h * bits + j) * 2 + 2] for j in range(bits)]
        for h in range(2)
    ]
    slots = [hop_slots(fsdp_size, order) for order in orders]
    ctx, fsdp = lax.axis_index("ctx"), lax.axis_index("fsdp")
    chip, side = ctx // 2, ctx % 2
    if halos or swaps:
        greet(front_masks(ctx_size, fsdp_size, True))
    else:
        greet(
            [(0, 1, 0)]
            + [(0, 0, m) for m in masks]
            + [(1 << bit, 0, 0) for bit in range(chips.bit_length() - 1)]
        )
    back = []
    for n in range(halos):
        reach = halo_got[n].shape[0]
        rows_of = halo_got[n].shape[1]
        for step in range(1, reach + 1):
            copy = pltpu.make_async_remote_copy(
                src_ref=sent[n].at[pl.ds((reach - step) * rows_of, rows_of)],
                dst_ref=halo_got[n].at[step - 1],
                send_sem=halo_send.at[n, step - 1],
                recv_sem=halo_recv.at[n, step - 1],
                device_id=(lax.rem(ctx - step + ctx_size, ctx_size), fsdp),
                device_id_type=pl.DeviceIdType.MESH,
            )
            back.append((step, copy))
            pl.when(ctx - step >= 0)(copy.start)
    swapped = []
    for source, target in zip(swap_in, swap_out):
        swapped.append(pltpu.make_async_copy(source.at[ctx], target.at[ctx], swap_own))
        for mask in range(1, ctx_size):
            swapped.append(
                remote(
                    source.at[ctx ^ mask], target.at[ctx],
                    swap_send.at[mask], swap_recv.at[mask], (mask // 2, mask % 2, 0),
                )
            )
    for copy in swapped:
        copy.start()

    def core_copy(i):
        return remote(
            terms.at[i, :, 1 - side], core_got.at[i], core_send.at[i], core_recv.at[i], (0, 1, 0)
        )

    def hop_copy(h, j, i):
        sent, got = hops[h][j]
        return remote(
            sent.at[i], got.at[i], hop_send.at[h, j, i], hop_recv.at[h, j, i], (0, 0, orders[h][j])
        )

    near_first = [1 << bit for bit in range(chips.bit_length() - 1)]
    line_slots = hop_slots(chips, near_first)
    line_first = [sum(chips >> (k + 1) for k in range(j)) for j in range(len(near_first))]

    def line_copy(j, i):
        blocks = pl.ds(line_first[j], chips >> (j + 1))
        return remote(
            line_sent.at[i, blocks], line_got.at[i, blocks],
            line_send.at[i, j], line_recv.at[i, j], (near_first[j], 0, 0),
        )

    def line_held(h, upto, i, r):
        cols = slice(h * half, (h + 1) * half)
        value = held(h, bits, i, chip ^ r, 0)
        for j in range(upto):
            value += line_got[i, line_first[j] + line_slots[j].index(r), :, cols].astype(
                jnp.float32
            )
        return value

    def held(h, upto, i, z, r):
        cols = pl.ds(h * half, half)
        value = terms[i, z, side, fsdp ^ r, :, cols].astype(jnp.float32)
        value += core_got[i, z, fsdp ^ r, :, cols].astype(jnp.float32)
        for j in range(upto):
            value += hops[h][j][1][i, slots[h][j].index(r), z].astype(jnp.float32)
        return value

    slack = 3
    last = bits + 1 + slack * len(near_first)

    def step(t, carry):
        @pl.when(t < products)
        def _():
            per_left = products // lefts.shape[0]
            cols = pl.ds(pl.multiple_of(t * chunk, chunk), chunk)
            term = jnp.dot(
                lefts[t // per_left], right[:, cols], preferred_element_type=jnp.float32
            )
            terms[t] = term.astype(jnp.bfloat16).reshape(terms.shape[1:])

        if extras:
            @pl.when((t >= products) & (t < count))
            def _():
                terms[t] = extra[t - products].reshape(terms.shape[1:])

        @pl.when(t < count)
        def _():
            core_copy(t).start()

        for j in range(bits):
            @pl.when((t >= j + 1) & (t < count + j + 1))
            def _(j=j):
                i = t - (j + 1)
                if j == 0:
                    core_copy(i).wait_recv()
                for h in range(2):
                    if j:
                        hop_copy(h, j - 1, i).wait_recv()
                    for s, r in enumerate(slots[h][j]):
                        for z in range(chips):
                            hops[h][j][0][i, s, z] = held(h, j, i, z, r | orders[h][j]).astype(
                                jnp.bfloat16
                            )
                    hop_copy(h, j, i).start()

        for j in range(len(near_first)):
            lag = bits + 1 + slack * j

            @pl.when((t >= lag) & (t < count + lag))
            def _(j=j, lag=lag):
                i = t - lag
                if j:
                    line_copy(j - 1, i).wait_recv()
                for h in range(2):
                    if j == 0:
                        hop_copy(h, bits - 1, i).wait_recv()
                    for s, r in enumerate(line_slots[j]):
                        line_sent[i, line_first[j] + s, :, h * half : (h + 1) * half] = line_held(
                            h, j, i, r | near_first[j]
                        ).astype(jnp.bfloat16)
                line_copy(j, i).start()

        @pl.when(t >= last)
        def _():
            i = t - last
            line_copy(len(near_first) - 1, i).wait_recv()
            for h in range(2):
                value = line_held(h, len(near_first), i, 0)
                total[:, pl.ds(pl.multiple_of(i * chunk + h * half, half), half)] = value

        return carry

    lax.fori_loop(0, count + last, step, 0)

    def finish(i, carry):
        core_copy(i).wait_send()
        for h in range(2):
            for j in range(bits):
                hop_copy(h, j, i).wait_send()
        for j in range(len(near_first)):
            line_copy(j, i).wait_send()
        return carry

    lax.fori_loop(0, count, finish, 0)
    for copy in swapped:
        copy.wait()
    for step, copy in back:
        pl.when(ctx + step < ctx_size)(copy.wait_recv)
    for step, copy in back:
        pl.when(ctx - step >= 0)(copy.wait_send)


def reduce_rows(lefts, right, extra, halos, swaps, chunk, sizes, collective_id):
    ctx_size, fsdp_size = sizes
    chips = ctx_size // 2
    depth = lefts.shape[1]
    rows = depth // (ctx_size * fsdp_size)
    products = right.shape[1] // chunk
    extras = 0 if extra is None else extra.shape[0]
    if extra is None:
        extra = jnp.zeros((1, 16, LANES), jnp.bfloat16)
    count = products + extras
    bits = fsdp_size.bit_length() - 1
    half = chunk // 2
    reach = WINDOW // STRETCH
    buffers = []
    for _ in range(2):
        for j in range(bits):
            shape = (count, fsdp_size >> (j + 1), chips, rows, half)
            buffers += [pltpu.VMEM(shape, jnp.bfloat16)] * 2
    line = pltpu.VMEM((count, max(chips - 1, 1), rows, chunk), jnp.bfloat16)
    vmem = pl.BlockSpec(memory_space=pltpu.VMEM)
    hbm = pl.BlockSpec(memory_space=pl.ANY)
    return pl.pallas_call(
        functools.partial(reduce_kernel, sizes, chunk, products, extras, len(halos), len(swaps)),
        in_specs=[vmem] * 3 + [hbm] * (len(halos) + len(swaps)),
        out_specs=[vmem] + [hbm] * (len(halos) + len(swaps)),
        out_shape=[jax.ShapeDtypeStruct((rows, count * chunk), jnp.float32)]
        + [
            jax.ShapeDtypeStruct((reach, array.shape[0] // reach, array.shape[1]), array.dtype)
            for array in halos
        ]
        + [jax.ShapeDtypeStruct(array.shape, array.dtype) for array in swaps],
        scratch_shapes=[
            pltpu.VMEM((count, chips, 2, fsdp_size, rows, chunk), jnp.bfloat16),
            pltpu.VMEM((count, chips, fsdp_size, rows, chunk), jnp.bfloat16),
            line,
            line,
            pltpu.SemaphoreType.DMA((count,)),
            pltpu.SemaphoreType.DMA((count,)),
            pltpu.SemaphoreType.DMA((2, bits, count)),
            pltpu.SemaphoreType.DMA((2, bits, count)),
            pltpu.SemaphoreType.DMA((count, chips.bit_length() - 1)),
            pltpu.SemaphoreType.DMA((count, chips.bit_length() - 1)),
            pltpu.SemaphoreType.DMA((max(len(halos), 1), reach)),
            pltpu.SemaphoreType.DMA((max(len(halos), 1), reach)),
            pltpu.SemaphoreType.DMA((ctx_size,)),
            pltpu.SemaphoreType.DMA((ctx_size,)),
            pltpu.SemaphoreType.DMA,
        ]
        + buffers,
        compiler_params=pltpu.CompilerParams(
            collective_id=collective_id, has_side_effects=True, vmem_limit_bytes=56 * 1024 * 1024
        ),
        cost_estimate=pl.CostEstimate(flops=80_000_000_000, bytes_accessed=30_000_000, transcendentals=0),
    )(lefts, right, extra, *halos, *swaps)


def hidden_grad_kernel(
    sizes, normed, gate, up, carried_in, pair_sum, carried,
    terms, pair_sent, pair_got, pair_send, pair_recv
):
    ctx_size, fsdp_size = sizes
    count, span = terms.shape[1], normed.shape[1] // terms.shape[1]
    masks = [1 << bit for bit in range(fsdp_size.bit_length() - 1)]
    orders = [masks, masks[::-1]]
    bits = len(masks)
    slots = [hop_slots(fsdp_size, order) for order in orders]
    fsdp = lax.axis_index("fsdp")
    greet([(0, 0, m) for m in masks])
    first = [sum(fsdp_size >> (k + 1) for k in range(j)) for j in range(bits)]

    def pair_copy(h, j, i):
        rows = pl.ds(first[j], fsdp_size >> (j + 1))
        return remote(
            pair_sent.at[h, i, rows], pair_got.at[h, i, rows],
            pair_send.at[h, j, i], pair_recv.at[h, j, i], (0, 0, orders[h][j]),
        )

    def pair_held(h, upto, i, r):
        value = terms[h, i, fsdp ^ r].astype(jnp.float32)
        for j in range(upto):
            value += pair_got[h, i, first[j] + slots[h][j].index(r)].astype(jnp.float32)
        return value

    def step(t, carry):
        @pl.when(t < count)
        def _():
            rows = pl.ds(pl.multiple_of(t * span, span), span)
            for h, grad in enumerate((gate, up)):
                term = across(normed[:, rows], grad[...])
                terms[h, t] = term.astype(jnp.bfloat16).reshape(terms.shape[2:])

        for j in range(bits):
            @pl.when((t >= j) & (t < count + j))
            def _(j=j):
                i = t - j
                for h in range(2):
                    if j:
                        pair_copy(h, j - 1, i).wait_recv()
                    for s, r in enumerate(slots[h][j]):
                        pair_sent[h, i, first[j] + s] = pair_held(
                            h, j, i, r | orders[h][j]
                        ).astype(jnp.bfloat16)
                    pair_copy(h, j, i).start()

        @pl.when(t >= bits)
        def _():
            i = t - bits
            for h in range(2):
                pair_copy(h, bits - 1, i).wait_recv()
                pair_sum[i, h] = pair_held(h, bits, i, 0).astype(jnp.bfloat16)

        return carry

    lax.fori_loop(0, count + bits, step, 0)

    def finish(i, carry):
        for h in range(2):
            for j in range(bits):
                pair_copy(h, j, i).wait_send()
        return carry

    lax.fori_loop(0, count, finish, 0)


def reduce_hidden(normed, gate, up, carried, sizes):
    ctx_size, fsdp_size = sizes
    bits = fsdp_size.bit_length() - 1
    rows, columns = normed.shape[1] // (ctx_size * fsdp_size), gate.shape[1]
    pair = pltpu.VMEM((2, ctx_size, fsdp_size - 1, rows, columns), jnp.bfloat16)
    vmem = pl.BlockSpec(memory_space=pltpu.VMEM)
    hbm = pl.BlockSpec(memory_space=pl.ANY)
    return pl.pallas_call(
        functools.partial(hidden_grad_kernel, sizes),
        in_specs=[vmem] * 3 + [hbm],
        out_specs=[vmem, hbm],
        out_shape=[
            jax.ShapeDtypeStruct((ctx_size, 2, rows, columns), jnp.bfloat16),
            jax.ShapeDtypeStruct(carried.shape, carried.dtype),
        ],
        input_output_aliases={3: 1},
        scratch_shapes=[
            pltpu.VMEM((2, ctx_size, fsdp_size, rows, columns), jnp.bfloat16), pair, pair,
        ]
        + [pltpu.SemaphoreType.DMA((2, bits, ctx_size))] * 2,
        compiler_params=pltpu.CompilerParams(
            collective_id=3, has_side_effects=True, vmem_limit_bytes=60 * 1024 * 1024
        ),
        cost_estimate=pl.CostEstimate(flops=60_000_000_000, bytes_accessed=30_000_000, transcendentals=0),
    )(normed, gate, up, carried)


def norm_keys_kernel(stream, gain, weight, cosine, sine, normed_ref, pair_ref):
    x = stream[...].astype(jnp.float32)
    inverse = lax.rsqrt(jnp.mean(x * x, axis=1, keepdims=True) + EPS)
    normed = (x * inverse * gain[...]).astype(jnp.bfloat16)
    normed_ref[...] = normed
    front = product(normed, weight[...])
    kv_width = KV_HEADS * HEAD_DIM
    keys = turn(front[:, :kv_width], cosine[...], sine[...])
    pair_ref[:, :kv_width] = keys.astype(jnp.bfloat16)
    pair_ref[:, kv_width:] = front[:, kv_width : 2 * kv_width].astype(jnp.bfloat16)


def norm_keys(stream, gain, weight, cosine, sine):
    rows = stream.shape[0]
    return pl.pallas_call(
        norm_keys_kernel,
        out_shape=[
            jax.ShapeDtypeStruct(stream.shape, jnp.bfloat16),
            jax.ShapeDtypeStruct((rows, 2 * KV_HEADS * HEAD_DIM), jnp.bfloat16),
        ],
        compiler_params=pltpu.CompilerParams(vmem_limit_bytes=40 * 1024 * 1024),
        cost_estimate=pl.CostEstimate(
            flops=2 * rows * weight.size, bytes_accessed=8_000_000, transcendentals=0
        ),
    )(stream, gain, weight, cosine, sine)


def out_norm_kernel(mix, weight, stream, gain, resid, normed, total):
    i, steps = pl.program_id(0), pl.num_programs(0)
    span = weight.shape[1]
    cols = pl.ds(pl.multiple_of(i * span, span), span)
    total[:, cols] = stream[:, cols].astype(jnp.float32) + product(mix[...], weight[...])

    @pl.when(i == steps - 1)
    def _():
        h = total[...]
        resid[...] = h
        inverse = lax.rsqrt(jnp.mean(h * h, axis=1, keepdims=True) + EPS)
        normed[...] = (h * inverse * gain[...]).astype(jnp.bfloat16)


def out_norm(mix, weight, stream, gain):
    rows, width = mix.shape
    steps = 4
    whole = pl.BlockSpec((rows, width), lambda i: (0, 0))
    return pl.pallas_call(
        out_norm_kernel,
        grid=(steps,),
        in_specs=[
            whole,
            pl.BlockSpec((width, width // steps), lambda i: (0, i)),
            whole,
            pl.BlockSpec((1, width), lambda i: (0, 0)),
        ],
        out_specs=[whole, whole],
        out_shape=[
            jax.ShapeDtypeStruct((rows, width), jnp.float32),
            jax.ShapeDtypeStruct((rows, width), jnp.bfloat16),
        ],
        scratch_shapes=[pltpu.VMEM((rows, width), jnp.float32)],
        compiler_params=pltpu.CompilerParams(vmem_limit_bytes=40 * 1024 * 1024),
        cost_estimate=pl.CostEstimate(
            flops=2 * rows * width * width, bytes_accessed=14_000_000, transcendentals=0
        ),
    )(mix, weight, stream, gain)


def norm_back_kernel(
    columns, resid, gain, cot, weight, earlier, carried_in,
    grad_ref, low_ref, mix_ref, gain_ref, carried
):
    @pl.when(pl.program_id(0) == 0)
    def _():
        h = resid[...]
        inverse = lax.rsqrt(jnp.mean(h * h, axis=1, keepdims=True) + EPS)
        normal = h * inverse
        slope = columns[...].astype(jnp.float32)
        gain_ref[...] = jnp.sum(slope * normal, axis=0, keepdims=True)
        grad = cot[...].astype(jnp.float32) + norm_back(slope * gain[...], normal, inverse)
        grad_ref[...] = grad
        low_ref[...] = grad.astype(jnp.bfloat16)

    mix_ref[...] = against(low_ref[...], weight[...]).astype(jnp.bfloat16)


def norm_back_mix(columns, resid, gain, cot, weight, earlier, carried):
    rows, width = resid.shape
    steps = 4
    whole = pl.BlockSpec((rows, width), lambda i: (0, 0))
    line = pl.BlockSpec((1, width), lambda i: (0, 0))
    return pl.pallas_call(
        norm_back_kernel,
        grid=(steps,),
        in_specs=[
            whole, whole, line, whole,
            pl.BlockSpec((width // steps, width), lambda i: (i, 0)),
            pl.BlockSpec(memory_space=pl.ANY),
            pl.BlockSpec(memory_space=pl.ANY),
        ],
        out_specs=[
            whole, whole,
            pl.BlockSpec((rows, width // steps), lambda i: (0, i)),
            line,
            pl.BlockSpec(memory_space=pl.ANY),
        ],
        out_shape=[
            jax.ShapeDtypeStruct((rows, width), jnp.float32),
            jax.ShapeDtypeStruct((rows, width), jnp.bfloat16),
            jax.ShapeDtypeStruct((rows, width), jnp.bfloat16),
            jax.ShapeDtypeStruct((1, width), jnp.float32),
            jax.ShapeDtypeStruct(carried.shape, carried.dtype),
        ],
        input_output_aliases={6: 4},
        compiler_params=pltpu.CompilerParams(vmem_limit_bytes=40 * 1024 * 1024),
        cost_estimate=pl.CostEstimate(
            flops=2 * rows * width * width, bytes_accessed=16_000_000, transcendentals=0
        ),
    )(columns, resid, gain, cot, weight, earlier, carried)


def input_grad_kernel(
    dk_own, dv_own, dk_got, dv_got, cosine, sine, dq, query_weight, kv_weight, stream, gain, resid_grad,
    kv_ref, gain_ref, grad_ref, total
):
    i, steps = pl.program_id(0), pl.num_programs(0)
    span = query_weight.shape[0]
    kv_width = dk_own.shape[1]

    @pl.when(i == 0)
    def _():
        ctx, size = lax.axis_index("ctx"), lax.axis_size("ctx")
        dk, dv = dk_own[...], dv_own[...]
        for step in range(1, dk_got.shape[0] + 1):
            there = ctx + step < size
            dk += jnp.where(there, dk_got[step - 1].astype(jnp.float32), 0.0)
            dv += jnp.where(there, dv_got[step - 1].astype(jnp.float32), 0.0)
        kv_ref[:, :kv_width] = turn(dk, cosine[...], -sine[...]).astype(jnp.bfloat16)
        kv_ref[:, kv_width:] = dv.astype(jnp.bfloat16)

    cols = pl.ds(pl.multiple_of(i * span, span), span)
    total[:, cols] = against(dq[...], query_weight[...]) + against(
        kv_ref[...], kv_weight[:, : 2 * kv_width]
    )

    @pl.when(i == steps - 1)
    def _():
        x = stream[...].astype(jnp.float32)
        inverse = lax.rsqrt(jnp.mean(x * x, axis=1, keepdims=True) + EPS)
        normal = x * inverse
        slope = total[...]
        gain_ref[...] = jnp.sum(slope * normal, axis=0, keepdims=True)
        grad = resid_grad[...] + norm_back(slope * gain[...], normal, inverse)
        grad_ref[...] = grad.astype(jnp.bfloat16)


def input_grad(dk_own, dv_own, dk_got, dv_got, cosine, sine, dq, query_weight, kv_weight, stream, gain, resid_grad):
    rows, width = stream.shape
    steps = 4
    span = width // steps

    def whole(array):
        return pl.BlockSpec(array.shape, lambda i: (0,) * array.ndim)

    def strip(array):
        return pl.BlockSpec((span, array.shape[1]), lambda i: (i, 0))

    kept = (dk_own, dv_own, dk_got, dv_got, cosine, sine, dq)
    kv_shape = (rows, 2 * dk_own.shape[1])
    return pl.pallas_call(
        input_grad_kernel,
        grid=(steps,),
        in_specs=[whole(array) for array in kept]
        + [strip(query_weight), strip(kv_weight)]
        + [whole(array) for array in (stream, gain, resid_grad)],
        out_specs=[
            pl.BlockSpec(kv_shape, lambda i: (0, 0)),
            pl.BlockSpec((1, width), lambda i: (0, 0)),
            pl.BlockSpec((rows, width), lambda i: (0, 0)),
        ],
        out_shape=[
            jax.ShapeDtypeStruct(kv_shape, jnp.bfloat16),
            jax.ShapeDtypeStruct((1, width), jnp.float32),
            jax.ShapeDtypeStruct((rows, width), jnp.bfloat16),
        ],
        scratch_shapes=[pltpu.VMEM((rows, width), jnp.float32)],
        compiler_params=pltpu.CompilerParams(vmem_limit_bytes=48 * 1024 * 1024),
        cost_estimate=pl.CostEstimate(
            flops=3 * rows * width * width, bytes_accessed=24_000_000, transcendentals=0
        ),
    )(*kept, query_weight, kv_weight, stream, gain, resid_grad)


def hidden_layer_kernel(
    normed, cot, gate_weight, up_weight, down_weight,
    hidden_ref, dgate_ref, dup_ref, down_ref, columns_ref
):
    x = normed[...]
    gate = product(x, gate_weight[...])
    up = product(x, up_weight[...])
    grad = against(cot[...], down_weight[...])
    sigmoid = jax.nn.sigmoid(gate)
    silu = gate * sigmoid
    hidden = (silu * up).astype(jnp.bfloat16)
    dgate = (grad * up * sigmoid * (1.0 + gate * (1.0 - sigmoid))).astype(jnp.bfloat16)
    dup = (grad * silu).astype(jnp.bfloat16)
    hidden_ref[...] = hidden
    dgate_ref[...] = dgate
    dup_ref[...] = dup
    columns = against(dgate, gate_weight[...]) + against(dup, up_weight[...])
    columns_ref[...] = columns.astype(jnp.bfloat16)
    down_ref[...] = product(hidden, down_weight[...]).astype(jnp.bfloat16)


def hidden_layer(normed, cot, pair, down_weight):
    tokens, width = normed.shape
    share = pair.shape[2]
    tile = min(256, tokens)
    wide = pl.BlockSpec((tile, width), lambda i: (i, 0))
    thin = pl.BlockSpec((tile, share), lambda i: (i, 0))
    once = pl.Buffered(buffer_count=1)
    weights = [
        pl.BlockSpec((None,) + pair.shape[1:], lambda i, n=n: (n, 0, 0), pipeline_mode=once)
        for n in range(2)
    ]
    down = pl.BlockSpec(down_weight.shape, lambda i: (0, 0), pipeline_mode=once)
    thin_out = jax.ShapeDtypeStruct((tokens, share), jnp.bfloat16)
    wide_out = jax.ShapeDtypeStruct((tokens, width), jnp.bfloat16)
    return pl.pallas_call(
        hidden_layer_kernel,
        grid=(tokens // tile,),
        in_specs=[wide, wide] + weights + [down],
        out_specs=[thin, thin, thin, wide, wide],
        out_shape=[thin_out] * 3 + [wide_out] * 2,
        compiler_params=pltpu.CompilerParams(vmem_limit_bytes=56 * 1024 * 1024),
        cost_estimate=pl.CostEstimate(
            flops=16 * tokens * width * share, bytes_accessed=30_000_000, transcendentals=0
        ),
    )(normed, cot, pair, pair, down_weight)


def local(
    tokens,
    cotangent,
    lengths,
    attn_gain,
    query_weight,
    key_weight,
    value_weight,
    out_weight,
    mlp_gain,
    gate_weight,
    up_weight,
    down_weight,
):
    both = ("ctx", "fsdp")
    ctx_size = lax.axis_size("ctx")
    fsdp_size = lax.axis_size("fsdp")
    chips = ctx_size // 2
    stream = tokens[0].astype(jnp.float32)
    tok_rows = stream.shape[0]
    own_rows = query_weight.shape[0]
    kv_width = KV_HEADS * HEAD_DIM
    ff_own = FF // ctx_size
    reach_blocks = WINDOW // STRETCH
    ctx_place = lax.axis_index("ctx")
    doc_lengths = lengths[0]
    query_index = ctx_place * tok_rows + jnp.arange(tok_rows, dtype=jnp.int32)
    key_index = (ctx_place - reach_blocks) * tok_rows + jnp.arange(
        (reach_blocks + 1) * tok_rows, dtype=jnp.int32
    )
    query_doc = doc_segment(doc_lengths, query_index)
    key_doc = doc_segment(doc_lengths, key_index)
    position = doc_position(doc_lengths, query_index, query_doc)
    visible = (key_index[:, None] >= 0) & (key_index[:, None] <= query_index[None, :])
    visible = (
        visible
        & (query_index[None, :] - key_index[:, None] < WINDOW)
        & (query_doc[None, :] == key_doc[:, None])
    )
    bias = jnp.where(visible, 0.0, -1e30).astype(jnp.float32)
    cosine, sine = turn_tables(position)

    sizes = (ctx_size, fsdp_size)
    gains = jnp.zeros((own_rows, LANES), jnp.bfloat16)
    gains = gains.at[:, 0].set(attn_gain).at[:, 1].set(mlp_gain)
    (kv_all,) = gather_front(
        (jnp.concatenate([key_weight, value_weight, gains], axis=1),), None, None, None, None, sizes, 1
    )
    kv_all = kv_all.reshape(D, -1)
    gain_one = kv_all[:, 2 * kv_width].astype(jnp.float32)
    gain_two = kv_all[:, 2 * kv_width + 1].astype(jnp.float32)

    inv_one = lax.rsqrt(jnp.mean(stream * stream, axis=1, keepdims=True) + EPS)
    normal_one = stream * inv_one
    normed_one, own_pair = norm_keys(tokens[0], gain_one[None], kv_all, cosine, sine)
    query_all, out_all, pair_all, down_own, window, cot_own = gather_front(
        (query_weight, out_weight), jnp.stack([gate_weight, up_weight]), down_weight,
        cotangent[0], own_pair, sizes, 6,
    )
    cot_all = lax.all_gather(cot_own, "ctx", axis=0, tiled=True)
    query_all = query_all.reshape(D, D)
    out_all = out_all.reshape(D, D)
    down_own = down_own.reshape(ff_own, D)
    window = window.reshape(-1, 2 * kv_width)
    key_window, value_window = window[:, :kv_width], window[:, kv_width:]
    attn_mix, query_low, log_total = attend_forward(
        normed_one, query_all, key_window, value_window, bias, cosine, sine
    )
    resid, normed_two = out_norm(attn_mix, out_all, tokens[0], gain_two[None])
    pair, normed_all = gather_hidden(pair_all, normed_two, sizes)
    pair = pair.reshape(2, D, ff_own)
    normed_all = normed_all.reshape(ctx_size * tok_rows, D)
    hidden, grad_gate_low, grad_up_low, down_part, columns = hidden_layer(
        normed_all, cot_all, pair, down_own
    )
    columns = lax.psum_scatter(columns, "ctx", scatter_dimension=0, tiled=True)
    pair_sum, down_part = reduce_hidden(normed_all, grad_gate_low, grad_up_low, down_part, sizes)
    down_terms = across(hidden, cot_all).astype(jnp.bfloat16)
    grad_resid, grad_resid_low, grad_mix_low, mlp_gain_local, down_terms = norm_back_mix(
        columns, resid, gain_two[None], cotangent[0], out_all, pair_sum, down_terms
    )
    down_sum = lax.psum_scatter(down_part, "ctx", scatter_dimension=0, tiled=True)
    grad_query_low, dk_low, dv_low, dk_own, dv_own, down_terms = attend_backward(
        query_low, key_window, value_window, grad_mix_low, attn_mix, log_total, bias, cosine, sine,
        down_terms,
    )
    grad_down = lax.psum_scatter(down_terms, "fsdp", scatter_dimension=0, tiled=True)
    wide_grad, dk_got, dv_got = reduce_rows(
        jnp.stack([normed_one.T, attn_mix.T]),
        jnp.concatenate([grad_query_low, grad_resid_low], axis=1),
        None, (dk_low, dv_low), (), 512, sizes, 4,
    )
    kv_low, attn_gain_local, grad_input = input_grad(
        dk_own, dv_own, dk_got, dv_got, cosine, sine, grad_query_low, query_all, kv_all,
        tokens[0], gain_one[None], grad_resid,
    )
    gain_terms = jnp.stack([attn_gain_local[0], mlp_gain_local[0]], axis=1).astype(jnp.bfloat16)
    gain_terms = jnp.pad(gain_terms, ((0, 0), (0, 2 * LANES - 2)))[None]
    kv_grad, pair_sum = reduce_rows(
        normed_one.T[None], kv_low, gain_terms, (), (pair_sum,), 2 * LANES, sizes, 5
    )
    mixed = after(resid, kv_grad) + after(down_sum, kv_grad).astype(jnp.float32)
    mixed = mixed.astype(jnp.bfloat16)
    pair_sum = pair_sum.transpose(1, 2, 0, 3).reshape(2, own_rows, FF).astype(jnp.float32)
    return (
        mixed[None],
        grad_input[None],
        kv_grad[:, 2 * kv_width],
        wide_grad[:, :D],
        kv_grad[:, :kv_width],
        kv_grad[:, kv_width : 2 * kv_width],
        wide_grad[:, D:],
        kv_grad[:, 2 * kv_width + 1],
        pair_sum[0],
        pair_sum[1],
        grad_down.astype(jnp.float32),
    )


def solution(mesh):
    in_specs = (
        P("fsdp", "ctx", None),
        P("fsdp", "ctx", None),
        P("fsdp", None),
        P(("ctx", "fsdp")),
        P(("ctx", "fsdp"), None),
        P(("ctx", "fsdp"), None),
        P(("ctx", "fsdp"), None),
        P(("ctx", "fsdp"), None),
        P(("ctx", "fsdp")),
        P(("ctx", "fsdp"), None),
        P(("ctx", "fsdp"), None),
        P(("ctx", "fsdp"), None),
    )
    out_specs = (
        P("fsdp", "ctx", None),
        P("fsdp", "ctx", None),
        P(("ctx", "fsdp")),
        P(("ctx", "fsdp"), None),
        P(("ctx", "fsdp"), None),
        P(("ctx", "fsdp"), None),
        P(("ctx", "fsdp"), None),
        P(("ctx", "fsdp")),
        P(("ctx", "fsdp"), None),
        P(("ctx", "fsdp"), None),
        P(("ctx", "fsdp"), None),
    )
    return jax.shard_map(local, mesh=mesh, in_specs=in_specs, out_specs=out_specs, check_vma=False)
```

```python
import functools

import jax
import jax.numpy as jnp
from jax import lax
from jax.experimental import pallas as pl
from jax.experimental.pallas import tpu as pltpu
from jax.sharding import PartitionSpec as P

D = 2048
FF = 8192
HEADS = 32
KV_HEADS = 8
HEAD_DIM = 64
WINDOW = 1024
STRETCH = 256
QTILE = 128
LANES = 128
EPS = 1e-05
THETA = 500000.0


def passed_along(x, axis, by):
    size = lax.axis_size(axis)
    pairs = [(i, i + by) for i in range(size) if 0 <= i + by < size]
    return lax.ppermute(x, axis, pairs)


def product(left, right):
    return jnp.dot(left, right, preferred_element_type=jnp.float32)


def against(left, right):
    return lax.dot_general(
        left, right, (((1,), (1,)), ((), ())), preferred_element_type=jnp.float32
    )


def across(left, right):
    return lax.dot_general(
        left, right, (((0,), (0,)), ((), ())), preferred_element_type=jnp.float32
    )


def doc_segment(doc_lengths, index):
    doc_ends = jnp.cumsum(doc_lengths)
    return jnp.sum((index[:, None] >= doc_ends[None, :]).astype(jnp.int32), axis=1)


def doc_position(doc_lengths, index, segment):
    doc_ends = jnp.cumsum(doc_lengths)
    doc_starts = doc_ends - doc_lengths
    member = segment[:, None] == jnp.arange(doc_lengths.shape[0], dtype=jnp.int32)[None, :]
    return index - jnp.sum(jnp.where(member, doc_starts[None, :], 0), axis=1)


def swap_halves(u):
    half = HEAD_DIM // 2
    width = u.shape[1]
    lane = lax.broadcasted_iota(jnp.int32, u.shape, 1)
    ahead = pltpu.roll(u, width - half, 1)
    behind = pltpu.roll(u, half, 1)
    return jnp.where(lane % HEAD_DIM < half, ahead, behind)


def turn(u, cosine, sine):
    copies = u.shape[1] // cosine.shape[1]
    cosine = jnp.concatenate([cosine] * copies, axis=1)
    sine = jnp.concatenate([sine] * copies, axis=1)
    return u * cosine + swap_halves(u) * sine


def nt(left, right):
    return lax.dot_general(left, right, (((1,), (1,)), ((), ())), preferred_element_type=jnp.float32)


def nn(left, right):
    return lax.dot_general(left, right, (((1,), (0,)), ((), ())), preferred_element_type=jnp.float32)


def attend_forward_kernel(
    n_ref, w_ref, k_ref, v_ref, bias_ref, cos_ref, sin_ref, o_ref, qr_ref, lse_ref
):
    rows = n_ref.shape[0]
    group = HEADS // KV_HEADS
    span = k_ref.shape[0] - rows + QTILE
    rotated = turn(product(n_ref[...], w_ref[...]), cos_ref[...], sin_ref[...])
    qr_ref[...] = rotated.astype(jnp.bfloat16)
    scaled = (qr_ref[...].astype(jnp.float32) * HEAD_DIM ** (-0.5)).astype(jnp.bfloat16)
    for tile in range(rows // QTILE):
        first = tile * QTILE
        bias = bias_ref[first : first + span, first : first + QTILE]
        for kv in range(LANES // HEAD_DIM):
            lo = kv * HEAD_DIM
            keys = k_ref[first : first + span, lo : lo + HEAD_DIM]
            values = v_ref[first : first + span, lo : lo + HEAD_DIM]
            values_t = values.T
            raises, totals = [], []
            for h in range(group):
                head = kv * group + h
                q_h = scaled[first : first + QTILE, head * HEAD_DIM : (head + 1) * HEAD_DIM]
                s = nt(keys, q_h) + bias
                top = jnp.max(s, axis=0, keepdims=True)
                raised = jnp.exp(s - top)
                total = jnp.sum(raised, axis=0, keepdims=True)
                lse_ref[head : head + 1, first : first + QTILE] = top + jnp.log(total)
                raises.append(raised.astype(jnp.bfloat16))
                totals.append(total)
            o_wide = nn(values_t, jnp.concatenate(raises, axis=1)) / jnp.concatenate(totals, axis=1)
            o_t = jnp.concatenate(
                [o_wide[:, h * QTILE : (h + 1) * QTILE] for h in range(group)], axis=0
            )
            o_ref[first : first + QTILE, kv * group * HEAD_DIM : (kv + 1) * group * HEAD_DIM] = (
                o_t.T.astype(jnp.bfloat16)
            )


def attend_forward(normed, weight, k, v, bias, cosine, sine):
    rows, width = normed.shape[0], weight.shape[1]
    steps = KV_HEADS * HEAD_DIM // LANES
    qw = width // steps
    heads = HEADS // steps
    window = k.shape[0]
    return pl.pallas_call(
        attend_forward_kernel,
        grid=(steps,),
        in_specs=[
            pl.BlockSpec(normed.shape, lambda i: (0, 0)),
            pl.BlockSpec((weight.shape[0], qw), lambda i: (0, i)),
            pl.BlockSpec((window, LANES), lambda i: (0, i)),
            pl.BlockSpec((window, LANES), lambda i: (0, i)),
            pl.BlockSpec((window, rows), lambda i: (0, 0)),
            pl.BlockSpec((rows, LANES), lambda i: (0, 0)),
            pl.BlockSpec((rows, LANES), lambda i: (0, 0)),
        ],
        out_specs=[
            pl.BlockSpec((rows, qw), lambda i: (0, i)),
            pl.BlockSpec((rows, qw), lambda i: (0, i)),
            pl.BlockSpec((heads, rows), lambda i: (i, 0)),
        ],
        out_shape=[
            jax.ShapeDtypeStruct((rows, width), jnp.bfloat16),
            jax.ShapeDtypeStruct((rows, width), jnp.bfloat16),
            jax.ShapeDtypeStruct((HEADS, rows), jnp.float32),
        ],
        compiler_params=pltpu.CompilerParams(vmem_limit_bytes=48 * 1024 * 1024),
        cost_estimate=pl.CostEstimate(flops=40_000_000_000, bytes_accessed=10_000_000, transcendentals=0),
    )(normed, weight, k, v, bias, cosine, sine)


def attend_backward_kernel(
    qr_ref, k_ref, v_ref, do_ref, o_ref, lse_ref, bias_ref, cos_ref, sin_ref,
    carried_in, dq_ref, dk_low, dv_low, dk_own, dv_own, carried, dk_ref, dv_ref
):
    rows = qr_ref.shape[0]
    group = HEADS // KV_HEADS
    span = k_ref.shape[0] - rows + QTILE
    scale = HEAD_DIM ** (-0.5)
    dk_ref[...] = jnp.zeros_like(dk_ref)
    dv_ref[...] = jnp.zeros_like(dv_ref)
    scaled = (qr_ref[...].astype(jnp.float32) * scale).astype(jnp.bfloat16)
    wide = LANES // HEAD_DIM * group * HEAD_DIM
    owner = lax.broadcasted_iota(jnp.int32, (8, wide), 1) // HEAD_DIM
    pick = (owner == lax.broadcasted_iota(jnp.int32, (8, wide), 0)).astype(jnp.float32)
    for tile in range(rows // QTILE):
        first = tile * QTILE
        bias = bias_ref[first : first + span, first : first + QTILE]
        both = do_ref[first : first + QTILE, :].astype(jnp.float32) * o_ref[
            first : first + QTILE, :
        ].astype(jnp.float32)
        delta = lax.dot_general(
            pick, both, (((1,), (1,)), ((), ())),
            precision=lax.Precision.HIGHEST, preferred_element_type=jnp.float32,
        )
        dk_pair, dv_pair, dqs = [], [], []
        for kv in range(LANES // HEAD_DIM):
            lo = kv * HEAD_DIM
            keys = k_ref[first : first + span, lo : lo + HEAD_DIM]
            values = v_ref[first : first + span, lo : lo + HEAD_DIM]
            keys_t = keys.T
            probs, slopes, qs, dos = [], [], [], []
            for h in range(group):
                head = kv * group + h
                cols = slice(head * HEAD_DIM, (head + 1) * HEAD_DIM)
                q_h = scaled[first : first + QTILE, cols]
                do_h = do_ref[first : first + QTILE, cols]
                s = nt(keys, q_h) + bias
                p = jnp.exp(s - lse_ref[head : head + 1, first : first + QTILE])
                dp = nt(values, do_h)
                ds = (p * (dp - delta[head : head + 1, :])).astype(jnp.bfloat16)
                probs.append(p.astype(jnp.bfloat16))
                slopes.append(ds)
                qs.append(q_h)
                dos.append(do_h)
            p_all = jnp.concatenate(probs, axis=1)
            ds_all = jnp.concatenate(slopes, axis=1)
            dv_pair.append(nn(p_all, jnp.concatenate(dos, axis=0)))
            dk_pair.append(nn(ds_all, jnp.concatenate(qs, axis=0)))
            dq_t = nn(keys_t, ds_all) * scale
            dqs.extend(dq_t[:, h * QTILE : (h + 1) * QTILE] for h in range(group))
        dk_ref[first : first + span, :] += jnp.concatenate(dk_pair, axis=1)
        dv_ref[first : first + span, :] += jnp.concatenate(dv_pair, axis=1)
        dq = jnp.concatenate(dqs, axis=0).T
        dq_ref[first : first + QTILE, :] = turn(
            dq, cos_ref[first : first + QTILE, :], -sin_ref[first : first + QTILE, :]
        ).astype(jnp.bfloat16)
    before = dk_low.shape[0]
    dk_low[...] = dk_ref[:before, :].astype(jnp.bfloat16)
    dv_low[...] = dv_ref[:before, :].astype(jnp.bfloat16)
    dk_own[...] = dk_ref[before:, :]
    dv_own[...] = dv_ref[before:, :]


def attend_backward(qr, k, v, do, o, lse, bias, cosine, sine, carried):
    rows, width = qr.shape
    steps = KV_HEADS * HEAD_DIM // LANES
    qw = width // steps
    heads = HEADS // steps
    window = k.shape[0]
    wide = pl.BlockSpec((rows, qw), lambda i: (0, i))
    tall = pl.BlockSpec((window, LANES), lambda i: (0, i))
    table = pl.BlockSpec((rows, LANES), lambda i: (0, 0))
    return pl.pallas_call(
        attend_backward_kernel,
        grid=(steps,),
        in_specs=[
            wide, tall, tall, wide, wide,
            pl.BlockSpec((heads, rows), lambda i: (i, 0)),
            pl.BlockSpec((window, rows), lambda i: (0, 0)),
            table, table,
            pl.BlockSpec(memory_space=pl.ANY),
        ],
        out_specs=[
            wide,
            pl.BlockSpec((window - rows, LANES), lambda i: (0, i)),
            pl.BlockSpec((window - rows, LANES), lambda i: (0, i)),
            pl.BlockSpec((rows, LANES), lambda i: (0, i)),
            pl.BlockSpec((rows, LANES), lambda i: (0, i)),
            pl.BlockSpec(memory_space=pl.ANY),
        ],
        out_shape=[
            jax.ShapeDtypeStruct((rows, width), jnp.bfloat16),
            jax.ShapeDtypeStruct((window - rows, k.shape[1]), jnp.bfloat16),
            jax.ShapeDtypeStruct((window - rows, k.shape[1]), jnp.bfloat16),
            jax.ShapeDtypeStruct((rows, k.shape[1]), jnp.float32),
            jax.ShapeDtypeStruct((rows, k.shape[1]), jnp.float32),
            jax.ShapeDtypeStruct(carried.shape, carried.dtype),
        ],
        input_output_aliases={9: 5},
        scratch_shapes=[pltpu.VMEM((window, LANES), jnp.float32)] * 2,
        compiler_params=pltpu.CompilerParams(vmem_limit_bytes=48 * 1024 * 1024),
        cost_estimate=pl.CostEstimate(flops=80_000_000_000, bytes_accessed=20_000_000, transcendentals=0),
    )(qr, k, v, do, o, lse, bias, cosine, sine, carried)


def turn_tables(position):
    half_dim = HEAD_DIM // 2
    frequency = THETA ** (-2.0 * jnp.arange(half_dim, dtype=jnp.float32) / HEAD_DIM)
    angles = position.astype(jnp.float32)[:, None] * frequency[None, :]
    cosine, sine = jnp.cos(angles), jnp.sin(angles)
    copies = LANES // HEAD_DIM
    return (
        jnp.concatenate([cosine, cosine] * copies, axis=1),
        jnp.concatenate([-sine, sine] * copies, axis=1),
    )


def rope(u, cosine, sine):
    half = HEAD_DIM // 2
    parts = u.reshape(u.shape[0], -1, 2, half)
    swapped_parts = parts[:, :, ::-1, :].reshape(u.shape)
    copies = u.shape[1] // LANES
    return u * jnp.tile(cosine, (1, copies)) + swapped_parts * jnp.tile(sine, (1, copies))


def norm_back(grad_normal, normal, inverse):
    return inverse * (grad_normal - normal * jnp.mean(grad_normal * normal, axis=1, keepdims=True))


def after(x, *others):
    return lax.optimization_barrier((x,) + others)[0]


def peer_of(chip_mask, side_mask, fsdp_mask):
    ctx = lax.axis_index("ctx")
    return (ctx ^ (2 * chip_mask + side_mask), lax.axis_index("fsdp") ^ fsdp_mask)


def greet(peers):
    barrier = pltpu.get_barrier_semaphore()
    for peer in peers:
        pl.semaphore_signal(
            barrier, inc=1, device_id=peer_of(*peer), device_id_type=pl.DeviceIdType.MESH
        )
    pl.semaphore_wait(barrier, len(peers))


def run_copies(copies, send_sems, recv_sems):
    started, arrived = {}, set()

    def arrive(name):
        if name not in arrived:
            arrived.add(name)
            started[name].wait_recv()

    for copy in copies:
        if callable(copy):
            copy()
            continue
        at = len(started)
        name, awaited, source, target, peer = copy
        for other in awaited:
            arrive(other)
        started[name] = pltpu.make_async_remote_copy(
            src_ref=source,
            dst_ref=target,
            send_sem=send_sems.at[at],
            recv_sem=recv_sems.at[at],
            device_id=peer_of(*peer),
            device_id_type=pl.DeviceIdType.MESH,
        )
        started[name].start()
    for name in started:
        arrive(name)
    for name in started:
        started[name].wait_send()


def doubling(name, size, order, awaited, block, target, along=2):
    hops, held = [], {0: awaited}
    for mask in order:
        hop, got = [], {}
        for r, needs in held.items():
            key = (name, r, mask)
            peer = tuple(mask if place == along else 0 for place in range(3))
            hop.append((key, needs, block(r), target(r), peer))
            got[r ^ mask] = (key,)
        held.update(got)
        hops.append(hop)
    return hops, held


def line_gather(name, own, whole, sizes):
    chips = sizes[0] // 2
    ctx = lax.axis_index("ctx")
    chip, side = ctx // 2, ctx % 2
    far_first = [1 << bit for bit in range(chips.bit_length() - 1)][::-1]
    target = lambda r: whole.at[chip ^ r, side]
    block = lambda r: target(r) if r else own
    hops, held = doubling((name, "z"), chips, far_first, (), block, target, 0)
    last = [
        ((name, "core", r), held[r], block(r), target(r), (0, 1, 0)) for r in range(chips)
    ]
    return hops + [last]


def front_masks(ctx_size, fsdp_size, paired):
    chips = ctx_size // 2
    peers = [
        (m, s, 0)
        for m in range(chips)
        for s in range(2)
        if (m or s) and (paired or m + s == 1 or (not s and not m & (m - 1)))
    ]
    return peers + [(0, 0, m) for m in range(1, fsdp_size)]


def front_copies(parts, wholes, pair_ref, pair_all, down_ref, down_all, sizes):
    ctx_size, fsdp_size = sizes
    chips = ctx_size // 2
    ctx, fsdp = lax.axis_index("ctx"), lax.axis_index("fsdp")
    chip, side = ctx // 2, ctx % 2
    masks = [1 << bit for bit in range(fsdp_size.bit_length() - 1)]
    orders = [masks, masks[::-1]]
    far_first = [1 << bit for bit in range(chips.bit_length() - 1)][::-1]
    copies, arrival = [], {}
    lines = []
    for n, (own, whole) in enumerate(zip(parts, wholes)):
        view = lambda r, own=own, whole=whole: (
            whole.at[chip ^ r, side, fsdp] if r else own
        )
        target = lambda r, whole=whole: whole.at[chip ^ r, side, fsdp]
        hops, held = doubling(("z", n), chips, far_first, (), view, target, 0)
        lines.append(hops)
        for r, keys in held.items():
            arrival[n, r] = keys
    for hop in zip(*lines):
        for pieces in hop:
            copies.extend(pieces)
    exchange = []
    if pair_ref is not None:
        ff_own = pair_ref.shape[2] // ctx_size
        for m in range(chips):
            for s in range(2):
                if m or s:
                    other = ctx ^ (2 * m + s)
                    columns = pl.ds(pl.multiple_of(other * ff_own, ff_own), ff_own)
                    exchange.append(
                        (
                            ("pair", m, s), (), pair_ref.at[:, :, columns],
                            pair_all.at[:, ctx, fsdp], (m, s, 0),
                        )
                    )
    queues = []
    if down_ref is not None:
        width = down_ref.shape[1] // 2
        lists = []
        for h, order in enumerate(orders):
            cols = pl.ds(h * width, width)
            target = lambda r, cols=cols: down_all.at[fsdp ^ r, :, cols]
            block = lambda r, cols=cols: (
                down_all.at[fsdp ^ r, :, cols] if r else down_ref.at[:, cols]
            )
            lists.append(doubling(("down", h), fsdp_size, order, (), block, target)[0])
        stages = [[copy for pieces in zip(*hop) for copy in pieces] for hop in zip(*lists)]
        queues.append(stages + [[]])
    for n, (own, whole) in enumerate(zip(parts, wholes)):
        width = own.shape[1]
        cut = (width // 2 + LANES - 1) // LANES * LANES
        halves = [(0, cut), (cut, width - cut)]
        for m in range(chips):
            first = arrival[n, m]
            lists, last = [], []
            for h, ((lo, span), order) in enumerate(zip(halves, orders)):
                cols = pl.ds(lo, span)

                def block(r, m=m, cols=cols, own=own, whole=whole):
                    if m == 0 and r == 0:
                        return own.at[:, cols]
                    return whole.at[chip ^ m, side, fsdp ^ r, :, cols]

                def target(r, m=m, cols=cols, whole=whole):
                    return whole.at[chip ^ m, side, fsdp ^ r, :, cols]

                hops, held = doubling(("f", n, m, h), fsdp_size, order, first, block, target)
                lists.append(hops)
                last.extend(key for keys in held.values() for key in keys)
            stages = [[copy for pieces in zip(*hop) for copy in pieces] for hop in zip(*lists)]
            row = whole.at[chip ^ m, side]
            if m:
                stages.append([(("core", n, m), tuple(last), row, row, (0, 1, 0))])
            else:
                stages.append(
                    [
                        (
                            ("core", n, m, r), tuple(last),
                            row.at[fsdp ^ r] if r else own, row.at[fsdp ^ r], (0, 1, 0),
                        )
                        for r in range(fsdp_size)
                    ]
                )
            queues.append(stages)
    sharing = []
    lag = 2
    for turn in range(len(queues) + lag * (len(orders[0]) + 1)):
        for stage in range(len(orders[0]) + 1):
            at = turn - lag * stage
            if 0 <= at < len(queues):
                sharing.extend(queues[at][stage])
        if turn == chips:
            sharing.extend(exchange)
    return copies, sharing


def front_kernel(sizes, count, paired, *refs):
    parts, refs = refs[:count], refs[count:]
    if paired:
        pair_ref, down_ref, kv_ref, zero_ref, cot_in, *refs = refs
    else:
        pair_ref = down_ref = None
    wholes, refs = refs[:count], refs[count:]
    if paired:
        pair_all, down_all, window, cot_out, *refs = refs
    else:
        pair_all = down_all = None
    send_sems, recv_sems, own_sems, halo_send, halo_recv = refs
    greet(front_masks(*sizes, paired))
    ctx, fsdp = lax.axis_index("ctx"), lax.axis_index("fsdp")
    reach = halo_send.shape[0]
    halos = []
    if paired:
        for step in range(1, reach + 1):
            copy = pltpu.make_async_remote_copy(
                src_ref=kv_ref,
                dst_ref=window.at[reach - step],
                send_sem=halo_send.at[step - 1],
                recv_sem=halo_recv.at[step - 1],
                device_id=(lax.rem(ctx + step, sizes[0]), fsdp),
                device_id_type=pl.DeviceIdType.MESH,
            )
            halos.append((step, copy))
    kept = []
    for n, (own, whole) in enumerate(zip(parts, wholes)):
        kept.append(
            pltpu.make_async_copy(own, whole.at[ctx // 2, ctx % 2, fsdp], own_sems.at[n])
        )
    empty = []
    if paired:
        ff_own = pair_ref.shape[2] // sizes[0]
        columns = pl.ds(pl.multiple_of(ctx * ff_own, ff_own), ff_own)
        for n, (source, target) in enumerate(
            (
                (pair_ref.at[:, :, columns], pair_all.at[:, ctx, fsdp]),
                (down_ref, down_all.at[fsdp]),
                (kv_ref, window.at[reach]),
            )
        ):
            kept.append(pltpu.make_async_copy(source, target, own_sems.at[count + n]))
        for step in range(1, reach + 1):
            copy = pltpu.make_async_copy(
                zero_ref, window.at[reach - step], own_sems.at[count + 2 + step]
            )
            empty.append((step, copy))
    for copy in kept:
        copy.start()
    for step, copy in empty:
        pl.when(ctx - step < 0)(copy.start)
    copies, sharing = front_copies(
        parts, wholes, pair_ref, pair_all, down_ref, down_all, sizes
    )
    for step, copy in halos:
        copies.append(lambda step=step, copy=copy: pl.when(ctx + step < sizes[0])(copy.start))
    copies += sharing
    run_copies(copies, send_sems, recv_sems)
    for copy in kept:
        copy.wait()
    for step, copy in empty:
        pl.when(ctx - step < 0)(copy.wait)
    for step, copy in halos:
        pl.when(ctx - step >= 0)(copy.wait_recv)
    for step, copy in halos:
        pl.when(ctx + step < sizes[0])(copy.wait_send)


def gather_front(parts, pair, down, cot, key_value, sizes, collective_id):
    ctx_size, fsdp_size = sizes
    chips = ctx_size // 2
    rows = parts[0].shape[0]
    paired = pair is not None
    reach = WINDOW // STRETCH
    count = len(parts) * (chips - 1 + chips * (2 * (fsdp_size - 1) + 1) + fsdp_size - 1)
    shapes = [
        jax.ShapeDtypeStruct((chips, 2, fsdp_size, rows, part.shape[1]), part.dtype)
        for part in parts
    ]
    arrays = list(parts)
    if paired:
        count += ctx_size - 1 + 2 * (fsdp_size - 1)
        columns = pair.shape[2] // ctx_size
        shapes += [
            jax.ShapeDtypeStruct((2, ctx_size, fsdp_size, rows, columns), pair.dtype),
            jax.ShapeDtypeStruct((fsdp_size,) + down.shape, down.dtype),
            jax.ShapeDtypeStruct((reach + 1,) + key_value.shape, key_value.dtype),
        ]
        arrays += [pair, down, key_value, jnp.zeros_like(key_value)]
    hbm = pl.BlockSpec(memory_space=pl.ANY)
    vmem = pl.BlockSpec(memory_space=pltpu.VMEM)
    return pl.pallas_call(
        functools.partial(front_kernel, sizes, len(parts), paired),
        in_specs=[vmem] * len(arrays) + [hbm] * paired,
        out_specs=[hbm] * (len(shapes) + paired),
        out_shape=shapes + ([jax.ShapeDtypeStruct(cot.shape, cot.dtype)] if paired else []),
        input_output_aliases={len(arrays): len(shapes)} if paired else {},
        scratch_shapes=[
            pltpu.SemaphoreType.DMA((count,)),
            pltpu.SemaphoreType.DMA((count,)),
            pltpu.SemaphoreType.DMA((len(shapes) + reach,)),
            pltpu.SemaphoreType.DMA((reach,)),
            pltpu.SemaphoreType.DMA((reach,)),
        ],
        compiler_params=pltpu.CompilerParams(collective_id=collective_id, has_side_effects=True),
        cost_estimate=pl.CostEstimate(
            flops=90_000_000_000, bytes_accessed=1_000_000, transcendentals=0
        ),
    )(*arrays, *([cot] if paired else []))


def hidden_kernel(sizes, pieces, pair_in, normed_ref, pair_all, normed_all, send_sems, recv_sems, own_sem):
    ctx_size, fsdp_size = sizes
    ctx, fsdp = lax.axis_index("ctx"), lax.axis_index("fsdp")
    masks = [1 << bit for bit in range(fsdp_size.bit_length() - 1)]
    far = [1 << bit for bit in range((ctx_size // 2).bit_length() - 1)]
    greet([(0, 0, m) for m in masks] + [(m, 0, 0) for m in far] + [(0, 1, 0)])
    mine = pltpu.make_async_copy(normed_ref, normed_all.at[ctx // 2, ctx % 2], own_sem)
    mine.start()
    lists = []
    for h, order in enumerate([masks, masks[::-1]]):
        view = lambda r, h=h: pair_all.at[h, :, fsdp ^ r]
        lists.append(doubling(("pair", h), fsdp_size, order, (), view, view)[0])
    rows = normed_ref.shape[0] // pieces
    lines = []
    for n in range(pieces):
        strip = pl.ds(n * rows, rows)
        lines.append(
            line_gather(("normed", n), normed_ref.at[strip], normed_all.at[:, :, strip], sizes)
        )
    ready = [[copy for hop in line for copy in hop if not copy[1]] for line in lines]
    later = [[copy for copy in hop if copy[1]] for line in lines for hop in line]
    later = [
        [hop for hop in later[n * len(lines[0]) : (n + 1) * len(lines[0])] if hop]
        for n in range(pieces)
    ]
    pair_hops = [
        [copy for pieces in zip(*(hops[n] for hops in lists)) for copy in pieces]
        for n in range(len(masks))
    ]
    ahead, depth = 2, len(later[0])
    copies = [copy for line in ready[:ahead] for copy in line] + pair_hops[0]
    for turn in range(pieces + depth - 1):
        for stage in range(depth):
            if 0 <= turn - stage < pieces:
                copies.extend(later[turn - stage][stage])
            if stage == 0 and turn + ahead < pieces:
                copies.extend(ready[turn + ahead])
        if turn == 1:
            for hop in pair_hops[1:]:
                copies.extend(hop)
    run_copies(copies, send_sems, recv_sems)
    mine.wait()


def gather_hidden(pair_all, normed, sizes):
    ctx_size, fsdp_size = sizes
    chips = ctx_size // 2
    pieces = 4
    count = 2 * (fsdp_size - 1) + pieces * (2 * chips - 1)
    hbm = pl.BlockSpec(memory_space=pl.ANY)
    return pl.pallas_call(
        functools.partial(hidden_kernel, sizes, pieces),
        in_specs=[hbm, pl.BlockSpec(memory_space=pltpu.VMEM)],
        out_specs=[hbm, hbm],
        out_shape=[
            jax.ShapeDtypeStruct(pair_all.shape, pair_all.dtype),
            jax.ShapeDtypeStruct((chips, 2) + normed.shape, normed.dtype),
        ],
        input_output_aliases={0: 0},
        scratch_shapes=[
            pltpu.SemaphoreType.DMA((count,)),
            pltpu.SemaphoreType.DMA((count,)),
            pltpu.SemaphoreType.DMA,
        ],
        compiler_params=pltpu.CompilerParams(collective_id=2, has_side_effects=True),
        cost_estimate=pl.CostEstimate(flops=90_000_000_000, bytes_accessed=30_000_000, transcendentals=0),
    )(pair_all, normed)


def hop_slots(size, order):
    slots, held = [], list(range(size))
    for mask in order:
        held = [r for r in held if not r & mask]
        slots.append(held)
    return slots


def remote(source, target, send_sem, recv_sem, peer):
    return pltpu.make_async_remote_copy(
        src_ref=source,
        dst_ref=target,
        send_sem=send_sem,
        recv_sem=recv_sem,
        device_id=peer_of(*peer),
        device_id_type=pl.DeviceIdType.MESH,
    )


def reduce_kernel(sizes, chunk, products, extras, halos, swaps, *refs):
    refs = list(refs)

    def take(amount):
        taken = refs[:amount]
        del refs[:amount]
        return taken

    lefts, right, extra = take(3)
    sent, swap_in = take(halos), take(swaps)
    (total,) = take(1)
    halo_got, swap_out = take(halos), take(swaps)
    terms, core_got, line_sent, line_got = take(4)
    core_send, core_recv, hop_send, hop_recv, line_send, line_recv = take(6)
    halo_send, halo_recv, swap_send, swap_recv, swap_own = take(5)
    hop_buffers = refs
    ctx_size, fsdp_size = sizes
    chips = ctx_size // 2
    rows = total.shape[0]
    count = products + extras
    half = chunk // 2
    masks = [1 << bit for bit in range(fsdp_size.bit_length() - 1)]
    orders = [masks, masks[::-1]]
    bits = len(masks)
    hops = [
        [hop_buffers[(h * bits + j) * 2 : (h * bits + j) * 2 + 2] for j in range(bits)]
        for h in range(2)
    ]
    slots = [hop_slots(fsdp_size, order) for order in orders]
    ctx, fsdp = lax.axis_index("ctx"), lax.axis_index("fsdp")
    chip, side = ctx // 2, ctx % 2
    if halos or swaps:
        greet(front_masks(ctx_size, fsdp_size, True))
    else:
        greet(
            [(0, 1, 0)]
            + [(0, 0, m) for m in masks]
            + [(1 << bit, 0, 0) for bit in range(chips.bit_length() - 1)]
        )
    back = []
    for n in range(halos):
        reach = halo_got[n].shape[0]
        rows_of = halo_got[n].shape[1]
        for step in range(1, reach + 1):
            copy = pltpu.make_async_remote_copy(
                src_ref=sent[n].at[pl.ds((reach - step) * rows_of, rows_of)],
                dst_ref=halo_got[n].at[step - 1],
                send_sem=halo_send.at[n, step - 1],
                recv_sem=halo_recv.at[n, step - 1],
                device_id=(lax.rem(ctx - step + ctx_size, ctx_size), fsdp),
                device_id_type=pl.DeviceIdType.MESH,
            )
            back.append((step, copy))
            pl.when(ctx - step >= 0)(copy.start)
    swapped = []
    for source, target in zip(swap_in, swap_out):
        swapped.append(pltpu.make_async_copy(source.at[ctx], target.at[ctx], swap_own))
        for mask in range(1, ctx_size):
            swapped.append(
                remote(
                    source.at[ctx ^ mask], target.at[ctx],
                    swap_send.at[mask], swap_recv.at[mask], (mask // 2, mask % 2, 0),
                )
            )
    for copy in swapped:
        copy.start()

    def core_copy(i):
        return remote(
            terms.at[i, :, 1 - side], core_got.at[i], core_send.at[i], core_recv.at[i], (0, 1, 0)
        )

    def hop_copy(h, j, i):
        sent, got = hops[h][j]
        return remote(
            sent.at[i], got.at[i], hop_send.at[h, j, i], hop_recv.at[h, j, i], (0, 0, orders[h][j])
        )

    near_first = [1 << bit for bit in range(chips.bit_length() - 1)]
    line_slots = hop_slots(chips, near_first)
    line_first = [sum(chips >> (k + 1) for k in range(j)) for j in range(len(near_first))]

    def line_copy(j, i):
        blocks = pl.ds(line_first[j], chips >> (j + 1))
        return remote(
            line_sent.at[i, blocks], line_got.at[i, blocks],
            line_send.at[i, j], line_recv.at[i, j], (near_first[j], 0, 0),
        )

    def line_held(h, upto, i, r):
        cols = slice(h * half, (h + 1) * half)
        value = held(h, bits, i, chip ^ r, 0)
        for j in range(upto):
            value += line_got[i, line_first[j] + line_slots[j].index(r), :, cols].astype(
                jnp.float32
            )
        return value

    def held(h, upto, i, z, r):
        cols = pl.ds(h * half, half)
        value = terms[i, z, side, fsdp ^ r, :, cols].astype(jnp.float32)
        value += core_got[i, z, fsdp ^ r, :, cols].astype(jnp.float32)
        for j in range(upto):
            value += hops[h][j][1][i, slots[h][j].index(r), z].astype(jnp.float32)
        return value

    slack = 3
    last = bits + 1 + slack * len(near_first)

    def step(t, carry):
        @pl.when(t < products)
        def _():
            per_left = products // lefts.shape[0]
            cols = pl.ds(pl.multiple_of(t * chunk, chunk), chunk)
            term = jnp.dot(
                lefts[t // per_left], right[:, cols], preferred_element_type=jnp.float32
            )
            terms[t] = term.astype(jnp.bfloat16).reshape(terms.shape[1:])

        if extras:
            @pl.when((t >= products) & (t < count))
            def _():
                terms[t] = extra[t - products].reshape(terms.shape[1:])

        @pl.when(t < count)
        def _():
            core_copy(t).start()

        for j in range(bits):
            @pl.when((t >= j + 1) & (t < count + j + 1))
            def _(j=j):
                i = t - (j + 1)
                if j == 0:
                    core_copy(i).wait_recv()
                for h in range(2):
                    if j:
                        hop_copy(h, j - 1, i).wait_recv()
                    for s, r in enumerate(slots[h][j]):
                        for z in range(chips):
                            hops[h][j][0][i, s, z] = held(h, j, i, z, r | orders[h][j]).astype(
                                jnp.bfloat16
                            )
                    hop_copy(h, j, i).start()

        for j in range(len(near_first)):
            lag = bits + 1 + slack * j

            @pl.when((t >= lag) & (t < count + lag))
            def _(j=j, lag=lag):
                i = t - lag
                if j:
                    line_copy(j - 1, i).wait_recv()
                for h in range(2):
                    if j == 0:
                        hop_copy(h, bits - 1, i).wait_recv()
                    for s, r in enumerate(line_slots[j]):
                        line_sent[i, line_first[j] + s, :, h * half : (h + 1) * half] = line_held(
                            h, j, i, r | near_first[j]
                        ).astype(jnp.bfloat16)
                line_copy(j, i).start()

        @pl.when(t >= last)
        def _():
            i = t - last
            line_copy(len(near_first) - 1, i).wait_recv()
            for h in range(2):
                value = line_held(h, len(near_first), i, 0)
                total[:, pl.ds(pl.multiple_of(i * chunk + h * half, half), half)] = value

        return carry

    lax.fori_loop(0, count + last, step, 0)

    def finish(i, carry):
        core_copy(i).wait_send()
        for h in range(2):
            for j in range(bits):
                hop_copy(h, j, i).wait_send()
        for j in range(len(near_first)):
            line_copy(j, i).wait_send()
        return carry

    lax.fori_loop(0, count, finish, 0)
    for copy in swapped:
        copy.wait()
    for step, copy in back:
        pl.when(ctx + step < ctx_size)(copy.wait_recv)
    for step, copy in back:
        pl.when(ctx - step >= 0)(copy.wait_send)


def reduce_rows(lefts, right, extra, halos, swaps, chunk, sizes, collective_id):
    ctx_size, fsdp_size = sizes
    chips = ctx_size // 2
    depth = lefts.shape[1]
    rows = depth // (ctx_size * fsdp_size)
    products = right.shape[1] // chunk
    extras = 0 if extra is None else extra.shape[0]
    if extra is None:
        extra = jnp.zeros((1, 16, LANES), jnp.bfloat16)
    count = products + extras
    bits = fsdp_size.bit_length() - 1
    half = chunk // 2
    reach = WINDOW // STRETCH
    buffers = []
    for _ in range(2):
        for j in range(bits):
            shape = (count, fsdp_size >> (j + 1), chips, rows, half)
            buffers += [pltpu.VMEM(shape, jnp.bfloat16)] * 2
    line = pltpu.VMEM((count, max(chips - 1, 1), rows, chunk), jnp.bfloat16)
    vmem = pl.BlockSpec(memory_space=pltpu.VMEM)
    hbm = pl.BlockSpec(memory_space=pl.ANY)
    return pl.pallas_call(
        functools.partial(reduce_kernel, sizes, chunk, products, extras, len(halos), len(swaps)),
        in_specs=[vmem] * 3 + [hbm] * (len(halos) + len(swaps)),
        out_specs=[vmem] + [hbm] * (len(halos) + len(swaps)),
        out_shape=[jax.ShapeDtypeStruct((rows, count * chunk), jnp.float32)]
        + [
            jax.ShapeDtypeStruct((reach, array.shape[0] // reach, array.shape[1]), array.dtype)
            for array in halos
        ]
        + [jax.ShapeDtypeStruct(array.shape, array.dtype) for array in swaps],
        scratch_shapes=[
            pltpu.VMEM((count, chips, 2, fsdp_size, rows, chunk), jnp.bfloat16),
            pltpu.VMEM((count, chips, fsdp_size, rows, chunk), jnp.bfloat16),
            line,
            line,
            pltpu.SemaphoreType.DMA((count,)),
            pltpu.SemaphoreType.DMA((count,)),
            pltpu.SemaphoreType.DMA((2, bits, count)),
            pltpu.SemaphoreType.DMA((2, bits, count)),
            pltpu.SemaphoreType.DMA((count, chips.bit_length() - 1)),
            pltpu.SemaphoreType.DMA((count, chips.bit_length() - 1)),
            pltpu.SemaphoreType.DMA((max(len(halos), 1), reach)),
            pltpu.SemaphoreType.DMA((max(len(halos), 1), reach)),
            pltpu.SemaphoreType.DMA((ctx_size,)),
            pltpu.SemaphoreType.DMA((ctx_size,)),
            pltpu.SemaphoreType.DMA,
        ]
        + buffers,
        compiler_params=pltpu.CompilerParams(
            collective_id=collective_id, has_side_effects=True, vmem_limit_bytes=56 * 1024 * 1024
        ),
        cost_estimate=pl.CostEstimate(flops=80_000_000_000, bytes_accessed=30_000_000, transcendentals=0),
    )(lefts, right, extra, *halos, *swaps)


def hidden_grad_kernel(
    sizes, normed, gate, up, hidden, cot, carried_in, pair_sum, down_terms, carried,
    terms, pair_sent, pair_got, pair_send, pair_recv
):
    ctx_size, fsdp_size = sizes
    count, span = terms.shape[1], normed.shape[1] // terms.shape[1]
    piece = max(LANES, hidden.shape[1] // count)
    masks = [1 << bit for bit in range(fsdp_size.bit_length() - 1)]
    orders = [masks, masks[::-1]]
    bits = len(masks)
    slots = [hop_slots(fsdp_size, order) for order in orders]
    fsdp = lax.axis_index("fsdp")
    greet([(0, 0, m) for m in masks])
    first = [sum(fsdp_size >> (k + 1) for k in range(j)) for j in range(bits)]

    def pair_copy(h, j, i):
        rows = pl.ds(first[j], fsdp_size >> (j + 1))
        return remote(
            pair_sent.at[h, i, rows], pair_got.at[h, i, rows],
            pair_send.at[h, j, i], pair_recv.at[h, j, i], (0, 0, orders[h][j]),
        )

    def pair_held(h, upto, i, r):
        value = terms[h, i, fsdp ^ r].astype(jnp.float32)
        for j in range(upto):
            value += pair_got[h, i, first[j] + slots[h][j].index(r)].astype(jnp.float32)
        return value

    def step(t, carry):
        @pl.when(t < count)
        def _():
            rows = pl.ds(pl.multiple_of(t * span, span), span)
            for h, grad in enumerate((gate, up)):
                term = across(normed[:, rows], grad[...])
                terms[h, t] = term.astype(jnp.bfloat16).reshape(terms.shape[2:])

        @pl.when(t < hidden.shape[1] // piece)
        def _():
            rows = pl.ds(pl.multiple_of(t * piece, piece), piece)
            down_terms[rows, :] = across(hidden[:, rows], cot[...]).astype(jnp.bfloat16)

        for j in range(bits):
            @pl.when((t >= j) & (t < count + j))
            def _(j=j):
                i = t - j
                for h in range(2):
                    if j:
                        pair_copy(h, j - 1, i).wait_recv()
                    for s, r in enumerate(slots[h][j]):
                        pair_sent[h, i, first[j] + s] = pair_held(
                            h, j, i, r | orders[h][j]
                        ).astype(jnp.bfloat16)
                    pair_copy(h, j, i).start()

        @pl.when(t >= bits)
        def _():
            i = t - bits
            for h in range(2):
                pair_copy(h, bits - 1, i).wait_recv()
                pair_sum[i, h] = pair_held(h, bits, i, 0).astype(jnp.bfloat16)

        return carry

    lax.fori_loop(0, count + bits, step, 0)

    def finish(i, carry):
        for h in range(2):
            for j in range(bits):
                pair_copy(h, j, i).wait_send()
        return carry

    lax.fori_loop(0, count, finish, 0)


def reduce_hidden(normed, gate, up, hidden, cot, carried, sizes):
    ctx_size, fsdp_size = sizes
    bits = fsdp_size.bit_length() - 1
    rows, columns = normed.shape[1] // (ctx_size * fsdp_size), gate.shape[1]
    pair = pltpu.VMEM((2, ctx_size, fsdp_size - 1, rows, columns), jnp.bfloat16)
    vmem = pl.BlockSpec(memory_space=pltpu.VMEM)
    hbm = pl.BlockSpec(memory_space=pl.ANY)
    return pl.pallas_call(
        functools.partial(hidden_grad_kernel, sizes),
        in_specs=[vmem] * 5 + [hbm],
        out_specs=[vmem, vmem, hbm],
        out_shape=[
            jax.ShapeDtypeStruct((ctx_size, 2, rows, columns), jnp.bfloat16),
            jax.ShapeDtypeStruct((hidden.shape[1], cot.shape[1]), jnp.bfloat16),
            jax.ShapeDtypeStruct(carried.shape, carried.dtype),
        ],
        input_output_aliases={5: 2},
        scratch_shapes=[
            pltpu.VMEM((2, ctx_size, fsdp_size, rows, columns), jnp.bfloat16), pair, pair,
        ]
        + [pltpu.SemaphoreType.DMA((2, bits, ctx_size))] * 2,
        compiler_params=pltpu.CompilerParams(
            collective_id=3, has_side_effects=True, vmem_limit_bytes=60 * 1024 * 1024
        ),
        cost_estimate=pl.CostEstimate(flops=60_000_000_000, bytes_accessed=30_000_000, transcendentals=0),
    )(normed, gate, up, hidden, cot, carried)


def norm_keys_kernel(stream, gain, weight, cosine, sine, normed_ref, pair_ref):
    x = stream[...].astype(jnp.float32)
    inverse = lax.rsqrt(jnp.mean(x * x, axis=1, keepdims=True) + EPS)
    normed = (x * inverse * gain[...]).astype(jnp.bfloat16)
    normed_ref[...] = normed
    front = product(normed, weight[...])
    kv_width = KV_HEADS * HEAD_DIM
    keys = turn(front[:, :kv_width], cosine[...], sine[...])
    pair_ref[:, :kv_width] = keys.astype(jnp.bfloat16)
    pair_ref[:, kv_width:] = front[:, kv_width : 2 * kv_width].astype(jnp.bfloat16)


def norm_keys(stream, gain, weight, cosine, sine):
    rows = stream.shape[0]
    return pl.pallas_call(
        norm_keys_kernel,
        out_shape=[
            jax.ShapeDtypeStruct(stream.shape, jnp.bfloat16),
            jax.ShapeDtypeStruct((rows, 2 * KV_HEADS * HEAD_DIM), jnp.bfloat16),
        ],
        compiler_params=pltpu.CompilerParams(vmem_limit_bytes=40 * 1024 * 1024),
        cost_estimate=pl.CostEstimate(
            flops=2 * rows * weight.size, bytes_accessed=8_000_000, transcendentals=0
        ),
    )(stream, gain, weight, cosine, sine)


def out_norm_kernel(mix, weight, stream, gain, resid, normed, total):
    i, steps = pl.program_id(0), pl.num_programs(0)
    span = weight.shape[1]
    cols = pl.ds(pl.multiple_of(i * span, span), span)
    total[:, cols] = stream[:, cols].astype(jnp.float32) + product(mix[...], weight[...])

    @pl.when(i == steps - 1)
    def _():
        h = total[...]
        resid[...] = h
        inverse = lax.rsqrt(jnp.mean(h * h, axis=1, keepdims=True) + EPS)
        normed[...] = (h * inverse * gain[...]).astype(jnp.bfloat16)


def out_norm(mix, weight, stream, gain):
    rows, width = mix.shape
    steps = 4
    whole = pl.BlockSpec((rows, width), lambda i: (0, 0))
    return pl.pallas_call(
        out_norm_kernel,
        grid=(steps,),
        in_specs=[
            whole,
            pl.BlockSpec((width, width // steps), lambda i: (0, i)),
            whole,
            pl.BlockSpec((1, width), lambda i: (0, 0)),
        ],
        out_specs=[whole, whole],
        out_shape=[
            jax.ShapeDtypeStruct((rows, width), jnp.float32),
            jax.ShapeDtypeStruct((rows, width), jnp.bfloat16),
        ],
        scratch_shapes=[pltpu.VMEM((rows, width), jnp.float32)],
        compiler_params=pltpu.CompilerParams(vmem_limit_bytes=40 * 1024 * 1024),
        cost_estimate=pl.CostEstimate(
            flops=2 * rows * width * width, bytes_accessed=14_000_000, transcendentals=0
        ),
    )(mix, weight, stream, gain)


def norm_back_kernel(
    columns, resid, gain, cot, weight, earlier, carried_in,
    grad_ref, low_ref, mix_ref, gain_ref, carried
):
    @pl.when(pl.program_id(0) == 0)
    def _():
        h = resid[...]
        inverse = lax.rsqrt(jnp.mean(h * h, axis=1, keepdims=True) + EPS)
        normal = h * inverse
        slope = columns[...].astype(jnp.float32)
        gain_ref[...] = jnp.sum(slope * normal, axis=0, keepdims=True)
        grad = cot[...].astype(jnp.float32) + norm_back(slope * gain[...], normal, inverse)
        grad_ref[...] = grad
        low_ref[...] = grad.astype(jnp.bfloat16)

    mix_ref[...] = against(low_ref[...], weight[...]).astype(jnp.bfloat16)


def norm_back_mix(columns, resid, gain, cot, weight, earlier, carried):
    rows, width = resid.shape
    steps = 4
    whole = pl.BlockSpec((rows, width), lambda i: (0, 0))
    line = pl.BlockSpec((1, width), lambda i: (0, 0))
    return pl.pallas_call(
        norm_back_kernel,
        grid=(steps,),
        in_specs=[
            whole, whole, line, whole,
            pl.BlockSpec((width // steps, width), lambda i: (i, 0)),
            pl.BlockSpec(memory_space=pl.ANY),
            pl.BlockSpec(memory_space=pl.ANY),
        ],
        out_specs=[
            whole, whole,
            pl.BlockSpec((rows, width // steps), lambda i: (0, i)),
            line,
            pl.BlockSpec(memory_space=pl.ANY),
        ],
        out_shape=[
            jax.ShapeDtypeStruct((rows, width), jnp.float32),
            jax.ShapeDtypeStruct((rows, width), jnp.bfloat16),
            jax.ShapeDtypeStruct((rows, width), jnp.bfloat16),
            jax.ShapeDtypeStruct((1, width), jnp.float32),
            jax.ShapeDtypeStruct(carried.shape, carried.dtype),
        ],
        input_output_aliases={6: 4},
        compiler_params=pltpu.CompilerParams(vmem_limit_bytes=40 * 1024 * 1024),
        cost_estimate=pl.CostEstimate(
            flops=2 * rows * width * width, bytes_accessed=16_000_000, transcendentals=0
        ),
    )(columns, resid, gain, cot, weight, earlier, carried)


def input_grad_kernel(
    dk_own, dv_own, dk_got, dv_got, cosine, sine, dq, query_weight, kv_weight, stream, gain, resid_grad,
    kv_ref, gain_ref, grad_ref, total
):
    i, steps = pl.program_id(0), pl.num_programs(0)
    span = query_weight.shape[0]
    kv_width = dk_own.shape[1]

    @pl.when(i == 0)
    def _():
        ctx, size = lax.axis_index("ctx"), lax.axis_size("ctx")
        dk, dv = dk_own[...], dv_own[...]
        for step in range(1, dk_got.shape[0] + 1):
            there = ctx + step < size
            dk += jnp.where(there, dk_got[step - 1].astype(jnp.float32), 0.0)
            dv += jnp.where(there, dv_got[step - 1].astype(jnp.float32), 0.0)
        kv_ref[:, :kv_width] = turn(dk, cosine[...], -sine[...]).astype(jnp.bfloat16)
        kv_ref[:, kv_width:] = dv.astype(jnp.bfloat16)

    cols = pl.ds(pl.multiple_of(i * span, span), span)
    total[:, cols] = against(dq[...], query_weight[...]) + against(
        kv_ref[...], kv_weight[:, : 2 * kv_width]
    )

    @pl.when(i == steps - 1)
    def _():
        x = stream[...].astype(jnp.float32)
        inverse = lax.rsqrt(jnp.mean(x * x, axis=1, keepdims=True) + EPS)
        normal = x * inverse
        slope = total[...]
        gain_ref[...] = jnp.sum(slope * normal, axis=0, keepdims=True)
        grad = resid_grad[...] + norm_back(slope * gain[...], normal, inverse)
        grad_ref[...] = grad.astype(jnp.bfloat16)


def input_grad(dk_own, dv_own, dk_got, dv_got, cosine, sine, dq, query_weight, kv_weight, stream, gain, resid_grad):
    rows, width = stream.shape
    steps = 4
    span = width // steps

    def whole(array):
        return pl.BlockSpec(array.shape, lambda i: (0,) * array.ndim)

    def strip(array):
        return pl.BlockSpec((span, array.shape[1]), lambda i: (i, 0))

    kept = (dk_own, dv_own, dk_got, dv_got, cosine, sine, dq)
    kv_shape = (rows, 2 * dk_own.shape[1])
    return pl.pallas_call(
        input_grad_kernel,
        grid=(steps,),
        in_specs=[whole(array) for array in kept]
        + [strip(query_weight), strip(kv_weight)]
        + [whole(array) for array in (stream, gain, resid_grad)],
        out_specs=[
            pl.BlockSpec(kv_shape, lambda i: (0, 0)),
            pl.BlockSpec((1, width), lambda i: (0, 0)),
            pl.BlockSpec((rows, width), lambda i: (0, 0)),
        ],
        out_shape=[
            jax.ShapeDtypeStruct(kv_shape, jnp.bfloat16),
            jax.ShapeDtypeStruct((1, width), jnp.float32),
            jax.ShapeDtypeStruct((rows, width), jnp.bfloat16),
        ],
        scratch_shapes=[pltpu.VMEM((rows, width), jnp.float32)],
        compiler_params=pltpu.CompilerParams(vmem_limit_bytes=48 * 1024 * 1024),
        cost_estimate=pl.CostEstimate(
            flops=3 * rows * width * width, bytes_accessed=24_000_000, transcendentals=0
        ),
    )(*kept, query_weight, kv_weight, stream, gain, resid_grad)


def hidden_layer_kernel(
    normed, cot, gate_weight, up_weight, down_weight,
    hidden_ref, dgate_ref, dup_ref, down_ref, columns_ref
):
    x = normed[...]
    gate = product(x, gate_weight[...])
    up = product(x, up_weight[...])
    grad = against(cot[...], down_weight[...])
    sigmoid = jax.nn.sigmoid(gate)
    silu = gate * sigmoid
    hidden = (silu * up).astype(jnp.bfloat16)
    dgate = (grad * up * sigmoid * (1.0 + gate * (1.0 - sigmoid))).astype(jnp.bfloat16)
    dup = (grad * silu).astype(jnp.bfloat16)
    hidden_ref[...] = hidden
    dgate_ref[...] = dgate
    dup_ref[...] = dup
    columns = against(dgate, gate_weight[...]) + against(dup, up_weight[...])
    columns_ref[...] = columns.astype(jnp.bfloat16)
    down_ref[...] = product(hidden, down_weight[...]).astype(jnp.bfloat16)


def hidden_layer(normed, cot, pair, down_weight):
    tokens, width = normed.shape
    share = pair.shape[2]
    tile = min(256, tokens)
    wide = pl.BlockSpec((tile, width), lambda i: (i, 0))
    thin = pl.BlockSpec((tile, share), lambda i: (i, 0))
    once = pl.Buffered(buffer_count=1)
    weights = [
        pl.BlockSpec((None,) + pair.shape[1:], lambda i, n=n: (n, 0, 0), pipeline_mode=once)
        for n in range(2)
    ]
    down = pl.BlockSpec(down_weight.shape, lambda i: (0, 0), pipeline_mode=once)
    thin_out = jax.ShapeDtypeStruct((tokens, share), jnp.bfloat16)
    wide_out = jax.ShapeDtypeStruct((tokens, width), jnp.bfloat16)
    return pl.pallas_call(
        hidden_layer_kernel,
        grid=(tokens // tile,),
        in_specs=[wide, wide] + weights + [down],
        out_specs=[thin, thin, thin, wide, wide],
        out_shape=[thin_out] * 3 + [wide_out] * 2,
        compiler_params=pltpu.CompilerParams(vmem_limit_bytes=56 * 1024 * 1024),
        cost_estimate=pl.CostEstimate(
            flops=16 * tokens * width * share, bytes_accessed=30_000_000, transcendentals=0
        ),
    )(normed, cot, pair, pair, down_weight)


def local(
    tokens,
    cotangent,
    lengths,
    attn_gain,
    query_weight,
    key_weight,
    value_weight,
    out_weight,
    mlp_gain,
    gate_weight,
    up_weight,
    down_weight,
):
    both = ("ctx", "fsdp")
    ctx_size = lax.axis_size("ctx")
    fsdp_size = lax.axis_size("fsdp")
    chips = ctx_size // 2
    stream = tokens[0].astype(jnp.float32)
    tok_rows = stream.shape[0]
    own_rows = query_weight.shape[0]
    kv_width = KV_HEADS * HEAD_DIM
    ff_own = FF // ctx_size
    reach_blocks = WINDOW // STRETCH
    ctx_place = lax.axis_index("ctx")
    doc_lengths = lengths[0]
    query_index = ctx_place * tok_rows + jnp.arange(tok_rows, dtype=jnp.int32)
    key_index = (ctx_place - reach_blocks) * tok_rows + jnp.arange(
        (reach_blocks + 1) * tok_rows, dtype=jnp.int32
    )
    query_doc = doc_segment(doc_lengths, query_index)
    key_doc = doc_segment(doc_lengths, key_index)
    position = doc_position(doc_lengths, query_index, query_doc)
    visible = (key_index[:, None] >= 0) & (key_index[:, None] <= query_index[None, :])
    visible = (
        visible
        & (query_index[None, :] - key_index[:, None] < WINDOW)
        & (query_doc[None, :] == key_doc[:, None])
    )
    bias = jnp.where(visible, 0.0, -1e30).astype(jnp.float32)
    cosine, sine = turn_tables(position)

    sizes = (ctx_size, fsdp_size)
    gains = jnp.zeros((own_rows, LANES), jnp.bfloat16)
    gains = gains.at[:, 0].set(attn_gain).at[:, 1].set(mlp_gain)
    (kv_all,) = gather_front(
        (jnp.concatenate([key_weight, value_weight, gains], axis=1),), None, None, None, None, sizes, 1
    )
    kv_all = kv_all.reshape(D, -1)
    gain_one = kv_all[:, 2 * kv_width].astype(jnp.float32)
    gain_two = kv_all[:, 2 * kv_width + 1].astype(jnp.float32)

    inv_one = lax.rsqrt(jnp.mean(stream * stream, axis=1, keepdims=True) + EPS)
    normal_one = stream * inv_one
    normed_one, own_pair = norm_keys(tokens[0], gain_one[None], kv_all, cosine, sine)
    query_all, out_all, pair_all, down_own, window, cot_own = gather_front(
        (query_weight, out_weight), jnp.stack([gate_weight, up_weight]), down_weight,
        cotangent[0], own_pair, sizes, 6,
    )
    cot_all = lax.all_gather(cot_own, "ctx", axis=0, tiled=True)
    query_all = query_all.reshape(D, D)
    out_all = out_all.reshape(D, D)
    down_own = down_own.reshape(ff_own, D)
    window = window.reshape(-1, 2 * kv_width)
    key_window, value_window = window[:, :kv_width], window[:, kv_width:]
    attn_mix, query_low, log_total = attend_forward(
        normed_one, query_all, key_window, value_window, bias, cosine, sine
    )
    resid, normed_two = out_norm(attn_mix, out_all, tokens[0], gain_two[None])
    pair, normed_all = gather_hidden(pair_all, normed_two, sizes)
    pair = pair.reshape(2, D, ff_own)
    normed_all = normed_all.reshape(ctx_size * tok_rows, D)
    hidden, grad_gate_low, grad_up_low, down_part, columns = hidden_layer(
        normed_all, cot_all, pair, down_own
    )
    columns = lax.psum_scatter(columns, "ctx", scatter_dimension=0, tiled=True)
    pair_sum, down_terms, down_part = reduce_hidden(
        normed_all, grad_gate_low, grad_up_low, hidden, cot_all, down_part, sizes
    )
    grad_resid, grad_resid_low, grad_mix_low, mlp_gain_local, down_terms = norm_back_mix(
        columns, resid, gain_two[None], cotangent[0], out_all, pair_sum, down_terms
    )
    down_sum = lax.psum_scatter(down_part, "ctx", scatter_dimension=0, tiled=True)
    grad_query_low, dk_low, dv_low, dk_own, dv_own, down_terms = attend_backward(
        query_low, key_window, value_window, grad_mix_low, attn_mix, log_total, bias, cosine, sine,
        down_terms,
    )
    grad_down = lax.psum_scatter(down_terms, "fsdp", scatter_dimension=0, tiled=True)
    wide_grad, dk_got, dv_got = reduce_rows(
        jnp.stack([normed_one.T, attn_mix.T]),
        jnp.concatenate([grad_query_low, grad_resid_low], axis=1),
        None, (dk_low, dv_low), (), 4 * LANES, sizes, 4,
    )
    kv_low, attn_gain_local, grad_input = input_grad(
        dk_own, dv_own, dk_got, dv_got, cosine, sine, grad_query_low, query_all, kv_all,
        tokens[0], gain_one[None], grad_resid,
    )
    gain_terms = jnp.stack([attn_gain_local[0], mlp_gain_local[0]], axis=1).astype(jnp.bfloat16)
    gain_terms = jnp.pad(gain_terms, ((0, 0), (0, 2 * LANES - 2)))[None]
    kv_grad, pair_sum = reduce_rows(
        normed_one.T[None], kv_low, gain_terms, (), (pair_sum,), 2 * LANES, sizes, 5
    )
    mixed = after(resid, kv_grad) + after(down_sum, kv_grad).astype(jnp.float32)
    mixed = mixed.astype(jnp.bfloat16)
    pair_sum = pair_sum.transpose(1, 2, 0, 3).reshape(2, own_rows, FF).astype(jnp.float32)
    return (
        mixed[None],
        grad_input[None],
        kv_grad[:, 2 * kv_width],
        wide_grad[:, :D],
        kv_grad[:, :kv_width],
        kv_grad[:, kv_width : 2 * kv_width],
        wide_grad[:, D:],
        kv_grad[:, 2 * kv_width + 1],
        pair_sum[0],
        pair_sum[1],
        grad_down.astype(jnp.float32),
    )


def solution(mesh):
    in_specs = (
        P("fsdp", "ctx", None),
        P("fsdp", "ctx", None),
        P("fsdp", None),
        P(("ctx", "fsdp")),
        P(("ctx", "fsdp"), None),
        P(("ctx", "fsdp"), None),
        P(("ctx", "fsdp"), None),
        P(("ctx", "fsdp"), None),
        P(("ctx", "fsdp")),
        P(("ctx", "fsdp"), None),
        P(("ctx", "fsdp"), None),
        P(("ctx", "fsdp"), None),
    )
    out_specs = (
        P("fsdp", "ctx", None),
        P("fsdp", "ctx", None),
        P(("ctx", "fsdp")),
        P(("ctx", "fsdp"), None),
        P(("ctx", "fsdp"), None),
        P(("ctx", "fsdp"), None),
        P(("ctx", "fsdp"), None),
        P(("ctx", "fsdp")),
        P(("ctx", "fsdp"), None),
        P(("ctx", "fsdp"), None),
        P(("ctx", "fsdp"), None),
    )
    return jax.shard_map(local, mesh=mesh, in_specs=in_specs, out_specs=out_specs, check_vma=False)
```

```python
import functools

import jax
import jax.numpy as jnp
from jax import lax
from jax.experimental import pallas as pl
from jax.experimental.pallas import tpu as pltpu
from jax.sharding import PartitionSpec as P

D = 2048
FF = 8192
HEADS = 32
KV_HEADS = 8
HEAD_DIM = 64
WINDOW = 1024
STRETCH = 256
QTILE = 128
LANES = 128
EPS = 1e-05
THETA = 500000.0


def passed_along(x, axis, by):
    size = lax.axis_size(axis)
    pairs = [(i, i + by) for i in range(size) if 0 <= i + by < size]
    return lax.ppermute(x, axis, pairs)


def product(left, right):
    return jnp.dot(left, right, preferred_element_type=jnp.float32)


def against(left, right):
    return lax.dot_general(
        left, right, (((1,), (1,)), ((), ())), preferred_element_type=jnp.float32
    )


def across(left, right):
    return lax.dot_general(
        left, right, (((0,), (0,)), ((), ())), preferred_element_type=jnp.float32
    )


def doc_segment(doc_lengths, index):
    doc_ends = jnp.cumsum(doc_lengths)
    return jnp.sum((index[:, None] >= doc_ends[None, :]).astype(jnp.int32), axis=1)


def doc_position(doc_lengths, index, segment):
    doc_ends = jnp.cumsum(doc_lengths)
    doc_starts = doc_ends - doc_lengths
    member = segment[:, None] == jnp.arange(doc_lengths.shape[0], dtype=jnp.int32)[None, :]
    return index - jnp.sum(jnp.where(member, doc_starts[None, :], 0), axis=1)


def swap_halves(u):
    half = HEAD_DIM // 2
    width = u.shape[1]
    lane = lax.broadcasted_iota(jnp.int32, u.shape, 1)
    ahead = pltpu.roll(u, width - half, 1)
    behind = pltpu.roll(u, half, 1)
    return jnp.where(lane % HEAD_DIM < half, ahead, behind)


def turn(u, cosine, sine):
    copies = u.shape[1] // cosine.shape[1]
    cosine = jnp.concatenate([cosine] * copies, axis=1)
    sine = jnp.concatenate([sine] * copies, axis=1)
    return u * cosine + swap_halves(u) * sine


def nt(left, right):
    return lax.dot_general(left, right, (((1,), (1,)), ((), ())), preferred_element_type=jnp.float32)


def nn(left, right):
    return lax.dot_general(left, right, (((1,), (0,)), ((), ())), preferred_element_type=jnp.float32)


def attend_forward_kernel(
    n_ref, w_ref, k_ref, v_ref, bias_ref, cos_ref, sin_ref, o_ref, qr_ref, lse_ref
):
    rows = n_ref.shape[0]
    group = HEADS // KV_HEADS
    span = k_ref.shape[0] - rows + QTILE
    rotated = turn(product(n_ref[...], w_ref[...]), cos_ref[...], sin_ref[...])
    qr_ref[...] = rotated.astype(jnp.bfloat16)
    scaled = (qr_ref[...].astype(jnp.float32) * HEAD_DIM ** (-0.5)).astype(jnp.bfloat16)
    for tile in range(rows // QTILE):
        first = tile * QTILE
        bias = bias_ref[first : first + span, first : first + QTILE]
        for kv in range(LANES // HEAD_DIM):
            lo = kv * HEAD_DIM
            keys = k_ref[first : first + span, lo : lo + HEAD_DIM]
            values = v_ref[first : first + span, lo : lo + HEAD_DIM]
            values_t = values.T
            raises, totals = [], []
            for h in range(group):
                head = kv * group + h
                q_h = scaled[first : first + QTILE, head * HEAD_DIM : (head + 1) * HEAD_DIM]
                s = nt(keys, q_h) + bias
                top = jnp.max(s, axis=0, keepdims=True)
                raised = jnp.exp(s - top)
                total = jnp.sum(raised, axis=0, keepdims=True)
                lse_ref[head : head + 1, first : first + QTILE] = top + jnp.log(total)
                raises.append(raised.astype(jnp.bfloat16))
                totals.append(total)
            o_wide = nn(values_t, jnp.concatenate(raises, axis=1)) / jnp.concatenate(totals, axis=1)
            o_t = jnp.concatenate(
                [o_wide[:, h * QTILE : (h + 1) * QTILE] for h in range(group)], axis=0
            )
            o_ref[first : first + QTILE, kv * group * HEAD_DIM : (kv + 1) * group * HEAD_DIM] = (
                o_t.T.astype(jnp.bfloat16)
            )


def attend_forward(normed, weight, k, v, bias, cosine, sine):
    rows, width = normed.shape[0], weight.shape[1]
    steps = KV_HEADS * HEAD_DIM // LANES
    qw = width // steps
    heads = HEADS // steps
    window = k.shape[0]
    return pl.pallas_call(
        attend_forward_kernel,
        grid=(steps,),
        in_specs=[
            pl.BlockSpec(normed.shape, lambda i: (0, 0)),
            pl.BlockSpec((weight.shape[0], qw), lambda i: (0, i)),
            pl.BlockSpec((window, LANES), lambda i: (0, i)),
            pl.BlockSpec((window, LANES), lambda i: (0, i)),
            pl.BlockSpec((window, rows), lambda i: (0, 0)),
            pl.BlockSpec((rows, LANES), lambda i: (0, 0)),
            pl.BlockSpec((rows, LANES), lambda i: (0, 0)),
        ],
        out_specs=[
            pl.BlockSpec((rows, qw), lambda i: (0, i)),
            pl.BlockSpec((rows, qw), lambda i: (0, i)),
            pl.BlockSpec((heads, rows), lambda i: (i, 0)),
        ],
        out_shape=[
            jax.ShapeDtypeStruct((rows, width), jnp.bfloat16),
            jax.ShapeDtypeStruct((rows, width), jnp.bfloat16),
            jax.ShapeDtypeStruct((HEADS, rows), jnp.float32),
        ],
        compiler_params=pltpu.CompilerParams(vmem_limit_bytes=48 * 1024 * 1024),
        cost_estimate=pl.CostEstimate(flops=40_000_000_000, bytes_accessed=10_000_000, transcendentals=0),
    )(normed, weight, k, v, bias, cosine, sine)


def attend_backward_kernel(
    qr_ref, k_ref, v_ref, do_ref, o_ref, lse_ref, bias_ref, cos_ref, sin_ref,
    carried_in, dq_ref, dk_low, dv_low, dk_own, dv_own, carried, dk_ref, dv_ref
):
    rows = qr_ref.shape[0]
    group = HEADS // KV_HEADS
    span = k_ref.shape[0] - rows + QTILE
    scale = HEAD_DIM ** (-0.5)
    dk_ref[...] = jnp.zeros_like(dk_ref)
    dv_ref[...] = jnp.zeros_like(dv_ref)
    scaled = (qr_ref[...].astype(jnp.float32) * scale).astype(jnp.bfloat16)
    wide = LANES // HEAD_DIM * group * HEAD_DIM
    owner = lax.broadcasted_iota(jnp.int32, (8, wide), 1) // HEAD_DIM
    pick = (owner == lax.broadcasted_iota(jnp.int32, (8, wide), 0)).astype(jnp.float32)
    for tile in range(rows // QTILE):
        first = tile * QTILE
        bias = bias_ref[first : first + span, first : first + QTILE]
        both = do_ref[first : first + QTILE, :].astype(jnp.float32) * o_ref[
            first : first + QTILE, :
        ].astype(jnp.float32)
        delta = lax.dot_general(
            pick, both, (((1,), (1,)), ((), ())),
            precision=lax.Precision.HIGHEST, preferred_element_type=jnp.float32,
        )
        dk_pair, dv_pair, dqs = [], [], []
        for kv in range(LANES // HEAD_DIM):
            lo = kv * HEAD_DIM
            keys = k_ref[first : first + span, lo : lo + HEAD_DIM]
            values = v_ref[first : first + span, lo : lo + HEAD_DIM]
            keys_t = keys.T
            probs, slopes, qs, dos = [], [], [], []
            for h in range(group):
                head = kv * group + h
                cols = slice(head * HEAD_DIM, (head + 1) * HEAD_DIM)
                q_h = scaled[first : first + QTILE, cols]
                do_h = do_ref[first : first + QTILE, cols]
                s = nt(keys, q_h) + bias
                p = jnp.exp(s - lse_ref[head : head + 1, first : first + QTILE])
                dp = nt(values, do_h)
                ds = (p * (dp - delta[head : head + 1, :])).astype(jnp.bfloat16)
                probs.append(p.astype(jnp.bfloat16))
                slopes.append(ds)
                qs.append(q_h)
                dos.append(do_h)
            p_all = jnp.concatenate(probs, axis=1)
            ds_all = jnp.concatenate(slopes, axis=1)
            dv_pair.append(nn(p_all, jnp.concatenate(dos, axis=0)))
            dk_pair.append(nn(ds_all, jnp.concatenate(qs, axis=0)))
            dq_t = nn(keys_t, ds_all) * scale
            dqs.extend(dq_t[:, h * QTILE : (h + 1) * QTILE] for h in range(group))
        dk_ref[first : first + span, :] += jnp.concatenate(dk_pair, axis=1)
        dv_ref[first : first + span, :] += jnp.concatenate(dv_pair, axis=1)
        dq = jnp.concatenate(dqs, axis=0).T
        dq_ref[first : first + QTILE, :] = turn(
            dq, cos_ref[first : first + QTILE, :], -sin_ref[first : first + QTILE, :]
        ).astype(jnp.bfloat16)
    before = dk_low.shape[0]
    dk_low[...] = dk_ref[:before, :].astype(jnp.bfloat16)
    dv_low[...] = dv_ref[:before, :].astype(jnp.bfloat16)
    dk_own[...] = dk_ref[before:, :]
    dv_own[...] = dv_ref[before:, :]


def attend_backward(qr, k, v, do, o, lse, bias, cosine, sine, carried):
    rows, width = qr.shape
    steps = KV_HEADS * HEAD_DIM // LANES
    qw = width // steps
    heads = HEADS // steps
    window = k.shape[0]
    wide = pl.BlockSpec((rows, qw), lambda i: (0, i))
    tall = pl.BlockSpec((window, LANES), lambda i: (0, i))
    table = pl.BlockSpec((rows, LANES), lambda i: (0, 0))
    return pl.pallas_call(
        attend_backward_kernel,
        grid=(steps,),
        in_specs=[
            wide, tall, tall, wide, wide,
            pl.BlockSpec((heads, rows), lambda i: (i, 0)),
            pl.BlockSpec((window, rows), lambda i: (0, 0)),
            table, table,
            pl.BlockSpec(memory_space=pl.ANY),
        ],
        out_specs=[
            wide,
            pl.BlockSpec((window - rows, LANES), lambda i: (0, i)),
            pl.BlockSpec((window - rows, LANES), lambda i: (0, i)),
            pl.BlockSpec((rows, LANES), lambda i: (0, i)),
            pl.BlockSpec((rows, LANES), lambda i: (0, i)),
            pl.BlockSpec(memory_space=pl.ANY),
        ],
        out_shape=[
            jax.ShapeDtypeStruct((rows, width), jnp.bfloat16),
            jax.ShapeDtypeStruct((window - rows, k.shape[1]), jnp.bfloat16),
            jax.ShapeDtypeStruct((window - rows, k.shape[1]), jnp.bfloat16),
            jax.ShapeDtypeStruct((rows, k.shape[1]), jnp.float32),
            jax.ShapeDtypeStruct((rows, k.shape[1]), jnp.float32),
            jax.ShapeDtypeStruct(carried.shape, carried.dtype),
        ],
        input_output_aliases={9: 5},
        scratch_shapes=[pltpu.VMEM((window, LANES), jnp.float32)] * 2,
        compiler_params=pltpu.CompilerParams(vmem_limit_bytes=48 * 1024 * 1024),
        cost_estimate=pl.CostEstimate(flops=80_000_000_000, bytes_accessed=20_000_000, transcendentals=0),
    )(qr, k, v, do, o, lse, bias, cosine, sine, carried)


def turn_tables(position):
    half_dim = HEAD_DIM // 2
    frequency = THETA ** (-2.0 * jnp.arange(half_dim, dtype=jnp.float32) / HEAD_DIM)
    angles = position.astype(jnp.float32)[:, None] * frequency[None, :]
    cosine, sine = jnp.cos(angles), jnp.sin(angles)
    copies = LANES // HEAD_DIM
    return (
        jnp.concatenate([cosine, cosine] * copies, axis=1),
        jnp.concatenate([-sine, sine] * copies, axis=1),
    )


def rope(u, cosine, sine):
    half = HEAD_DIM // 2
    parts = u.reshape(u.shape[0], -1, 2, half)
    swapped_parts = parts[:, :, ::-1, :].reshape(u.shape)
    copies = u.shape[1] // LANES
    return u * jnp.tile(cosine, (1, copies)) + swapped_parts * jnp.tile(sine, (1, copies))


def norm_back(grad_normal, normal, inverse):
    return inverse * (grad_normal - normal * jnp.mean(grad_normal * normal, axis=1, keepdims=True))


def after(x, *others):
    return lax.optimization_barrier((x,) + others)[0]


def peer_of(chip_mask, side_mask, fsdp_mask):
    ctx = lax.axis_index("ctx")
    return (ctx ^ (2 * chip_mask + side_mask), lax.axis_index("fsdp") ^ fsdp_mask)


def greet(peers):
    barrier = pltpu.get_barrier_semaphore()
    for peer in peers:
        pl.semaphore_signal(
            barrier, inc=1, device_id=peer_of(*peer), device_id_type=pl.DeviceIdType.MESH
        )
    pl.semaphore_wait(barrier, len(peers))


def run_copies(copies, send_sems, recv_sems):
    started, arrived = {}, set()

    def arrive(name):
        if name not in arrived:
            arrived.add(name)
            started[name].wait_recv()

    for copy in copies:
        if callable(copy):
            copy()
            continue
        at = len(started)
        name, awaited, source, target, peer = copy
        for other in awaited:
            arrive(other)
        started[name] = pltpu.make_async_remote_copy(
            src_ref=source,
            dst_ref=target,
            send_sem=send_sems.at[at],
            recv_sem=recv_sems.at[at],
            device_id=peer_of(*peer),
            device_id_type=pl.DeviceIdType.MESH,
        )
        started[name].start()
    for name in started:
        arrive(name)
    for name in started:
        started[name].wait_send()


def doubling(name, size, order, awaited, block, target, along=2):
    hops, held = [], {0: awaited}
    for mask in order:
        hop, got = [], {}
        for r, needs in held.items():
            key = (name, r, mask)
            peer = tuple(mask if place == along else 0 for place in range(3))
            hop.append((key, needs, block(r), target(r), peer))
            got[r ^ mask] = (key,)
        held.update(got)
        hops.append(hop)
    return hops, held


def line_gather(name, own, whole, sizes):
    chips = sizes[0] // 2
    ctx = lax.axis_index("ctx")
    chip, side = ctx // 2, ctx % 2
    far_first = [1 << bit for bit in range(chips.bit_length() - 1)][::-1]
    target = lambda r: whole.at[chip ^ r, side]
    block = lambda r: target(r) if r else own
    hops, held = doubling((name, "z"), chips, far_first, (), block, target, 0)
    last = [
        ((name, "core", r), held[r], block(r), target(r), (0, 1, 0)) for r in range(chips)
    ]
    return hops + [last]


def front_masks(ctx_size, fsdp_size, paired):
    chips = ctx_size // 2
    peers = [
        (m, s, 0)
        for m in range(chips)
        for s in range(2)
        if (m or s) and (paired or m + s == 1 or (not s and not m & (m - 1)))
    ]
    return peers + [(0, 0, m) for m in range(1, fsdp_size)]


def front_copies(parts, wholes, pair_ref, pair_all, down_ref, down_all, sizes):
    ctx_size, fsdp_size = sizes
    chips = ctx_size // 2
    ctx, fsdp = lax.axis_index("ctx"), lax.axis_index("fsdp")
    chip, side = ctx // 2, ctx % 2
    masks = [1 << bit for bit in range(fsdp_size.bit_length() - 1)]
    orders = [masks, masks[::-1]]
    far_first = [1 << bit for bit in range(chips.bit_length() - 1)][::-1]
    copies, arrival = [], {}
    lines = []
    for n, (own, whole) in enumerate(zip(parts, wholes)):
        view = lambda r, own=own, whole=whole: (
            whole.at[chip ^ r, side, fsdp] if r else own
        )
        target = lambda r, whole=whole: whole.at[chip ^ r, side, fsdp]
        hops, held = doubling(("z", n), chips, far_first, (), view, target, 0)
        lines.append(hops)
        for r, keys in held.items():
            arrival[n, r] = keys
    for hop in zip(*lines):
        for pieces in hop:
            copies.extend(pieces)
    exchange = []
    if pair_ref is not None:
        ff_own = pair_ref.shape[2] // ctx_size
        for m in range(chips):
            for s in range(2):
                if m or s:
                    other = ctx ^ (2 * m + s)
                    columns = pl.ds(pl.multiple_of(other * ff_own, ff_own), ff_own)
                    exchange.append(
                        (
                            ("pair", m, s), (), pair_ref.at[:, :, columns],
                            pair_all.at[:, ctx, fsdp], (m, s, 0),
                        )
                    )
    queues = []
    if down_ref is not None:
        width = down_ref.shape[1] // 2
        lists = []
        for h, order in enumerate(orders):
            cols = pl.ds(h * width, width)
            target = lambda r, cols=cols: down_all.at[fsdp ^ r, :, cols]
            block = lambda r, cols=cols: (
                down_all.at[fsdp ^ r, :, cols] if r else down_ref.at[:, cols]
            )
            lists.append(doubling(("down", h), fsdp_size, order, (), block, target)[0])
        stages = [[copy for pieces in zip(*hop) for copy in pieces] for hop in zip(*lists)]
        queues.append(stages + [[]])
    for n, (own, whole) in enumerate(zip(parts, wholes)):
        width = own.shape[1]
        cut = (width // 2 + LANES - 1) // LANES * LANES
        halves = [(0, cut), (cut, width - cut)]
        for m in range(chips):
            first = arrival[n, m]
            lists, last = [], []
            for h, ((lo, span), order) in enumerate(zip(halves, orders)):
                cols = pl.ds(lo, span)

                def block(r, m=m, cols=cols, own=own, whole=whole):
                    if m == 0 and r == 0:
                        return own.at[:, cols]
                    return whole.at[chip ^ m, side, fsdp ^ r, :, cols]

                def target(r, m=m, cols=cols, whole=whole):
                    return whole.at[chip ^ m, side, fsdp ^ r, :, cols]

                hops, held = doubling(("f", n, m, h), fsdp_size, order, first, block, target)
                lists.append(hops)
                last.extend(key for keys in held.values() for key in keys)
            stages = [[copy for pieces in zip(*hop) for copy in pieces] for hop in zip(*lists)]
            row = whole.at[chip ^ m, side]
            if m:
                stages.append([(("core", n, m), tuple(last), row, row, (0, 1, 0))])
            else:
                stages.append(
                    [
                        (
                            ("core", n, m, r), tuple(last),
                            row.at[fsdp ^ r] if r else own, row.at[fsdp ^ r], (0, 1, 0),
                        )
                        for r in range(fsdp_size)
                    ]
                )
            queues.append(stages)
    sharing = []
    lag = 2
    for turn in range(len(queues) + lag * (len(orders[0]) + 1)):
        for stage in range(len(orders[0]) + 1):
            at = turn - lag * stage
            if 0 <= at < len(queues):
                sharing.extend(queues[at][stage])
        if turn == chips:
            sharing.extend(exchange)
    return copies, sharing


def front_kernel(sizes, count, paired, *refs):
    parts, refs = refs[:count], refs[count:]
    if paired:
        pair_ref, down_ref, kv_ref, zero_ref, cot_in, *refs = refs
    else:
        pair_ref = down_ref = None
    wholes, refs = refs[:count], refs[count:]
    if paired:
        pair_all, down_all, window, cot_out, *refs = refs
    else:
        pair_all = down_all = None
    send_sems, recv_sems, own_sems, halo_send, halo_recv = refs
    greet(front_masks(*sizes, paired))
    ctx, fsdp = lax.axis_index("ctx"), lax.axis_index("fsdp")
    reach = halo_send.shape[0]
    halos = []
    if paired:
        for step in range(1, reach + 1):
            copy = pltpu.make_async_remote_copy(
                src_ref=kv_ref,
                dst_ref=window.at[reach - step],
                send_sem=halo_send.at[step - 1],
                recv_sem=halo_recv.at[step - 1],
                device_id=(lax.rem(ctx + step, sizes[0]), fsdp),
                device_id_type=pl.DeviceIdType.MESH,
            )
            halos.append((step, copy))
    kept = []
    for n, (own, whole) in enumerate(zip(parts, wholes)):
        kept.append(
            pltpu.make_async_copy(own, whole.at[ctx // 2, ctx % 2, fsdp], own_sems.at[n])
        )
    empty = []
    if paired:
        ff_own = pair_ref.shape[2] // sizes[0]
        columns = pl.ds(pl.multiple_of(ctx * ff_own, ff_own), ff_own)
        for n, (source, target) in enumerate(
            (
                (pair_ref.at[:, :, columns], pair_all.at[:, ctx, fsdp]),
                (down_ref, down_all.at[fsdp]),
                (kv_ref, window.at[reach]),
            )
        ):
            kept.append(pltpu.make_async_copy(source, target, own_sems.at[count + n]))
        for step in range(1, reach + 1):
            copy = pltpu.make_async_copy(
                zero_ref, window.at[reach - step], own_sems.at[count + 2 + step]
            )
            empty.append((step, copy))
    for copy in kept:
        copy.start()
    for step, copy in empty:
        pl.when(ctx - step < 0)(copy.start)
    copies, sharing = front_copies(
        parts, wholes, pair_ref, pair_all, down_ref, down_all, sizes
    )
    for step, copy in halos:
        copies.append(lambda step=step, copy=copy: pl.when(ctx + step < sizes[0])(copy.start))
    copies += sharing
    run_copies(copies, send_sems, recv_sems)
    for copy in kept:
        copy.wait()
    for step, copy in empty:
        pl.when(ctx - step < 0)(copy.wait)
    for step, copy in halos:
        pl.when(ctx - step >= 0)(copy.wait_recv)
    for step, copy in halos:
        pl.when(ctx + step < sizes[0])(copy.wait_send)


def gather_front(parts, pair, down, cot, key_value, sizes, collective_id):
    ctx_size, fsdp_size = sizes
    chips = ctx_size // 2
    rows = parts[0].shape[0]
    paired = pair is not None
    reach = WINDOW // STRETCH
    count = len(parts) * (chips - 1 + chips * (2 * (fsdp_size - 1) + 1) + fsdp_size - 1)
    shapes = [
        jax.ShapeDtypeStruct((chips, 2, fsdp_size, rows, part.shape[1]), part.dtype)
        for part in parts
    ]
    arrays = list(parts)
    if paired:
        count += ctx_size - 1 + 2 * (fsdp_size - 1)
        columns = pair.shape[2] // ctx_size
        shapes += [
            jax.ShapeDtypeStruct((2, ctx_size, fsdp_size, rows, columns), pair.dtype),
            jax.ShapeDtypeStruct((fsdp_size,) + down.shape, down.dtype),
            jax.ShapeDtypeStruct((reach + 1,) + key_value.shape, key_value.dtype),
        ]
        arrays += [pair, down, key_value, jnp.zeros_like(key_value)]
    hbm = pl.BlockSpec(memory_space=pl.ANY)
    vmem = pl.BlockSpec(memory_space=pltpu.VMEM)
    return pl.pallas_call(
        functools.partial(front_kernel, sizes, len(parts), paired),
        in_specs=[vmem] * len(arrays) + [hbm] * paired,
        out_specs=[hbm] * (len(shapes) + paired),
        out_shape=shapes + ([jax.ShapeDtypeStruct(cot.shape, cot.dtype)] if paired else []),
        input_output_aliases={len(arrays): len(shapes)} if paired else {},
        scratch_shapes=[
            pltpu.SemaphoreType.DMA((count,)),
            pltpu.SemaphoreType.DMA((count,)),
            pltpu.SemaphoreType.DMA((len(shapes) + reach,)),
            pltpu.SemaphoreType.DMA((reach,)),
            pltpu.SemaphoreType.DMA((reach,)),
        ],
        compiler_params=pltpu.CompilerParams(collective_id=collective_id, has_side_effects=True),
        cost_estimate=pl.CostEstimate(
            flops=90_000_000_000, bytes_accessed=1_000_000, transcendentals=0
        ),
    )(*arrays, *([cot] if paired else []))


def hidden_kernel(sizes, pieces, pair_in, normed_ref, pair_all, normed_all, send_sems, recv_sems, own_sem):
    ctx_size, fsdp_size = sizes
    ctx, fsdp = lax.axis_index("ctx"), lax.axis_index("fsdp")
    masks = [1 << bit for bit in range(fsdp_size.bit_length() - 1)]
    far = [1 << bit for bit in range((ctx_size // 2).bit_length() - 1)]
    greet([(0, 0, m) for m in masks] + [(m, 0, 0) for m in far] + [(0, 1, 0)])
    mine = pltpu.make_async_copy(normed_ref, normed_all.at[ctx // 2, ctx % 2], own_sem)
    mine.start()
    lists = []
    for h, order in enumerate([masks, masks[::-1]]):
        view = lambda r, h=h: pair_all.at[h, :, fsdp ^ r]
        lists.append(doubling(("pair", h), fsdp_size, order, (), view, view)[0])
    rows = normed_ref.shape[0] // pieces
    lines = []
    for n in range(pieces):
        strip = pl.ds(n * rows, rows)
        lines.append(
            line_gather(("normed", n), normed_ref.at[strip], normed_all.at[:, :, strip], sizes)
        )
    ready = [[copy for hop in line for copy in hop if not copy[1]] for line in lines]
    later = [[copy for copy in hop if copy[1]] for line in lines for hop in line]
    later = [
        [hop for hop in later[n * len(lines[0]) : (n + 1) * len(lines[0])] if hop]
        for n in range(pieces)
    ]
    pair_hops = [
        [copy for pieces in zip(*(hops[n] for hops in lists)) for copy in pieces]
        for n in range(len(masks))
    ]
    ahead, depth = 2, len(later[0])
    copies = [copy for line in ready[:ahead] for copy in line] + pair_hops[0]
    for turn in range(pieces + depth - 1):
        for stage in range(depth):
            if 0 <= turn - stage < pieces:
                copies.extend(later[turn - stage][stage])
            if stage == 0 and turn + ahead < pieces:
                copies.extend(ready[turn + ahead])
        if turn == 1:
            for hop in pair_hops[1:]:
                copies.extend(hop)
    run_copies(copies, send_sems, recv_sems)
    mine.wait()


def gather_hidden(pair_all, normed, sizes):
    ctx_size, fsdp_size = sizes
    chips = ctx_size // 2
    pieces = 4
    count = 2 * (fsdp_size - 1) + pieces * (2 * chips - 1)
    hbm = pl.BlockSpec(memory_space=pl.ANY)
    return pl.pallas_call(
        functools.partial(hidden_kernel, sizes, pieces),
        in_specs=[hbm, pl.BlockSpec(memory_space=pltpu.VMEM)],
        out_specs=[hbm, hbm],
        out_shape=[
            jax.ShapeDtypeStruct(pair_all.shape, pair_all.dtype),
            jax.ShapeDtypeStruct((chips, 2) + normed.shape, normed.dtype),
        ],
        input_output_aliases={0: 0},
        scratch_shapes=[
            pltpu.SemaphoreType.DMA((count,)),
            pltpu.SemaphoreType.DMA((count,)),
            pltpu.SemaphoreType.DMA,
        ],
        compiler_params=pltpu.CompilerParams(collective_id=2, has_side_effects=True),
        cost_estimate=pl.CostEstimate(flops=90_000_000_000, bytes_accessed=30_000_000, transcendentals=0),
    )(pair_all, normed)


def hop_slots(size, order):
    slots, held = [], list(range(size))
    for mask in order:
        held = [r for r in held if not r & mask]
        slots.append(held)
    return slots


def remote(source, target, send_sem, recv_sem, peer):
    return pltpu.make_async_remote_copy(
        src_ref=source,
        dst_ref=target,
        send_sem=send_sem,
        recv_sem=recv_sem,
        device_id=peer_of(*peer),
        device_id_type=pl.DeviceIdType.MESH,
    )


def reduce_kernel(sizes, chunk, products, extras, halos, swaps, *refs):
    refs = list(refs)

    def take(amount):
        taken = refs[:amount]
        del refs[:amount]
        return taken

    lefts, right, extra = take(3)
    sent, swap_in = take(halos), take(swaps)
    (total,) = take(1)
    halo_got, swap_out = take(halos), take(swaps)
    terms, core_got, line_sent, line_got = take(4)
    core_send, core_recv, hop_send, hop_recv, line_send, line_recv = take(6)
    halo_send, halo_recv, swap_send, swap_recv, swap_own = take(5)
    hop_buffers = refs
    ctx_size, fsdp_size = sizes
    chips = ctx_size // 2
    rows = total.shape[0]
    count = products + extras
    half = chunk // 2
    masks = [1 << bit for bit in range(fsdp_size.bit_length() - 1)]
    orders = [masks, masks[::-1]]
    bits = len(masks)
    hops = [
        [hop_buffers[(h * bits + j) * 2 : (h * bits + j) * 2 + 2] for j in range(bits)]
        for h in range(2)
    ]
    slots = [hop_slots(fsdp_size, order) for order in orders]
    ctx, fsdp = lax.axis_index("ctx"), lax.axis_index("fsdp")
    chip, side = ctx // 2, ctx % 2
    if halos or swaps:
        greet(front_masks(ctx_size, fsdp_size, True))
    else:
        greet(
            [(0, 1, 0)]
            + [(0, 0, m) for m in masks]
            + [(1 << bit, 0, 0) for bit in range(chips.bit_length() - 1)]
        )
    back = []
    for n in range(halos):
        reach = halo_got[n].shape[0]
        rows_of = halo_got[n].shape[1]
        for step in range(1, reach + 1):
            copy = pltpu.make_async_remote_copy(
                src_ref=sent[n].at[pl.ds((reach - step) * rows_of, rows_of)],
                dst_ref=halo_got[n].at[step - 1],
                send_sem=halo_send.at[n, step - 1],
                recv_sem=halo_recv.at[n, step - 1],
                device_id=(lax.rem(ctx - step + ctx_size, ctx_size), fsdp),
                device_id_type=pl.DeviceIdType.MESH,
            )
            back.append((step, copy))
            pl.when(ctx - step >= 0)(copy.start)
    swapped = []
    for source, target in zip(swap_in, swap_out):
        swapped.append(pltpu.make_async_copy(source.at[ctx], target.at[ctx], swap_own))
        for mask in range(1, ctx_size):
            swapped.append(
                remote(
                    source.at[ctx ^ mask], target.at[ctx],
                    swap_send.at[mask], swap_recv.at[mask], (mask // 2, mask % 2, 0),
                )
            )
    for copy in swapped:
        copy.start()

    def core_copy(i):
        return remote(
            terms.at[i, :, 1 - side], core_got.at[i], core_send.at[i], core_recv.at[i], (0, 1, 0)
        )

    def hop_copy(h, j, i):
        sent, got = hops[h][j]
        return remote(
            sent.at[i], got.at[i], hop_send.at[h, j, i], hop_recv.at[h, j, i], (0, 0, orders[h][j])
        )

    near_first = [1 << bit for bit in range(chips.bit_length() - 1)]
    line_slots = hop_slots(chips, near_first)
    line_first = [sum(chips >> (k + 1) for k in range(j)) for j in range(len(near_first))]

    def line_copy(j, i):
        blocks = pl.ds(line_first[j], chips >> (j + 1))
        return remote(
            line_sent.at[i, blocks], line_got.at[i, blocks],
            line_send.at[i, j], line_recv.at[i, j], (near_first[j], 0, 0),
        )

    def line_held(h, upto, i, r):
        cols = slice(h * half, (h + 1) * half)
        value = held(h, bits, i, chip ^ r, 0)
        for j in range(upto):
            value += line_got[i, line_first[j] + line_slots[j].index(r), :, cols].astype(
                jnp.float32
            )
        return value

    def held(h, upto, i, z, r):
        cols = pl.ds(h * half, half)
        value = terms[i, z, side, fsdp ^ r, :, cols].astype(jnp.float32)
        value += core_got[i, z, fsdp ^ r, :, cols].astype(jnp.float32)
        for j in range(upto):
            value += hops[h][j][1][i, slots[h][j].index(r), z].astype(jnp.float32)
        return value

    slack = 6
    last = bits + 1 + slack * len(near_first)

    def step(t, carry):
        @pl.when(t < products)
        def _():
            per_left = products // lefts.shape[0]
            cols = pl.ds(pl.multiple_of(t * chunk, chunk), chunk)
            term = jnp.dot(
                lefts[t // per_left], right[:, cols], preferred_element_type=jnp.float32
            )
            terms[t] = term.astype(jnp.bfloat16).reshape(terms.shape[1:])

        if extras:
            @pl.when((t >= products) & (t < count))
            def _():
                terms[t] = extra[t - products].reshape(terms.shape[1:])

        @pl.when(t < count)
        def _():
            core_copy(t).start()

        for j in range(bits):
            @pl.when((t >= j + 1) & (t < count + j + 1))
            def _(j=j):
                i = t - (j + 1)
                if j == 0:
                    core_copy(i).wait_recv()
                for h in range(2):
                    if j:
                        hop_copy(h, j - 1, i).wait_recv()
                    for s, r in enumerate(slots[h][j]):
                        for z in range(chips):
                            hops[h][j][0][i, s, z] = held(h, j, i, z, r | orders[h][j]).astype(
                                jnp.bfloat16
                            )
                    hop_copy(h, j, i).start()

        for j in range(len(near_first)):
            lag = bits + 1 + slack * j

            @pl.when((t >= lag) & (t < count + lag))
            def _(j=j, lag=lag):
                i = t - lag
                if j:
                    line_copy(j - 1, i).wait_recv()
                for h in range(2):
                    if j == 0:
                        hop_copy(h, bits - 1, i).wait_recv()
                    for s, r in enumerate(line_slots[j]):
                        line_sent[i, line_first[j] + s, :, h * half : (h + 1) * half] = line_held(
                            h, j, i, r | near_first[j]
                        ).astype(jnp.bfloat16)
                line_copy(j, i).start()

        @pl.when(t >= last)
        def _():
            i = t - last
            line_copy(len(near_first) - 1, i).wait_recv()
            for h in range(2):
                value = line_held(h, len(near_first), i, 0)
                total[:, pl.ds(pl.multiple_of(i * chunk + h * half, half), half)] = value

        return carry

    lax.fori_loop(0, count + last, step, 0)

    def finish(i, carry):
        core_copy(i).wait_send()
        for h in range(2):
            for j in range(bits):
                hop_copy(h, j, i).wait_send()
        for j in range(len(near_first)):
            line_copy(j, i).wait_send()
        return carry

    lax.fori_loop(0, count, finish, 0)
    for copy in swapped:
        copy.wait()
    for step, copy in back:
        pl.when(ctx + step < ctx_size)(copy.wait_recv)
    for step, copy in back:
        pl.when(ctx - step >= 0)(copy.wait_send)


def reduce_rows(lefts, right, extra, halos, swaps, chunk, sizes, collective_id):
    ctx_size, fsdp_size = sizes
    chips = ctx_size // 2
    depth = lefts.shape[1]
    rows = depth // (ctx_size * fsdp_size)
    products = right.shape[1] // chunk
    extras = 0 if extra is None else extra.shape[0]
    if extra is None:
        extra = jnp.zeros((1, 16, LANES), jnp.bfloat16)
    count = products + extras
    bits = fsdp_size.bit_length() - 1
    half = chunk // 2
    reach = WINDOW // STRETCH
    buffers = []
    for _ in range(2):
        for j in range(bits):
            shape = (count, fsdp_size >> (j + 1), chips, rows, half)
            buffers += [pltpu.VMEM(shape, jnp.bfloat16)] * 2
    line = pltpu.VMEM((count, max(chips - 1, 1), rows, chunk), jnp.bfloat16)
    vmem = pl.BlockSpec(memory_space=pltpu.VMEM)
    hbm = pl.BlockSpec(memory_space=pl.ANY)
    return pl.pallas_call(
        functools.partial(reduce_kernel, sizes, chunk, products, extras, len(halos), len(swaps)),
        in_specs=[vmem] * 3 + [hbm] * (len(halos) + len(swaps)),
        out_specs=[vmem] + [hbm] * (len(halos) + len(swaps)),
        out_shape=[jax.ShapeDtypeStruct((rows, count * chunk), jnp.float32)]
        + [
            jax.ShapeDtypeStruct((reach, array.shape[0] // reach, array.shape[1]), array.dtype)
            for array in halos
        ]
        + [jax.ShapeDtypeStruct(array.shape, array.dtype) for array in swaps],
        scratch_shapes=[
            pltpu.VMEM((count, chips, 2, fsdp_size, rows, chunk), jnp.bfloat16),
            pltpu.VMEM((count, chips, fsdp_size, rows, chunk), jnp.bfloat16),
            line,
            line,
            pltpu.SemaphoreType.DMA((count,)),
            pltpu.SemaphoreType.DMA((count,)),
            pltpu.SemaphoreType.DMA((2, bits, count)),
            pltpu.SemaphoreType.DMA((2, bits, count)),
            pltpu.SemaphoreType.DMA((count, chips.bit_length() - 1)),
            pltpu.SemaphoreType.DMA((count, chips.bit_length() - 1)),
            pltpu.SemaphoreType.DMA((max(len(halos), 1), reach)),
            pltpu.SemaphoreType.DMA((max(len(halos), 1), reach)),
            pltpu.SemaphoreType.DMA((ctx_size,)),
            pltpu.SemaphoreType.DMA((ctx_size,)),
            pltpu.SemaphoreType.DMA,
        ]
        + buffers,
        compiler_params=pltpu.CompilerParams(
            collective_id=collective_id, has_side_effects=True, vmem_limit_bytes=56 * 1024 * 1024
        ),
        cost_estimate=pl.CostEstimate(flops=80_000_000_000, bytes_accessed=30_000_000, transcendentals=0),
    )(lefts, right, extra, *halos, *swaps)


def hidden_grad_kernel(
    sizes, normed, gate, up, carried_in, pair_sum, carried,
    terms, pair_sent, pair_got, pair_send, pair_recv
):
    ctx_size, fsdp_size = sizes
    count, span = terms.shape[1], normed.shape[1] // terms.shape[1]
    masks = [1 << bit for bit in range(fsdp_size.bit_length() - 1)]
    orders = [masks, masks[::-1]]
    bits = len(masks)
    slots = [hop_slots(fsdp_size, order) for order in orders]
    fsdp = lax.axis_index("fsdp")
    greet([(0, 0, m) for m in masks])
    first = [sum(fsdp_size >> (k + 1) for k in range(j)) for j in range(bits)]

    def pair_copy(h, j, i):
        rows = pl.ds(first[j], fsdp_size >> (j + 1))
        return remote(
            pair_sent.at[h, i, rows], pair_got.at[h, i, rows],
            pair_send.at[h, j, i], pair_recv.at[h, j, i], (0, 0, orders[h][j]),
        )

    def pair_held(h, upto, i, r):
        value = terms[h, i, fsdp ^ r].astype(jnp.float32)
        for j in range(upto):
            value += pair_got[h, i, first[j] + slots[h][j].index(r)].astype(jnp.float32)
        return value

    def step(t, carry):
        @pl.when(t < count)
        def _():
            rows = pl.ds(pl.multiple_of(t * span, span), span)
            for h, grad in enumerate((gate, up)):
                term = across(normed[:, rows], grad[...])
                terms[h, t] = term.astype(jnp.bfloat16).reshape(terms.shape[2:])

        for j in range(bits):
            @pl.when((t >= j) & (t < count + j))
            def _(j=j):
                i = t - j
                for h in range(2):
                    if j:
                        pair_copy(h, j - 1, i).wait_recv()
                    for s, r in enumerate(slots[h][j]):
                        pair_sent[h, i, first[j] + s] = pair_held(
                            h, j, i, r | orders[h][j]
                        ).astype(jnp.bfloat16)
                    pair_copy(h, j, i).start()

        @pl.when(t >= bits)
        def _():
            i = t - bits
            for h in range(2):
                pair_copy(h, bits - 1, i).wait_recv()
                pair_sum[i, h] = pair_held(h, bits, i, 0).astype(jnp.bfloat16)

        return carry

    lax.fori_loop(0, count + bits, step, 0)

    def finish(i, carry):
        for h in range(2):
            for j in range(bits):
                pair_copy(h, j, i).wait_send()
        return carry

    lax.fori_loop(0, count, finish, 0)


def reduce_hidden(normed, gate, up, carried, sizes):
    ctx_size, fsdp_size = sizes
    bits = fsdp_size.bit_length() - 1
    rows, columns = normed.shape[1] // (ctx_size * fsdp_size), gate.shape[1]
    pair = pltpu.VMEM((2, ctx_size, fsdp_size - 1, rows, columns), jnp.bfloat16)
    vmem = pl.BlockSpec(memory_space=pltpu.VMEM)
    hbm = pl.BlockSpec(memory_space=pl.ANY)
    return pl.pallas_call(
        functools.partial(hidden_grad_kernel, sizes),
        in_specs=[vmem] * 3 + [hbm],
        out_specs=[vmem, hbm],
        out_shape=[
            jax.ShapeDtypeStruct((ctx_size, 2, rows, columns), jnp.bfloat16),
            jax.ShapeDtypeStruct(carried.shape, carried.dtype),
        ],
        input_output_aliases={3: 1},
        scratch_shapes=[
            pltpu.VMEM((2, ctx_size, fsdp_size, rows, columns), jnp.bfloat16), pair, pair,
        ]
        + [pltpu.SemaphoreType.DMA((2, bits, ctx_size))] * 2,
        compiler_params=pltpu.CompilerParams(
            collective_id=3, has_side_effects=True, vmem_limit_bytes=60 * 1024 * 1024
        ),
        cost_estimate=pl.CostEstimate(flops=60_000_000_000, bytes_accessed=30_000_000, transcendentals=0),
    )(normed, gate, up, carried)


def norm_keys_kernel(stream, gain, weight, cosine, sine, normed_ref, pair_ref):
    x = stream[...].astype(jnp.float32)
    inverse = lax.rsqrt(jnp.mean(x * x, axis=1, keepdims=True) + EPS)
    normed = (x * inverse * gain[...]).astype(jnp.bfloat16)
    normed_ref[...] = normed
    front = product(normed, weight[...])
    kv_width = KV_HEADS * HEAD_DIM
    keys = turn(front[:, :kv_width], cosine[...], sine[...])
    pair_ref[:, :kv_width] = keys.astype(jnp.bfloat16)
    pair_ref[:, kv_width:] = front[:, kv_width : 2 * kv_width].astype(jnp.bfloat16)


def norm_keys(stream, gain, weight, cosine, sine):
    rows = stream.shape[0]
    return pl.pallas_call(
        norm_keys_kernel,
        out_shape=[
            jax.ShapeDtypeStruct(stream.shape, jnp.bfloat16),
            jax.ShapeDtypeStruct((rows, 2 * KV_HEADS * HEAD_DIM), jnp.bfloat16),
        ],
        compiler_params=pltpu.CompilerParams(vmem_limit_bytes=40 * 1024 * 1024),
        cost_estimate=pl.CostEstimate(
            flops=2 * rows * weight.size, bytes_accessed=8_000_000, transcendentals=0
        ),
    )(stream, gain, weight, cosine, sine)


def out_norm_kernel(mix, weight, stream, gain, resid, normed, total):
    i, steps = pl.program_id(0), pl.num_programs(0)
    span = weight.shape[1]
    cols = pl.ds(pl.multiple_of(i * span, span), span)
    total[:, cols] = stream[:, cols].astype(jnp.float32) + product(mix[...], weight[...])

    @pl.when(i == steps - 1)
    def _():
        h = total[...]
        resid[...] = h
        inverse = lax.rsqrt(jnp.mean(h * h, axis=1, keepdims=True) + EPS)
        normed[...] = (h * inverse * gain[...]).astype(jnp.bfloat16)


def out_norm(mix, weight, stream, gain):
    rows, width = mix.shape
    steps = 4
    whole = pl.BlockSpec((rows, width), lambda i: (0, 0))
    return pl.pallas_call(
        out_norm_kernel,
        grid=(steps,),
        in_specs=[
            whole,
            pl.BlockSpec((width, width // steps), lambda i: (0, i)),
            whole,
            pl.BlockSpec((1, width), lambda i: (0, 0)),
        ],
        out_specs=[whole, whole],
        out_shape=[
            jax.ShapeDtypeStruct((rows, width), jnp.float32),
            jax.ShapeDtypeStruct((rows, width), jnp.bfloat16),
        ],
        scratch_shapes=[pltpu.VMEM((rows, width), jnp.float32)],
        compiler_params=pltpu.CompilerParams(vmem_limit_bytes=40 * 1024 * 1024),
        cost_estimate=pl.CostEstimate(
            flops=2 * rows * width * width, bytes_accessed=14_000_000, transcendentals=0
        ),
    )(mix, weight, stream, gain)


def norm_back_kernel(
    columns, resid, gain, cot, weight, earlier, carried_in,
    grad_ref, low_ref, mix_ref, gain_ref, carried
):
    @pl.when(pl.program_id(0) == 0)
    def _():
        h = resid[...]
        inverse = lax.rsqrt(jnp.mean(h * h, axis=1, keepdims=True) + EPS)
        normal = h * inverse
        slope = columns[...].astype(jnp.float32)
        gain_ref[...] = jnp.sum(slope * normal, axis=0, keepdims=True)
        grad = cot[...].astype(jnp.float32) + norm_back(slope * gain[...], normal, inverse)
        grad_ref[...] = grad
        low_ref[...] = grad.astype(jnp.bfloat16)

    mix_ref[...] = against(low_ref[...], weight[...]).astype(jnp.bfloat16)


def norm_back_mix(columns, resid, gain, cot, weight, earlier, carried):
    rows, width = resid.shape
    steps = 4
    whole = pl.BlockSpec((rows, width), lambda i: (0, 0))
    line = pl.BlockSpec((1, width), lambda i: (0, 0))
    return pl.pallas_call(
        norm_back_kernel,
        grid=(steps,),
        in_specs=[
            whole, whole, line, whole,
            pl.BlockSpec((width // steps, width), lambda i: (i, 0)),
            pl.BlockSpec(memory_space=pl.ANY),
            pl.BlockSpec(memory_space=pl.ANY),
        ],
        out_specs=[
            whole, whole,
            pl.BlockSpec((rows, width // steps), lambda i: (0, i)),
            line,
            pl.BlockSpec(memory_space=pl.ANY),
        ],
        out_shape=[
            jax.ShapeDtypeStruct((rows, width), jnp.float32),
            jax.ShapeDtypeStruct((rows, width), jnp.bfloat16),
            jax.ShapeDtypeStruct((rows, width), jnp.bfloat16),
            jax.ShapeDtypeStruct((1, width), jnp.float32),
            jax.ShapeDtypeStruct(carried.shape, carried.dtype),
        ],
        input_output_aliases={6: 4},
        compiler_params=pltpu.CompilerParams(vmem_limit_bytes=40 * 1024 * 1024),
        cost_estimate=pl.CostEstimate(
            flops=2 * rows * width * width, bytes_accessed=16_000_000, transcendentals=0
        ),
    )(columns, resid, gain, cot, weight, earlier, carried)


def input_grad_kernel(
    dk_own, dv_own, dk_got, dv_got, cosine, sine, dq, query_weight, kv_weight, stream, gain, resid_grad,
    kv_ref, gain_ref, grad_ref, total
):
    i, steps = pl.program_id(0), pl.num_programs(0)
    span = query_weight.shape[0]
    kv_width = dk_own.shape[1]

    @pl.when(i == 0)
    def _():
        ctx, size = lax.axis_index("ctx"), lax.axis_size("ctx")
        dk, dv = dk_own[...], dv_own[...]
        for step in range(1, dk_got.shape[0] + 1):
            there = ctx + step < size
            dk += jnp.where(there, dk_got[step - 1].astype(jnp.float32), 0.0)
            dv += jnp.where(there, dv_got[step - 1].astype(jnp.float32), 0.0)
        kv_ref[:, :kv_width] = turn(dk, cosine[...], -sine[...]).astype(jnp.bfloat16)
        kv_ref[:, kv_width:] = dv.astype(jnp.bfloat16)

    cols = pl.ds(pl.multiple_of(i * span, span), span)
    total[:, cols] = against(dq[...], query_weight[...]) + against(
        kv_ref[...], kv_weight[:, : 2 * kv_width]
    )

    @pl.when(i == steps - 1)
    def _():
        x = stream[...].astype(jnp.float32)
        inverse = lax.rsqrt(jnp.mean(x * x, axis=1, keepdims=True) + EPS)
        normal = x * inverse
        slope = total[...]
        gain_ref[...] = jnp.sum(slope * normal, axis=0, keepdims=True)
        grad = resid_grad[...] + norm_back(slope * gain[...], normal, inverse)
        grad_ref[...] = grad.astype(jnp.bfloat16)


def input_grad(dk_own, dv_own, dk_got, dv_got, cosine, sine, dq, query_weight, kv_weight, stream, gain, resid_grad):
    rows, width = stream.shape
    steps = 4
    span = width // steps

    def whole(array):
        return pl.BlockSpec(array.shape, lambda i: (0,) * array.ndim)

    def strip(array):
        return pl.BlockSpec((span, array.shape[1]), lambda i: (i, 0))

    kept = (dk_own, dv_own, dk_got, dv_got, cosine, sine, dq)
    kv_shape = (rows, 2 * dk_own.shape[1])
    return pl.pallas_call(
        input_grad_kernel,
        grid=(steps,),
        in_specs=[whole(array) for array in kept]
        + [strip(query_weight), strip(kv_weight)]
        + [whole(array) for array in (stream, gain, resid_grad)],
        out_specs=[
            pl.BlockSpec(kv_shape, lambda i: (0, 0)),
            pl.BlockSpec((1, width), lambda i: (0, 0)),
            pl.BlockSpec((rows, width), lambda i: (0, 0)),
        ],
        out_shape=[
            jax.ShapeDtypeStruct(kv_shape, jnp.bfloat16),
            jax.ShapeDtypeStruct((1, width), jnp.float32),
            jax.ShapeDtypeStruct((rows, width), jnp.bfloat16),
        ],
        scratch_shapes=[pltpu.VMEM((rows, width), jnp.float32)],
        compiler_params=pltpu.CompilerParams(vmem_limit_bytes=48 * 1024 * 1024),
        cost_estimate=pl.CostEstimate(
            flops=3 * rows * width * width, bytes_accessed=24_000_000, transcendentals=0
        ),
    )(*kept, query_weight, kv_weight, stream, gain, resid_grad)


def hidden_layer_kernel(
    normed, cot, gate_weight, up_weight, down_weight,
    hidden_ref, dgate_ref, dup_ref, down_ref, columns_ref
):
    x = normed[...]
    gate = product(x, gate_weight[...])
    up = product(x, up_weight[...])
    grad = against(cot[...], down_weight[...])
    sigmoid = jax.nn.sigmoid(gate)
    silu = gate * sigmoid
    hidden = (silu * up).astype(jnp.bfloat16)
    dgate = (grad * up * sigmoid * (1.0 + gate * (1.0 - sigmoid))).astype(jnp.bfloat16)
    dup = (grad * silu).astype(jnp.bfloat16)
    hidden_ref[...] = hidden
    dgate_ref[...] = dgate
    dup_ref[...] = dup
    columns = against(dgate, gate_weight[...]) + against(dup, up_weight[...])
    columns_ref[...] = columns.astype(jnp.bfloat16)
    down_ref[...] = product(hidden, down_weight[...]).astype(jnp.bfloat16)


def hidden_layer(normed, cot, pair, down_weight):
    tokens, width = normed.shape
    share = pair.shape[2]
    tile = min(256, tokens)
    wide = pl.BlockSpec((tile, width), lambda i: (i, 0))
    thin = pl.BlockSpec((tile, share), lambda i: (i, 0))
    once = pl.Buffered(buffer_count=1)
    weights = [
        pl.BlockSpec((None,) + pair.shape[1:], lambda i, n=n: (n, 0, 0), pipeline_mode=once)
        for n in range(2)
    ]
    down = pl.BlockSpec(down_weight.shape, lambda i: (0, 0), pipeline_mode=once)
    thin_out = jax.ShapeDtypeStruct((tokens, share), jnp.bfloat16)
    wide_out = jax.ShapeDtypeStruct((tokens, width), jnp.bfloat16)
    return pl.pallas_call(
        hidden_layer_kernel,
        grid=(tokens // tile,),
        in_specs=[wide, wide] + weights + [down],
        out_specs=[thin, thin, thin, wide, wide],
        out_shape=[thin_out] * 3 + [wide_out] * 2,
        compiler_params=pltpu.CompilerParams(vmem_limit_bytes=56 * 1024 * 1024),
        cost_estimate=pl.CostEstimate(
            flops=16 * tokens * width * share, bytes_accessed=30_000_000, transcendentals=0
        ),
    )(normed, cot, pair, pair, down_weight)


def local(
    tokens,
    cotangent,
    lengths,
    attn_gain,
    query_weight,
    key_weight,
    value_weight,
    out_weight,
    mlp_gain,
    gate_weight,
    up_weight,
    down_weight,
):
    both = ("ctx", "fsdp")
    ctx_size = lax.axis_size("ctx")
    fsdp_size = lax.axis_size("fsdp")
    chips = ctx_size // 2
    stream = tokens[0].astype(jnp.float32)
    tok_rows = stream.shape[0]
    own_rows = query_weight.shape[0]
    kv_width = KV_HEADS * HEAD_DIM
    ff_own = FF // ctx_size
    reach_blocks = WINDOW // STRETCH
    ctx_place = lax.axis_index("ctx")
    doc_lengths = lengths[0]
    query_index = ctx_place * tok_rows + jnp.arange(tok_rows, dtype=jnp.int32)
    key_index = (ctx_place - reach_blocks) * tok_rows + jnp.arange(
        (reach_blocks + 1) * tok_rows, dtype=jnp.int32
    )
    query_doc = doc_segment(doc_lengths, query_index)
    key_doc = doc_segment(doc_lengths, key_index)
    position = doc_position(doc_lengths, query_index, query_doc)
    visible = (key_index[:, None] >= 0) & (key_index[:, None] <= query_index[None, :])
    visible = (
        visible
        & (query_index[None, :] - key_index[:, None] < WINDOW)
        & (query_doc[None, :] == key_doc[:, None])
    )
    bias = jnp.where(visible, 0.0, -1e30).astype(jnp.float32)
    cosine, sine = turn_tables(position)

    sizes = (ctx_size, fsdp_size)
    gains = jnp.zeros((own_rows, LANES), jnp.bfloat16)
    gains = gains.at[:, 0].set(attn_gain).at[:, 1].set(mlp_gain)
    (kv_all,) = gather_front(
        (jnp.concatenate([key_weight, value_weight, gains], axis=1),), None, None, None, None, sizes, 1
    )
    kv_all = kv_all.reshape(D, -1)
    gain_one = kv_all[:, 2 * kv_width].astype(jnp.float32)
    gain_two = kv_all[:, 2 * kv_width + 1].astype(jnp.float32)

    inv_one = lax.rsqrt(jnp.mean(stream * stream, axis=1, keepdims=True) + EPS)
    normal_one = stream * inv_one
    normed_one, own_pair = norm_keys(tokens[0], gain_one[None], kv_all, cosine, sine)
    query_all, out_all, pair_all, down_own, window, cot_own = gather_front(
        (query_weight, out_weight), jnp.stack([gate_weight, up_weight]), down_weight,
        cotangent[0], own_pair, sizes, 6,
    )
    cot_all = lax.all_gather(cot_own, "ctx", axis=0, tiled=True)
    query_all = query_all.reshape(D, D)
    out_all = out_all.reshape(D, D)
    down_own = down_own.reshape(ff_own, D)
    window = window.reshape(-1, 2 * kv_width)
    key_window, value_window = window[:, :kv_width], window[:, kv_width:]
    attn_mix, query_low, log_total = attend_forward(
        normed_one, query_all, key_window, value_window, bias, cosine, sine
    )
    resid, normed_two = out_norm(attn_mix, out_all, tokens[0], gain_two[None])
    pair, normed_all = gather_hidden(pair_all, normed_two, sizes)
    pair = pair.reshape(2, D, ff_own)
    normed_all = normed_all.reshape(ctx_size * tok_rows, D)
    hidden, grad_gate_low, grad_up_low, down_part, columns = hidden_layer(
        normed_all, cot_all, pair, down_own
    )
    columns = lax.psum_scatter(columns, "ctx", scatter_dimension=0, tiled=True)
    pair_sum, down_part = reduce_hidden(normed_all, grad_gate_low, grad_up_low, down_part, sizes)
    down_terms = across(hidden, cot_all).astype(jnp.bfloat16)
    grad_resid, grad_resid_low, grad_mix_low, mlp_gain_local, down_terms = norm_back_mix(
        columns, resid, gain_two[None], cotangent[0], out_all, pair_sum, down_terms
    )
    down_sum = lax.psum_scatter(down_part, "ctx", scatter_dimension=0, tiled=True)
    grad_query_low, dk_low, dv_low, dk_own, dv_own, down_terms = attend_backward(
        query_low, key_window, value_window, grad_mix_low, attn_mix, log_total, bias, cosine, sine,
        down_terms,
    )
    grad_down = lax.psum_scatter(down_terms, "fsdp", scatter_dimension=0, tiled=True)
    wide_grad, dk_got, dv_got = reduce_rows(
        jnp.stack([normed_one.T, attn_mix.T]),
        jnp.concatenate([grad_query_low, grad_resid_low], axis=1),
        None, (dk_low, dv_low), (), 512, sizes, 4,
    )
    kv_low, attn_gain_local, grad_input = input_grad(
        dk_own, dv_own, dk_got, dv_got, cosine, sine, grad_query_low, query_all, kv_all,
        tokens[0], gain_one[None], grad_resid,
    )
    gain_terms = jnp.stack([attn_gain_local[0], mlp_gain_local[0]], axis=1).astype(jnp.bfloat16)
    gain_terms = jnp.pad(gain_terms, ((0, 0), (0, 2 * LANES - 2)))[None]
    kv_grad, pair_sum = reduce_rows(
        normed_one.T[None], kv_low, gain_terms, (), (pair_sum,), 2 * LANES, sizes, 5
    )
    mixed = after(resid, kv_grad) + after(down_sum, kv_grad).astype(jnp.float32)
    mixed = mixed.astype(jnp.bfloat16)
    pair_sum = pair_sum.transpose(1, 2, 0, 3).reshape(2, own_rows, FF).astype(jnp.float32)
    return (
        mixed[None],
        grad_input[None],
        kv_grad[:, 2 * kv_width],
        wide_grad[:, :D],
        kv_grad[:, :kv_width],
        kv_grad[:, kv_width : 2 * kv_width],
        wide_grad[:, D:],
        kv_grad[:, 2 * kv_width + 1],
        pair_sum[0],
        pair_sum[1],
        grad_down.astype(jnp.float32),
    )


def solution(mesh):
    in_specs = (
        P("fsdp", "ctx", None),
        P("fsdp", "ctx", None),
        P("fsdp", None),
        P(("ctx", "fsdp")),
        P(("ctx", "fsdp"), None),
        P(("ctx", "fsdp"), None),
        P(("ctx", "fsdp"), None),
        P(("ctx", "fsdp"), None),
        P(("ctx", "fsdp")),
        P(("ctx", "fsdp"), None),
        P(("ctx", "fsdp"), None),
        P(("ctx", "fsdp"), None),
    )
    out_specs = (
        P("fsdp", "ctx", None),
        P("fsdp", "ctx", None),
        P(("ctx", "fsdp")),
        P(("ctx", "fsdp"), None),
        P(("ctx", "fsdp"), None),
        P(("ctx", "fsdp"), None),
        P(("ctx", "fsdp"), None),
        P(("ctx", "fsdp")),
        P(("ctx", "fsdp"), None),
        P(("ctx", "fsdp"), None),
        P(("ctx", "fsdp"), None),
    )
    return jax.shard_map(local, mesh=mesh, in_specs=in_specs, out_specs=out_specs, check_vma=False)
```
